32 devices in a mesh: rad: 4 (over y, x), lon: 8 (over z, core).
Axes of the slice: x: 2, y: 2, z: 4, core: 2. Of those that a mesh axis runs over, the one named last changes fastest.
Arguments:
- state: float32 [8, 256, 128, 256], P(None, 'rad', 'lon'), may hold values from -6 to 6
- flux_matrices: float32 [2, 8, 8], replicated, may hold values from -2 to 2
- wave_speed: float32 [2], replicated, may hold values from 0.5 to 2
- flux_volume: float32 [256, 128, 256], P('rad', 'lon'), may hold values from 0.02 to 0.2
- block_tile: int32 [8, 256, 1], P('lon', 'rad'), may hold values from 0 to 31; in each aligned block of 64 rows (0 to 63, 64 to 127, ..., all dimensions but the last counted through in order) at most 2 rows name the same one
- tile_of_device: int32 [32], replicated, may hold values from 0 to 31, each once
- phase_density: float32 [32, 200, 128], P(('rad', 'lon')), may hold values from -6 to 6
- injection: float32 [2, 200], replicated, may hold values from -3 to 3
- drift_courant: float32 [200], replicated, may hold values from 0.05 to 0.9
- energy_weight: float32 [200], replicated, may hold values from 0.01 to 0.1
Outputs:
- coupled_state: float32 [8, 256, 128, 256], P(None, 'rad', 'lon')
- drifted_density: float32 [32, 200, 128], P(('rad', 'lon'))
The draws below stay inside these ranges and needn't reach their ends.
Inputs may be any that keep to these rules, and one draw needn't show every extreme that they name: `block_tile`: in each longitude sector and each aligned run of 64 radial rows, no tile is reached by more than 2 blocks. `tile_of_device`: every tile has exactly one owner.
All inputs are finite; a program needn't handle non-finite values.
Results may differ from the reference program's by a relative error of at most 0.000067.
Values sent between devices are 32-bit elements; how exact they have to be, the bound alone decides.
No kernel may reach another device: no remote copies, remote signals or barrier semaphores. Data moves between devices by JAX's collectives and lax.ppermute only.
A program may use at most 192 MiB of HBM per device.

```python
import math
import jax
import jax.numpy as jnp
import numpy as np
from jax import lax

NF = 8
CR = 64
CL = 16
CZ = 256
ZSEG = 8
CH = 200
MOST = 2
DRIFT = 3
TP = 128
NR = 256
NL = 128
N_LON = 8
DEVICES = 32


def block_levels(key, shape, shards, smallest, high):
    loudness, own = 1.0, jax.random.fold_in(key, 6)
    for axis_at, shards_of in shards:
        steps = jnp.exp(jax.random.uniform(jax.random.fold_in(own, axis_at), (shards_of,), jnp.float32, smallest / len(shards), high / len(shards)))
        loudness = loudness * jnp.repeat(steps, shape[axis_at] // shards_of).reshape([-1 if axis == axis_at else 1 for axis in range(len(shape))])
    return loudness


def assign_block(stream_key, own, number, rows, number_of, top, limit, slope):
    order = jax.random.permutation(stream_key, number_of)
    packed, common = shares(number_of, rows * top, limit, slope, True), shares(number_of, rows * top, limit, slope, False)
    places = jnp.arange(number_of)

    def named(sizes, rotation):
        used = int((sizes > 0).sum())
        fixed = max(1, used // 4)
        moved = fixed + (places - fixed + rotation * (used - fixed)) % max(1, number_of - fixed)
        return jnp.zeros((number_of,), jnp.int32).at[order[jnp.where(places < fixed, places, moved)]].set(jnp.asarray(sizes, jnp.int32))

    sizes = jnp.where(number % 4 == 0, named(packed, number // 4), named(common, number - number // 4 - 1))
    mixed = jax.random.permutation(jax.random.fold_in(own, 3), number_of)
    donor, sink = mixed[0:number_of // 2 * 2:2], mixed[1:number_of // 2 * 2:2]
    slack = jnp.minimum(sizes[donor] - 1, limit - sizes[sink]) // 2
    slack = jnp.where((donor == order[0]) | (sink == order[0]) | (sizes[sink] == 0), 0, jnp.maximum(slack, 0))
    moved = jax.random.randint(jax.random.fold_in(own, 4), (number_of // 2,), 0, 1 << 20) % (slack + 1)
    sizes = sizes.at[donor].add(-moved).at[sink].add(moved)
    members = jnp.searchsorted(jnp.cumsum(sizes), jnp.arange(rows * top), side="right").astype(jnp.int32)
    grid = members.reshape(top, rows).T
    grid = grid[jax.random.permutation(jax.random.fold_in(own, 1), rows)]
    rotation = jax.random.randint(jax.random.fold_in(own, 2), (rows, 1), 0, top)
    return jnp.take_along_axis(grid, (jnp.arange(top)[None, :] + rotation) % top, axis=1)


def shares(number_of, total, reach, slope, full):
    weights = [(1 << 20) // math.isqrt(grade ** slope) + 1 for grade in range(1, number_of + 1)]
    largest = reach if full else min(reach, max(-(-total // number_of), total * weights[0] // sum(weights)))
    least = 1 if total - largest >= number_of - 1 else 0
    holding, surplus = [largest] + [least] * (number_of - 1), total - largest - least * (number_of - 1)
    while surplus > 0:
        free = [i for i in range(1, number_of) if holding[i] < largest] or [i for i in range(1, number_of) if holding[i] < reach]
        whole, budget = sum([weights[i] for i in free]), surplus
        for i in free:
            addition = min(reach - holding[i], max(1, budget * weights[i] // whole), surplus)
            holding[i] = holding[i] + addition
            surplus = surplus - addition
    return np.array(holding)


def gaussian(key, shape, scale, reach, shards=(), held_as=jnp.bfloat16):
    level = block_levels(key, shape, shards, -0.22, 0.18) if shards else 1.0
    values = jax.random.normal(key, shape, jnp.float32) * scale * level
    return jnp.minimum(jnp.maximum(values, -reach), reach).astype(held_as)


def setup_inputs(seed: int = 0) -> dict:
    keys = jax.random.split(jax.random.key(seed), 11)
    state = gaussian(keys[0], (NF, NR, NL, CZ), 1.0, 6.0, ((1, 4), (2, 8)), jnp.float32)
    flux_matrices = gaussian(keys[1], (2, NF, NF), NF ** -0.5, 2.0, (), jnp.float32)
    wave_speed = jnp.clip(jnp.exp(jax.random.uniform(keys[2], (2,), jnp.float32, math.log(0.5), math.log(2.0))), 0.5, 2.0)
    flux_volume = jnp.clip(jnp.exp(math.log(0.2) - 2.3025851 * jax.random.uniform(keys[3], (NR, NL, CZ), jnp.float32) ** block_levels(keys[3], (NR, NL, CZ), ((0, 4), (1, 8)), -0.2, 0.2)), 0.02, 0.2)
    block_tile_keys = jax.random.split(jax.random.fold_in(keys[4], 1), N_LON * NR // CR)
    block_tile_turns = jax.random.permutation(jax.random.fold_in(keys[4], 3), N_LON * NR // CR)
    block_tile = jax.vmap(lambda own, number: assign_block(jax.random.fold_in(keys[4], 2), own, number, CR, DEVICES, 1, MOST, 2))(block_tile_keys, block_tile_turns).reshape((N_LON, NR, 1))
    tile_of_device = jax.random.permutation(keys[5], DEVICES).astype(jnp.int32)
    phase_density = gaussian(keys[6], (DEVICES, CH, TP), 1.0, 6.0, ((0, 32),), jnp.float32)
    injection = gaussian(keys[7], (2, CH), 0.5, 3.0, (), jnp.float32)
    drift_courant = jnp.clip(jnp.exp(jax.random.uniform(keys[8], (CH,), jnp.float32, math.log(0.05), math.log(0.9))), 0.05, 0.9)
    energy_weight = jnp.clip(jnp.exp(jax.random.uniform(keys[9], (CH,), jnp.float32, math.log(0.01), math.log(0.1))), 0.01, 0.1)
    return {"state": state, "flux_matrices": flux_matrices, "wave_speed": wave_speed, "flux_volume": flux_volume, "block_tile": block_tile, "tile_of_device": tile_of_device, "phase_density": phase_density, "injection": injection, "drift_courant": drift_courant, "energy_weight": energy_weight}


courant_step = 0.4
nudge_rate = 0.5
inner_step = 0.5


def divergence(padded, along_axis, extent, matrix, wave_rate):
    shifted = [lax.slice_in_dim(padded, offset, offset + extent + 1, axis=along_axis) for offset in range(6)]
    left_state = (2.0 * shifted[0] - 13.0 * shifted[1] + 47.0 * shifted[2] + 27.0 * shifted[3] - 3.0 * shifted[4]) / 60.0
    right_state = (-3.0 * shifted[1] + 27.0 * shifted[2] + 47.0 * shifted[3] - 13.0 * shifted[4] + 2.0 * shifted[5]) / 60.0
    face_flux = 0.5 * jnp.einsum("ab,bxyz->axyz", matrix, left_state + right_state, precision=lax.Precision.HIGHEST) - 0.5 * wave_rate * (right_state - left_state)
    return lax.slice_in_dim(face_flux, 1, extent + 1, axis=along_axis) - lax.slice_in_dim(face_flux, 0, extent, axis=along_axis)


def reference(state, flux_matrices, wave_speed, flux_volume, block_tile, tile_of_device, phase_density, injection, drift_courant, energy_weight):
    seg_cells = CZ // ZSEG
    state_parts = jnp.moveaxis(state.reshape(NF, NR, NL, ZSEG, seg_cells), 3, 0)
    volume_parts = jnp.moveaxis(flux_volume.reshape(NR, NL, ZSEG, seg_cells), 2, 0)

    def advance(pair):
        segment, volume = pair
        radial = jnp.pad(segment, ((0, 0), (3, 3), (0, 0), (0, 0)))
        beside_all = jnp.pad(segment, ((0, 0), (0, 0), (3, 3), (0, 0)), mode="wrap")
        change = divergence(radial, 1, NR, flux_matrices[0], wave_speed[0]) + divergence(beside_all, 2, NL, flux_matrices[1], wave_speed[1])
        updated = segment - courant_step * change
        picked = jnp.stack([updated[0], updated[7]])
        return updated, jnp.sum(picked * volume[None], axis=-1)

    updated_parts, line_parts = lax.map(advance, (state_parts, volume_parts))
    line_sums = jnp.moveaxis(line_parts, 0, -1)
    payload = line_sums.reshape(2, NR, N_LON, CL, ZSEG).transpose(2, 1, 0, 3, 4).reshape(N_LON, NR, 2, TP)
    targets = block_tile[..., 0]
    one_hot = (targets[..., None] == jnp.arange(DEVICES, dtype=jnp.int32)).astype(jnp.float32)
    tile_source = jnp.einsum("jrt,jrcp->tcp", one_hot, payload, precision=lax.Precision.HIGHEST)
    owned_source = tile_source[tile_of_device]

    def inner(density_tile, source_tile):
        density = density_tile + inner_step * (injection[0][:, None] * source_tile[0][None, :] + injection[1][:, None] * source_tile[1][None, :])
        for substep in range(DRIFT):
            density = density - drift_courant[:, None] * (density - jnp.roll(density, 1, axis=1))
        return density, jnp.dot(energy_weight, density, precision=lax.Precision.HIGHEST)

    drifted_density, owner_pressure = jax.vmap(inner)(phase_density, owned_source)
    tile_pressure = jnp.zeros((DEVICES, TP), jnp.float32).at[tile_of_device].set(owner_pressure)
    returned = tile_pressure[targets]
    returned = returned.reshape(N_LON, NR, CL, ZSEG).transpose(1, 0, 2, 3).reshape(NR, NL, ZSEG)
    returned = jnp.moveaxis(returned, 2, 0)[..., None]
    pressure_old = updated_parts[:, 7]
    pressure_new = pressure_old + nudge_rate * (returned - pressure_old)
    coupled_parts = updated_parts.at[:, 7].set(pressure_new)
    coupled_state = jnp.moveaxis(coupled_parts, 0, 3).reshape(NF, NR, NL, CZ)
    return coupled_state, drifted_density
```

```python
import functools

import jax
import jax.numpy as jnp
import numpy as np
from jax import lax
from jax.experimental import pallas as pl
from jax.experimental.pallas import tpu as pltpu
from jax.sharding import PartitionSpec as P

ZSEG = 8
DRIFT = 3
REACH = 3

courant_step = 0.4
nudge_rate = 0.5
inner_step = 0.5

SUM_TAPS = {k: v / 60.0 for k, v in zip(range(-3, 4), (-2.0, 18.0, -90.0, 0.0, 90.0, -18.0, 2.0))}
GAP_TAPS = {k: v / 60.0 for k, v in zip(range(-3, 4), (2.0, -12.0, 30.0, -40.0, 30.0, -12.0, 2.0))}

PACKED = (0, 7, 1, 2, 3, 4, 5, 6)

f32 = jnp.float32
bf16 = jnp.bfloat16


def cost(flops, bytes_accessed):
    return pl.CostEstimate(flops=int(flops), bytes_accessed=int(bytes_accessed), transcendentals=0)


def parts_of(x, count):
    parts = []
    for _ in range(count):
        part = x.astype(bf16)
        parts.append(part)
        x = x - part.astype(f32)
    return parts


def dot(a, b):
    return jnp.dot(a, b, preferred_element_type=f32)


def exact_dot(x, ones):
    return sum(dot(part, ones) for part in parts_of(x, 3))


def lon_tables(rows, cols):
    fields = 1 + max(f for f, _ in cols)
    pick_row = np.array([[float(f == a) for a in range(fields)] for f, _ in rows], np.float32)
    pick_col = np.array([[float(f == b) for f, _ in cols] for b in range(fields)], np.float32)
    summed = np.array([[0.0 if s is None else SUM_TAPS.get(s - t, 0.0) for _, s in cols] for _, t in rows], np.float32)
    gapped = np.array(
        [[0.0 if s is None or f != g else GAP_TAPS.get(s - t, 0.0) for g, s in cols] for f, t in rows], np.float32
    )
    return pick_row, pick_col, summed, gapped


def lon_weights(matrix, wave_rate, pick_row, pick_col, summed, gapped):
    half = 0.5 * courant_step
    spread = f32_dot(f32_dot(pick_row, matrix), pick_col)
    return (half * wave_rate) * gapped - half * spread * summed


def f32_dot(a, b):
    return jnp.dot(a, b, precision=lax.Precision.HIGHEST, preferred_element_type=f32)


def whole(array):
    zeros = (0,) * array.ndim
    return pl.BlockSpec(array.shape, lambda *_: zeros)


SMEM = pl.BlockSpec(memory_space=pltpu.SMEM)
VMEM = pl.BlockSpec(memory_space=pltpu.VMEM)
HBM = pl.BlockSpec(memory_space=pltpu.HBM)
LARGE = pltpu.CompilerParams(vmem_limit_bytes=16 * 2**20)
SMALL = pltpu.CompilerParams(vmem_limit_bytes=4 * 2**20)
CHUNK = 8
AHEAD = 3


def in_vmem(*shape):
    return pltpu.VMEM(shape, f32)


def pinned(x):
    return pltpu.with_memory_space_constraint(x, pltpu.VMEM)


def lon_edge_kernel(lon_ref, rad_ref, place_ref, state_hbm, speed_hbm, matrix_hbm, table_hbm, cells, ids_ref, same, *refs):
    *crosses, speed_ref, matrix_ref, table_ref, weights, sem, few_sem = refs
    fields, rows, cols, depth = state_hbm.shape
    chunks = rows // CHUNK
    size = same.shape[1]

    def load(c):
        return pltpu.make_async_copy(
            state_hbm.at[:, pl.ds(c * CHUNK, CHUNK)], cells.at[:, pl.ds(REACH + c * CHUNK, CHUNK)], sem.at[c]
        )

    ids_ref[0] = lon_ref[0]
    ids_ref[1] = rad_ref[0]
    ids_ref[2] = place_ref[0]
    few = [
        pltpu.make_async_copy(source, target, few_sem.at[i])
        for i, (source, target) in enumerate(
            ((speed_hbm, speed_ref), (matrix_hbm, matrix_ref), (table_hbm, table_ref))
        )
    ]
    for copy in few:
        copy.start()
    for c in range(AHEAD):
        load(c).start()
    for edge in (0, REACH + rows):
        cells[:, edge : edge + REACH] = jnp.zeros((fields, REACH, cols, depth), f32)
    for copy in few:
        copy.wait()
    wide = 8 * fields
    w = lon_weights(
        matrix_ref[1], speed_ref[1], table_ref[0, :, :fields], table_ref[1, :fields, :wide], table_ref[2, :, :wide],
        table_ref[3, :, :wide],
    )
    swap = lon_ref[0] % 2 == 1
    w = jnp.concatenate([jnp.where(swap, w[size:], w[:size]), jnp.where(swap, w[:size], w[size:])], axis=0)
    high, low = parts_of(w, 2)
    weights[...] = jnp.concatenate([high, high, low], axis=1)
    low_half = lax.broadcasted_iota(jnp.int32, (fields, 8, depth), 1) < 4

    def step(c, carry):
        load(c).wait()

        @pl.when(c + AHEAD < chunks)
        def _():
            load(c + AHEAD).start()

        for j in range(CHUNK):
            r = c * CHUNK + j
            edge = jnp.where(low_half, cells[:, REACH + r, :8, :], cells[:, REACH + r, 8:, :])
            high, low = parts_of(edge.reshape(-1, depth), 2)
            sums = dot(weights[...], jnp.concatenate([high, low, high], axis=0))
            same[r] = sums[:size]
            for i, out in enumerate(crosses):
                out[r] = sums[size + 8 * i : size + 8 * i + 8]
        return carry

    lax.fori_loop(0, chunks, step, 0)


def lon_edges(state, matrices, speed, lon, rad, place):
    fields, rows, cols, depth = state.shape
    sources = [(f, l if l < 4 else cols - 8 + l) for f in range(fields) for l in range(8)]
    sources = [(f, l if l < REACH or l >= cols - REACH else None) for f, l in sources]
    to_right = [(f, cols + t) for f in PACKED for t in range(REACH)]
    to_left = [(f, t - REACH) for f in PACKED for t in range(REACH)]
    size = fields * REACH
    tables = np.zeros((4, 2 * size, 128), np.float32)
    for i, table in enumerate(lon_tables(to_right + to_left, sources)):
        tables[i, : table.shape[0], : table.shape[1]] = table
    tiles = size // 8
    return pl.pallas_call(
        lon_edge_kernel,
        in_specs=[SMEM] * 3 + [HBM] * 4,
        out_specs=[VMEM, SMEM] + [VMEM] * (1 + tiles),
        out_shape=[
            in_vmem(fields, rows + 2 * REACH, cols, depth),
            jax.ShapeDtypeStruct((3,), jnp.int32),
            in_vmem(rows, size, depth),
        ]
        + [in_vmem(rows, 8, depth)] * tiles,
        scratch_shapes=[
            pltpu.SMEM(speed.shape, f32),
            pltpu.VMEM(matrices.shape, f32),
            pltpu.VMEM(tables.shape, f32),
            pltpu.VMEM((2 * size, 3 * len(sources)), bf16),
            pltpu.SemaphoreType.DMA((rows // CHUNK,)),
            pltpu.SemaphoreType.DMA((3,)),
        ],
        compiler_params=LARGE,
        cost_estimate=cost(1e3, 1e3),
        name="lon_edges",
    )(lon, rad, place, *[pltpu.with_memory_space_constraint(x, pltpu.HBM) for x in (state, speed, matrices, jnp.asarray(tables))])


def turn_weights(matrix, pick, same):
    return (-0.5 * courant_step) * same * f32_dot(f32_dot(pick, matrix), pick.T)


def turn_tables(fields, cols):
    every = [(f, l) for f in range(fields) for l in range(cols)]
    pick = np.array([[float(f == a) for a in range(fields)] for f, _ in every], np.float32)
    same = np.array([[float(l == m) for _, m in every] for _, l in every], np.float32)
    return pick, same


def rad_edge_kernel(ids_ref, speed_ref, cells_ref, matrix_ref, pick_ref, same_ref, near_a, near_b, far_a, far_b):
    fields, padded, cols, depth = cells_ref.shape
    rate = (0.5 * courant_step) * speed_ref[0]
    even = ids_ref[1] % 2 == 0
    high, low = parts_of(turn_weights(matrix_ref[0], pick_ref[...], same_ref[...]), 2)
    w = jnp.concatenate([high, high, low], axis=1)

    def turned(cells):
        high, low = parts_of(cells.reshape(-1, depth), 2)
        return dot(w, jnp.concatenate([high, low, high], axis=0)).reshape(fields, cols, depth)

    first = [cells_ref[:, REACH + j] for j in range(REACH)]
    last = [cells_ref[:, padded - 2 * REACH + j] for j in range(REACH)]
    first_turned = [turned(cells) for cells in first]
    last_turned = [turned(cells) for cells in last]
    for t in range(REACH):
        up = sum(
            SUM_TAPS[j - REACH - t] * last_turned[j] + (rate * GAP_TAPS[j - REACH - t]) * last[j]
            for j in range(t, REACH)
        )
        down = sum(
            SUM_TAPS[j + REACH - t] * first_turned[j] + (rate * GAP_TAPS[j + REACH - t]) * first[j]
            for j in range(t + 1)
        )
        near, far = jnp.where(even, up, down), jnp.where(even, down, up)
        for total, a, b in ((near, near_a, near_b), (far, far_a, far_b)):
            a[0, t] = total[0]
            a[1, t] = total[7]
            b[:, t] = total[1:7]


def rad_edges(ids, cells, matrices, speed):
    fields, _, cols, depth = cells.shape
    tables = turn_tables(fields, cols)
    few, many = in_vmem(2, REACH, cols, depth), in_vmem(fields - 2, REACH, cols, depth)
    return pl.pallas_call(
        rad_edge_kernel,
        in_specs=[SMEM] * 2 + [VMEM] * (2 + len(tables)),
        out_specs=[VMEM] * 4,
        out_shape=[few, many, few, many],
        compiler_params=LARGE,
        cost_estimate=cost(1e3, 1e3),
        name="rad_edges",
    )(ids, speed, pinned(cells), matrices, *tables)


def add_radial(speed_ref, cells, turned, total, fields, first):
    cols, depth = total.shape[2:]
    rate = (0.5 * courant_step) * speed_ref[0]
    for f in fields:
        for half in range(cols // 8):
            for lane in range(depth // 128):
                lanes = pl.ds(128 * lane, 128)
                u = [cells[f, first + j, pl.ds(8 * half, 8), lanes] for j in range(CHUNK + 2 * REACH)]
                v = [turned[first + j, pl.ds(f * cols + 8 * half, 8), lanes] for j in range(CHUNK + 2 * REACH)]
                for j in range(CHUNK):
                    at = j + REACH
                    value = total[f, first + j, pl.ds(8 * half, 8), lanes] + (rate * GAP_TAPS[0]) * u[at]
                    for k in range(1, REACH + 1):
                        value = value + SUM_TAPS[k] * (v[at + k] - v[at - k])
                        value = value + (rate * GAP_TAPS[k]) * (u[at + k] + u[at - k])
                    total[f, first + j, pl.ds(8 * half, 8), lanes] = value


def local_kernel(mine, speed_ref, cells, matrix_ref, pick_ref, same_ref, sum_ref, gap_ref, total, turned, w_ref):
    _, rows, cols, depth = total.shape
    chunks = rows // CHUNK
    pick = pick_ref[...]
    own = lon_weights(matrix_ref[1], speed_ref[1], pick, pick.T, sum_ref[...], gap_ref[...])
    turn = turn_weights(matrix_ref[0], pick, same_ref[...])
    own, turn = [jnp.concatenate([w[f * cols : (f + 1) * cols] for f in mine], axis=0) for w in (own, turn)]
    high, low = parts_of(jnp.concatenate([own, turn], axis=0), 2)
    w_ref[...] = jnp.concatenate([high, high, low], axis=1)
    size = len(mine) * cols
    for edge in (0, REACH + rows):
        turned[edge : edge + REACH] = jnp.zeros((REACH, size, depth), f32)

    def rows_of(c, carry):
        for j in range(CHUNK):
            r = c * CHUNK + j
            high, low = parts_of(cells[:, REACH + r].reshape(-1, depth), 2)
            both = dot(w_ref[...], jnp.concatenate([high, low, high], axis=0))
            for i, f in enumerate(mine):
                total[i, r] = cells[f, REACH + r] + both[i * cols : (i + 1) * cols]
            turned[REACH + r] = both[size:]
        return carry

    rate = (0.5 * courant_step) * speed_ref[0]

    def radial(c, carry):
        first = c * CHUNK
        for i, f in enumerate(mine):
            for half in range(cols // 8):
                for lane in range(depth // 128):
                    lanes, subs = pl.ds(128 * lane, 128), pl.ds(8 * half, 8)
                    u = [cells[f, first + j, subs, lanes] for j in range(CHUNK + 2 * REACH)]
                    v = [
                        turned[first + j, pl.ds(i * cols + 8 * half, 8), lanes] for j in range(CHUNK + 2 * REACH)
                    ]
                    for j in range(CHUNK):
                        at = j + REACH
                        value = total[i, first + j, subs, lanes] + (rate * GAP_TAPS[0]) * u[at]
                        for k in range(1, REACH + 1):
                            value = value + SUM_TAPS[k] * (v[at + k] - v[at - k])
                            value = value + (rate * GAP_TAPS[k]) * (u[at + k] + u[at - k])
                        total[i, first + j, subs, lanes] = value
        return carry

    lax.fori_loop(0, chunks, rows_of, 0)
    lax.fori_loop(0, chunks, radial, 0)


def local_update(mine, cells, matrices, speed):
    fields, padded, cols, depth = cells.shape
    rows = padded - 2 * REACH
    every = [(f, l) for f in range(fields) for l in range(cols)]
    _, _, summed, gapped = lon_tables(every, every)
    size = len(mine) * cols
    return pl.pallas_call(
        functools.partial(local_kernel, mine),
        in_specs=[SMEM] + [VMEM] * 6,
        out_specs=VMEM,
        out_shape=in_vmem(len(mine), rows, cols, depth),
        scratch_shapes=[
            pltpu.VMEM((padded, size, depth), f32),
            pltpu.VMEM((2 * size, 3 * fields * cols), bf16),
        ],
        compiler_params=LARGE,
        cost_estimate=cost(1e3, 1e3),
        name="local_update",
    )(speed, pinned(cells), matrices, *turn_tables(fields, cols), summed, gapped)


def placed(tiles, field, from_left):
    start = REACH * PACKED.index(field)
    tile, offset = start // 8, start % 8
    cells = tiles[tile]
    sub = lax.broadcasted_iota(jnp.int32, cells.shape, 1)
    if offset + REACH > 8:
        cells = jnp.where(sub >= offset, cells, tiles[tile + 1])
    goal = 0 if from_left else 8 - REACH
    shift = (goal - offset) % 8
    if shift:
        cells = pltpu.roll(cells, shift, 1)
    keep = sub < REACH if from_left else sub >= 8 - REACH
    return jnp.where(keep, cells, 0.0)


def by_side(lon, same, crosses):
    even = lon % 2 == 0
    lefts, rights = {}, {}
    for t, cross in enumerate(crosses):
        near = same[:, 8 * t : 8 * t + 8]
        lefts[t] = jnp.where(even, cross, near)
        rights[t] = jnp.where(even, near, cross)
    return lefts, rights


def with_sides(cells, lefts, rights, field):
    cols = cells.shape[1]
    return jnp.concatenate(
        [cells[:, :8] + placed(lefts, field, True), cells[:, cols - 8 :] + placed(rights, field, False)], axis=1
    )


def with_ends(cells, step, steps, rad, near, far):
    rows = cells.shape[0]
    even = rad % 2 == 0
    below, above = jnp.where(even, far, near), jnp.where(even, near, far)
    at_low = (step == 0).astype(f32)
    at_top = (step == steps - 1).astype(f32)
    return jnp.concatenate(
        [cells[:REACH] + at_low * below, cells[REACH : rows - REACH], cells[rows - REACH :] + at_top * above], axis=0
    )


def tile_sum_kernel(
    ids_ref, part_ref, vol_ref, same_ref, cross_ref, near_ref, far_ref, rest_ref, hit_ref, seg_ref, spot_ref,
    out_ref, lines_ref,
):
    all_rows, cols, depth = vol_ref.shape
    tiles, points = out_ref.shape[0], out_ref.shape[1] // 3
    rows = 16
    steps = all_rows // rows

    def add(step, carry):
        here = pl.ds(pl.multiple_of(step * rows, rows), rows)
        lefts, rights = by_side(ids_ref[0], same_ref[here, :8], [cross_ref[here]])
        vol = vol_ref[here]
        for c, field in enumerate((0, 7)):
            cells = with_sides(part_ref[c, here], lefts, rights, field)
            cells = with_ends(cells, step, steps, ids_ref[1], near_ref[c], far_ref[c])
            lines = exact_dot((cells * vol).reshape(rows * cols, depth), seg_ref[...])
            lines_ref[c, here] = jnp.sum(lines.reshape(rows, cols, -1) * spot_ref[...][None], axis=1)
        return carry

    lax.fori_loop(0, steps, add, 0)
    for c in range(2):
        sums = sum(dot(hit_ref[...], part) for part in parts_of(lines_ref[c], 3))
        out_ref[:, c * points : (c + 1) * points] = sums
    mine = lax.broadcasted_iota(jnp.int32, (tiles, points), 0) == ids_ref[2]
    out_ref[:, 2 * points :] = jnp.where(mine, rest_ref[8:9], 0.0)


def tile_sums(ids, part, vol, same, cross, near, far, rest, hits, seg, spot):
    _, rows, _, _ = part.shape
    points = seg.shape[1]
    tiles = hits.shape[0]
    return pl.pallas_call(
        tile_sum_kernel,
        in_specs=[SMEM] + [VMEM] * 10,
        out_specs=VMEM,
        out_shape=in_vmem(tiles, 3 * points),
        scratch_shapes=[pltpu.VMEM((2, rows, points), f32)],
        compiler_params=LARGE,
        cost_estimate=cost(1e3, 1e3),
        name="tile_sums",
    )(ids, *[pinned(x) for x in (part, vol, same, cross, near, far, rest)], hits, seg, spot)


def drifted(density, courant):
    for _ in range(DRIFT):
        density = density - courant * (density - pltpu.roll(density, 1, 1))
    return density


def columns_of(packed_ref, channels):
    turned = jnp.transpose(packed_ref[...])
    return [turned[:channels, i : i + 1] for i in range(4)]


def rest_kernel(density_ref, packed_ref, out_ref):
    _, channels, points = density_ref.shape
    courant, weight, first, second = columns_of(packed_ref, channels)
    rows = []
    for given in (first, second):
        for k, choices in enumerate((1.0, 3.0, 3.0, 1.0)):
            gain = (inner_step * choices) * weight * given
            for _ in range(k):
                gain = gain * courant
            for _ in range(DRIFT - k):
                gain = gain * (1.0 - courant)
            rows.append(jnp.broadcast_to(jnp.sum(gain, axis=0, keepdims=True), (1, points)))
    rest = jnp.sum(weight * drifted(density_ref[0], courant), axis=0, keepdims=True)
    out_ref[...] = jnp.concatenate(rows + [rest] * 8, axis=0)


def rest_of(density, packed):
    points = density.shape[2]
    return pl.pallas_call(
        rest_kernel,
        out_shape=jax.ShapeDtypeStruct((16, points), f32),
        compiler_params=SMALL,
        cost_estimate=cost(1e3, 1e3),
        name="rest_pressure",
    )(density, packed)


def drift_kernel(ids_ref, density_ref, packed_ref, sums_ref, out_ref):
    _, channels, points = density_ref.shape
    courant, _, first, second = columns_of(packed_ref, channels)
    source = sums_ref[pl.ds(ids_ref[2], 1), :]
    density = density_ref[0] + inner_step * (first * source[:, :points] + second * source[:, points : 2 * points])
    out_ref[0] = drifted(density, courant)


def drift(ids, density, packed, sums):
    return pl.pallas_call(
        drift_kernel,
        in_specs=[SMEM] + [VMEM] * 3,
        out_shape=jax.ShapeDtypeStruct(density.shape, f32),
        compiler_params=SMALL,
        cost_estimate=cost(1e3, 1e3),
        name="drift",
    )(ids, density, packed, sums)


def pressures_of(sums, rest_ref):
    points = sums.shape[1] // 3
    pressure = sums[:, 2 * points :]
    for c in range(2):
        source = sums[:, c * points : (c + 1) * points]
        for k in range(DRIFT + 1):
            shifted = pltpu.roll(source, k, 1) if k else source
            pressure = pressure + rest_ref[(DRIFT + 1) * c + k : (DRIFT + 1) * c + k + 1] * shifted
    return pressure


def finish_kernel(
    ids_ref, ends_ref, part_ref, near_a, far_a, near_b, far_b, same_ref, cross_0, cross_1, cross_2,
    hit_ref, sums_ref, rest_ref, spot_ref, seg_ref, out_hbm, done, back_ref, sem,
):
    fields, all_rows, cols, depth = done.shape
    rows = CHUNK
    steps = all_rows // rows

    def store(field):
        return pltpu.make_async_copy(done.at[field], out_hbm.at[field], sem.at[field])

    def run(field):
        def step(i, carry):
            here = pl.ds(pl.multiple_of(i * rows, rows), rows)
            first = REACH * PACKED.index(field) // 8
            last = (REACH * PACKED.index(field) + REACH - 1) // 8
            lefts, rights = {}, {}
            for t in range(first, last + 1):
                one = by_side(ids_ref[0], same_ref[here, 8 * t : 8 * t + 8], [(cross_0, cross_1, cross_2)[t][here]])
                lefts[t], rights[t] = one[0][0], one[1][0]
            if field in (0, fields - 1):
                near, far = near_a[field // (fields - 1)], far_a[field // (fields - 1)]
                own = ends_ref[field // (fields - 1), here]
            else:
                near, far = near_b[field - 1], far_b[field - 1]
                own = part_ref[field - 1, here]
            cells = with_sides(own, lefts, rights, field)
            cells = with_ends(cells, i, steps, ids_ref[1], near, far)
            if field == fields - 1:
                spread = (back_ref[here][:, None, :] * spot_ref[...][None]).reshape(rows * cols, -1)
                returned = exact_dot(spread, seg_ref[...]).reshape(rows, cols, depth)
                cells = cells + nudge_rate * (returned - cells)
            done[field, here] = cells
            return carry

        lax.fori_loop(0, steps, step, 0)
        store(field).start()

    for field in range(fields - 3):
        run(field)
    back_ref[...] = sum(dot(hit_ref[...], p) for p in parts_of(pressures_of(sums_ref[...], rest_ref), 3))
    run(fields - 1)
    run(fields - 3)
    run(fields - 2)
    for field in range(fields):
        store(field).wait()


def finish(ids, ends, part, rad_a, rad_b, same, crosses, hits, sums, rest, spot, seg):
    _, rows, cols, depth = part.shape
    shape = (ends.shape[0] + part.shape[0], rows, cols, depth)
    pins = [pinned(x) for x in (ends, part, *rad_a, *rad_b, same, *crosses)]
    return pl.pallas_call(
        finish_kernel,
        in_specs=[SMEM] + [VMEM] * (len(pins) + 5),
        out_specs=HBM,
        out_shape=jax.ShapeDtypeStruct(shape, f32),
        scratch_shapes=[
            pltpu.VMEM(shape, f32),
            pltpu.VMEM((rows, spot.shape[1]), f32),
            pltpu.SemaphoreType.DMA((shape[0],)),
        ],
        compiler_params=LARGE,
        cost_estimate=cost(1e3, 1e3),
        name="finish",
    )(ids, *pins, hits, sums, rest, spot, seg)


def swap(x, axis, bit):
    return lax.ppermute(x, axis, [(i, i ^ bit) for i in range(lax.axis_size(axis))])


def per_device(
    state,
    flux_matrices,
    wave_speed,
    flux_volume,
    block_tile,
    tile_of_device,
    phase_density,
    injection,
    drift_courant,
    energy_weight,
):
    fields, rows, cols, depth = state.shape
    n_rad, n_lon = lax.axis_size("rad"), lax.axis_size("lon")
    points = cols * ZSEG
    lon, rad, place = [lax.axis_index(axes).astype(jnp.int32).reshape(1) for axes in ("lon", "rad", ("rad", "lon"))]

    across = [(i, (i + 1 if i % 2 else i - 1) % n_lon) for i in range(n_lon)]
    beyond = [(i, j) for i in range(n_rad) for j in [i + 1 if i % 2 else i - 1] if 0 <= j < n_rad]
    cells, ids, same, *crosses = lon_edges(state, flux_matrices, wave_speed, lon, rad, place)
    cross_0 = lax.ppermute(crosses[0], "lon", across)
    same = swap(same, "lon", 1)
    cross_1 = lax.ppermute(crosses[1], "lon", across)

    near_a, near_b, far_a, far_b = rad_edges(ids, cells, flux_matrices, wave_speed)
    rad_a = swap(near_a, "rad", 1), lax.ppermute(far_a, "rad", beyond)

    packed = jnp.concatenate([drift_courant[None], energy_weight[None], injection], axis=0)
    packed = jnp.pad(packed, ((0, 4), (0, -packed.shape[1] % 128)))
    rest = rest_of(phase_density, packed)

    ends = local_update((0, fields - 1), cells, flux_matrices, wave_speed)

    targets = block_tile[0, :, 0]
    hits = (tile_of_device[:, None] == targets[None, :]).astype(bf16)
    hits_back = (targets[:, None] == tile_of_device[None, :]).astype(bf16)
    seg_cells = depth // ZSEG
    seg = np.array([[float(p % ZSEG == z // seg_cells) for p in range(points)] for z in range(depth)], np.float32)
    spot = np.array([[float(p // ZSEG == l) for p in range(points)] for l in range(cols)], np.float32)
    sums = tile_sums(
        ids, ends, flux_volume, same, cross_0, *rad_a, rest, hits, jnp.asarray(seg, bf16), jnp.asarray(spot)
    )
    def summed(sums, axis, steps):
        return sum([swap(sums, axis, step) for step in steps], sums)

    sums = summed(sums, "rad", range(1, n_rad))
    near_b, far_b, sums = lax.optimization_barrier((near_b, far_b, sums))
    rad_b = swap(near_b, "rad", 1), lax.ppermute(far_b, "rad", beyond)
    sums = summed(sums, "lon", [1])
    sums, cross_1 = lax.optimization_barrier((sums, cross_1))
    sums = summed(sums, "lon", range(2, n_lon, 2))
    last, sums = lax.optimization_barrier((crosses[2], sums))
    cross_2 = lax.ppermute(last, "lon", across)
    part = local_update(tuple(range(1, fields - 1)), cells, flux_matrices, wave_speed)
    density = drift(ids, phase_density, packed, sums)

    done = finish(
        ids, ends, part, rad_a, rad_b, same, (cross_0, cross_1, cross_2), hits_back, sums, rest, jnp.asarray(spot),
        jnp.asarray(seg.T, bf16),
    )
    return done, density


def solution(mesh):
    in_specs = (
        P(None, "rad", "lon", None),
        P(),
        P(),
        P("rad", "lon", None),
        P("lon", "rad", None),
        P(),
        P(("rad", "lon"), None, None),
        P(),
        P(),
        P(),
    )
    out_specs = (P(None, "rad", "lon", None), P(("rad", "lon"), None, None))
    return jax.shard_map(per_device, mesh=mesh, in_specs=in_specs, out_specs=out_specs, check_vma=False)
```

```python
import functools

import jax
import jax.numpy as jnp
import numpy as np
from jax import lax
from jax.experimental import pallas as pl
from jax.experimental.pallas import tpu as pltpu
from jax.sharding import PartitionSpec as P

ZSEG = 8
DRIFT = 3
REACH = 3

courant_step = 0.4
nudge_rate = 0.5
inner_step = 0.5

SUM_TAPS = {k: v / 60.0 for k, v in zip(range(-3, 4), (-2.0, 18.0, -90.0, 0.0, 90.0, -18.0, 2.0))}
GAP_TAPS = {k: v / 60.0 for k, v in zip(range(-3, 4), (2.0, -12.0, 30.0, -40.0, 30.0, -12.0, 2.0))}

PACKED = (0, 7, 1, 2, 3, 4, 5, 6)

f32 = jnp.float32
bf16 = jnp.bfloat16


def cost(flops, bytes_accessed):
    return pl.CostEstimate(flops=int(flops), bytes_accessed=int(bytes_accessed), transcendentals=0)


def parts_of(x, count):
    parts = []
    for _ in range(count):
        part = x.astype(bf16)
        parts.append(part)
        x = x - part.astype(f32)
    return parts


def dot(a, b):
    return jnp.dot(a, b, preferred_element_type=f32)


def exact_dot(x, ones):
    return sum(dot(part, ones) for part in parts_of(x, 3))


def lon_tables(rows, cols):
    fields = 1 + max(f for f, _ in cols)
    pick_row = np.array([[float(f == a) for a in range(fields)] for f, _ in rows], np.float32)
    pick_col = np.array([[float(f == b) for f, _ in cols] for b in range(fields)], np.float32)
    summed = np.array([[0.0 if s is None else SUM_TAPS.get(s - t, 0.0) for _, s in cols] for _, t in rows], np.float32)
    gapped = np.array(
        [[0.0 if s is None or f != g else GAP_TAPS.get(s - t, 0.0) for g, s in cols] for f, t in rows], np.float32
    )
    return pick_row, pick_col, summed, gapped


def lon_weights(matrix, wave_rate, pick_row, pick_col, summed, gapped):
    half = 0.5 * courant_step
    spread = f32_dot(f32_dot(pick_row, matrix), pick_col)
    return (half * wave_rate) * gapped - half * spread * summed


def f32_dot(a, b):
    return jnp.dot(a, b, precision=lax.Precision.HIGHEST, preferred_element_type=f32)


def whole(array):
    zeros = (0,) * array.ndim
    return pl.BlockSpec(array.shape, lambda *_: zeros)


SMEM = pl.BlockSpec(memory_space=pltpu.SMEM)
VMEM = pl.BlockSpec(memory_space=pltpu.VMEM)
HBM = pl.BlockSpec(memory_space=pltpu.HBM)
LARGE = pltpu.CompilerParams(vmem_limit_bytes=18 * 2**20)
SMALL = pltpu.CompilerParams(vmem_limit_bytes=4 * 2**20)
CHUNK = 8
AHEAD = 3
GROUP = 4
RING = 4


def in_vmem(*shape):
    return pltpu.VMEM(shape, f32)


def pinned(x):
    return pltpu.with_memory_space_constraint(x, pltpu.VMEM)


def lon_edge_kernel(lon_ref, rad_ref, place_ref, state_hbm, speed_hbm, matrix_hbm, table_hbm, rim, ids_ref, same, *refs):
    *crosses, speed_ref, matrix_ref, table_ref, edges, weights, sem, few_sem = refs
    fields, rows, cols, depth = state_hbm.shape
    chunks = rows // CHUNK
    size = same.shape[1]
    keep = edges.shape[2] // 2

    def loads(c):
        here = pl.ds(c * CHUNK, CHUNK)
        return [
            pltpu.make_async_copy(
                state_hbm.at[:, here, pl.ds(first, keep)], edges.at[:, here, pl.ds(slot, keep)], sem.at[2 * c + i]
            )
            for i, (first, slot) in enumerate(((0, 0), (cols - keep, keep)))
        ]

    few = [(speed_hbm, speed_ref), (matrix_hbm, matrix_ref), (table_hbm, table_ref)]
    few += [(state_hbm.at[:, pl.ds(0, REACH)], rim.at[:, pl.ds(0, REACH)])]
    few += [(state_hbm.at[:, pl.ds(rows - REACH, REACH)], rim.at[:, pl.ds(REACH, REACH)])]
    few = [pltpu.make_async_copy(source, target, few_sem.at[i]) for i, (source, target) in enumerate(few)]
    for copy in few[:3]:
        copy.start()
    for c in range(chunks):
        for copy in loads(c):
            copy.start()
    for copy in few[3:]:
        copy.start()
    ids_ref[0] = lon_ref[0]
    ids_ref[1] = rad_ref[0]
    ids_ref[2] = place_ref[0]
    for copy in few[:3]:
        copy.wait()
    wide = 8 * fields
    w = lon_weights(
        matrix_ref[1], speed_ref[1], table_ref[0, :, :fields], table_ref[1, :fields, :wide], table_ref[2, :, :wide],
        table_ref[3, :, :wide],
    )
    swap = lon_ref[0] % 2 == 1
    w = jnp.concatenate([jnp.where(swap, w[size:], w[:size]), jnp.where(swap, w[:size], w[size:])], axis=0)
    high, low = parts_of(w, 2)
    weights[...] = jnp.concatenate([high, high, low], axis=1)

    def step(c, carry):
        for copy in loads(c):
            copy.wait()
        for j in range(CHUNK):
            r = c * CHUNK + j
            high, low = parts_of(edges[:, r].reshape(-1, depth), 2)
            sums = dot(weights[...], jnp.concatenate([high, low, high], axis=0))
            same[r] = sums[:size]
            first, rest = crosses
            first[r] = sums[size : size + 8]
            rest[r] = sums[size + 8 :]
        return carry

    lax.fori_loop(0, chunks, step, 0)
    for copy in few[3:]:
        copy.wait()


def lon_edges(state, matrices, speed, lon, rad, place):
    fields, rows, cols, depth = state.shape
    keep = 4
    sources = [(f, l if l < keep else cols - 2 * keep + l) for f in range(fields) for l in range(2 * keep)]
    sources = [(f, l if l < REACH or l >= cols - REACH else None) for f, l in sources]
    to_right = [(f, cols + t) for f in PACKED for t in range(REACH)]
    to_left = [(f, t - REACH) for f in PACKED for t in range(REACH)]
    size = fields * REACH
    tables = np.zeros((4, 2 * size, 128), np.float32)
    for i, table in enumerate(lon_tables(to_right + to_left, sources)):
        tables[i, : table.shape[0], : table.shape[1]] = table
    return pl.pallas_call(
        lon_edge_kernel,
        in_specs=[SMEM] * 3 + [HBM] * 4,
        out_specs=[VMEM, SMEM] + [VMEM] * 3,
        out_shape=[
            in_vmem(fields, 2 * REACH, cols, depth),
            jax.ShapeDtypeStruct((3,), jnp.int32),
            in_vmem(rows, size, depth),
            in_vmem(rows, 8, depth),
            in_vmem(rows, size - 8, depth),
        ],
        scratch_shapes=[
            pltpu.SMEM(speed.shape, f32),
            pltpu.VMEM(matrices.shape, f32),
            pltpu.VMEM(tables.shape, f32),
            pltpu.VMEM((fields, rows, 2 * keep, depth), f32),
            pltpu.VMEM((2 * size, 3 * len(sources)), bf16),
            pltpu.SemaphoreType.DMA((2 * rows // CHUNK,)),
            pltpu.SemaphoreType.DMA((5,)),
        ],
        compiler_params=LARGE,
        cost_estimate=cost(1e3, 1e3),
        name="lon_edges",
    )(lon, rad, place, *[pltpu.with_memory_space_constraint(x, pltpu.HBM) for x in (state, speed, matrices, jnp.asarray(tables))])


def turn_weights(matrix, pick, same):
    return (-0.5 * courant_step) * same * f32_dot(f32_dot(pick, matrix), pick.T)


def turn_tables(fields, cols):
    every = [(f, l) for f in range(fields) for l in range(cols)]
    pick = np.array([[float(f == a) for a in range(fields)] for f, _ in every], np.float32)
    same = np.array([[float(l == m) for _, m in every] for _, l in every], np.float32)
    return pick, same


def rad_edge_kernel(ids_ref, speed_ref, rim_ref, matrix_ref, pick_ref, same_ref, near, far_a, far_b):
    fields, _, cols, depth = rim_ref.shape
    rate = (0.5 * courant_step) * speed_ref[0]
    even = ids_ref[1] % 2 == 0
    high, low = parts_of(turn_weights(matrix_ref[0], pick_ref[...], same_ref[...]), 2)
    w = jnp.concatenate([high, high, low], axis=1)

    def turned(cells):
        high, low = parts_of(cells.reshape(-1, depth), 2)
        return dot(w, jnp.concatenate([high, low, high], axis=0)).reshape(fields, cols, depth)

    first = [rim_ref[:, j] for j in range(REACH)]
    last = [rim_ref[:, REACH + j] for j in range(REACH)]
    first_turned = [turned(cells) for cells in first]
    last_turned = [turned(cells) for cells in last]
    for t in range(REACH):
        up = sum(
            SUM_TAPS[j - REACH - t] * last_turned[j] + (rate * GAP_TAPS[j - REACH - t]) * last[j]
            for j in range(t, REACH)
        )
        down = sum(
            SUM_TAPS[j + REACH - t] * first_turned[j] + (rate * GAP_TAPS[j + REACH - t]) * first[j]
            for j in range(t + 1)
        )
        near[:, t] = jnp.where(even, up, down)
        far = jnp.where(even, down, up)
        far_a[0, t] = far[0]
        far_a[1, t] = far[fields - 1]
        far_b[:, t] = far[1 : fields - 1]


def rad_edges(ids, rim, matrices, speed):
    fields, _, cols, depth = rim.shape
    tables = turn_tables(fields, cols)
    return pl.pallas_call(
        rad_edge_kernel,
        in_specs=[SMEM] * 2 + [VMEM] * (2 + len(tables)),
        out_specs=[VMEM] * 3,
        out_shape=[in_vmem(n, REACH, cols, depth) for n in (fields, 2, fields - 2)],
        compiler_params=LARGE,
        cost_estimate=cost(1e3, 1e3),
        name="rad_edges",
    )(ids, speed, pinned(rim), matrices, *tables)


def add_radial(speed_ref, cells, turned, total, fields, first):
    cols, depth = total.shape[2:]
    rate = (0.5 * courant_step) * speed_ref[0]
    for f in fields:
        for half in range(cols // 8):
            for lane in range(depth // 128):
                lanes = pl.ds(128 * lane, 128)
                u = [cells[f, first + j, pl.ds(8 * half, 8), lanes] for j in range(CHUNK + 2 * REACH)]
                v = [turned[first + j, pl.ds(f * cols + 8 * half, 8), lanes] for j in range(CHUNK + 2 * REACH)]
                for j in range(CHUNK):
                    at = j + REACH
                    value = total[f, first + j, pl.ds(8 * half, 8), lanes] + (rate * GAP_TAPS[0]) * u[at]
                    for k in range(1, REACH + 1):
                        value = value + SUM_TAPS[k] * (v[at + k] - v[at - k])
                        value = value + (rate * GAP_TAPS[k]) * (u[at + k] + u[at - k])
                    total[f, first + j, pl.ds(8 * half, 8), lanes] = value


def local_kernel(speed_ref, state_hbm, matrix_ref, pick_ref, same_ref, sum_ref, gap_ref, total, cells, w_ref, sem, *scratch):
    fields, rows, cols, depth = total.shape
    size = fields * cols
    turned, base = scratch[:RING], scratch[RING:]
    rate = (0.5 * courant_step) * speed_ref[0]
    last_row = cells.shape[1] - 1
    chunks = rows // CHUNK

    def load(c):
        return pltpu.make_async_copy(
            state_hbm.at[:, pl.ds(c * CHUNK, CHUNK)], cells.at[:, pl.ds(REACH + c * CHUNK, CHUNK)], sem.at[c]
        )

    for c in range(AHEAD):
        load(c).start()
    w_ref[...] = local_weights(
        matrix_ref, speed_ref, pick_ref[...], same_ref[...], sum_ref[...], gap_ref[...]
    )
    for edge in (0, REACH + rows):
        cells[:, edge : edge + REACH] = jnp.zeros((fields, REACH, cols, depth), f32)

    def multiply(c, slot, j):
        r = jnp.minimum(REACH + c * GROUP + j, last_row)
        here = cells[:, r].reshape(size, depth)
        high, low = parts_of(here, 2)
        both = dot(w_ref[...], jnp.concatenate([high, low, high], axis=0))
        base[slot][j] = here + both[:size]
        turned[slot][j] = both[size:]

    def radial(c, slot, quarter):
        first = c * GROUP
        groups = fields * (cols // 8) * (depth // 128)
        for g in range(quarter * groups // GROUP, (quarter + 1) * groups // GROUP):
            f, rest = divmod(g, (cols // 8) * (depth // 128))
            half, lane = divmod(rest, depth // 128)
            lanes = pl.ds(128 * lane, 128)
            u = [cells[f, first + j, pl.ds(8 * half, 8), lanes] for j in range(GROUP + 2 * REACH)]
            v = []
            for j in range(-REACH, GROUP + REACH):
                ref = turned[(slot + j // GROUP) % RING]
                v.append(ref[j % GROUP, pl.ds(f * cols + 8 * half, 8), lanes])
            for j in range(GROUP):
                at = j + REACH
                value = base[slot][j, pl.ds(f * cols + 8 * half, 8), lanes] + (rate * GAP_TAPS[0]) * u[at]
                for k in range(1, REACH + 1):
                    value = value + SUM_TAPS[k] * (v[at + k] - v[at - k])
                    value = value + (rate * GAP_TAPS[k]) * (u[at + k] + u[at - k])
                total[f, first + j, pl.ds(8 * half, 8), lanes] = value

    turned[RING - 1][...] = jnp.zeros((GROUP, size, depth), f32)
    load(0).wait()
    load(AHEAD).start()
    for c in range(2):
        for j in range(GROUP):
            multiply(c, c, j)

    ahead = GROUP * RING // CHUNK

    def step(i, carry):
        for c in range(1, ahead + 1):

            @pl.when(ahead * i + c < chunks)
            def _():
                load(ahead * i + c).wait()

            @pl.when(ahead * i + c + AHEAD < chunks)
            def _():
                load(ahead * i + c + AHEAD).start()

        for q in range(RING):
            for j in range(GROUP):
                multiply(RING * i + q + 2, (q + 2) % RING, j)
                radial(RING * i + q, q, j)
        return carry

    lax.fori_loop(0, rows // (GROUP * RING), step, 0)


def local_weights(matrices, speed_ref, pick, same, summed, gapped):
    own = lon_weights(matrices[1], speed_ref[1], pick, pick.T, summed, gapped)
    high, low = parts_of(jnp.concatenate([own, turn_weights(matrices[0], pick, same)], axis=0), 2)
    return jnp.concatenate([high, high, low], axis=1)


def local_update(state, matrices, speed):
    fields, rows, cols, depth = state.shape
    size = fields * cols
    every = [(f, l) for f in range(fields) for l in range(cols)]
    _, _, summed, gapped = lon_tables(every, every)
    return pl.pallas_call(
        local_kernel,
        in_specs=[SMEM, HBM] + [VMEM] * 5,
        out_specs=VMEM,
        out_shape=in_vmem(fields, rows, cols, depth),
        scratch_shapes=[
            pltpu.VMEM((fields, rows + 2 * REACH, cols, depth), f32),
            pltpu.VMEM((2 * size, 3 * size), bf16),
            pltpu.SemaphoreType.DMA((rows // CHUNK,)),
        ]
        + [pltpu.VMEM((GROUP, size, depth), f32)] * (2 * RING),
        compiler_params=LARGE,
        cost_estimate=cost(1e3, 1e3),
        name="local_update",
    )(
        speed, pltpu.with_memory_space_constraint(state, pltpu.HBM), matrices, *turn_tables(fields, cols), summed, gapped
    )


def placed(tiles, field, from_left):
    start = REACH * PACKED.index(field)
    tile, offset = start // 8, start % 8
    cells = tiles[tile]
    sub = lax.broadcasted_iota(jnp.int32, cells.shape, 1)
    if offset + REACH > 8:
        cells = jnp.where(sub >= offset, cells, tiles[tile + 1])
    goal = 0 if from_left else 8 - REACH
    shift = (goal - offset) % 8
    if shift:
        cells = pltpu.roll(cells, shift, 1)
    keep = sub < REACH if from_left else sub >= 8 - REACH
    return jnp.where(keep, cells, 0.0)


def by_side(lon, same, crosses):
    even = lon % 2 == 0
    lefts, rights = {}, {}
    for t, cross in enumerate(crosses):
        near = same[:, 8 * t : 8 * t + 8]
        lefts[t] = jnp.where(even, cross, near)
        rights[t] = jnp.where(even, near, cross)
    return lefts, rights


def with_sides(cells, lefts, rights, field):
    cols = cells.shape[1]
    return jnp.concatenate(
        [cells[:, :8] + placed(lefts, field, True), cells[:, cols - 8 :] + placed(rights, field, False)], axis=1
    )


def with_ends(cells, step, steps, rad, near, far):
    rows = cells.shape[0]
    even = rad % 2 == 0
    below, above = jnp.where(even, far, near), jnp.where(even, near, far)
    at_low = (step == 0).astype(f32)
    at_top = (step == steps - 1).astype(f32)
    return jnp.concatenate(
        [cells[:REACH] + at_low * below, cells[REACH : rows - REACH], cells[rows - REACH :] + at_top * above], axis=0
    )


def tile_sum_kernel(
    ids_ref, part_ref, vol_ref, same_ref, cross_ref, near_ref, far_ref, rest_ref, hit_ref, seg_ref, spot_ref,
    out_ref, lines_ref,
):
    all_rows, cols, depth = vol_ref.shape
    tiles, points = out_ref.shape[0], out_ref.shape[1] // 3
    rows = 16
    steps = all_rows // rows

    def add(step, carry):
        here = pl.ds(pl.multiple_of(step * rows, rows), rows)
        lefts, rights = by_side(ids_ref[0], same_ref[here, :8], [cross_ref[here]])
        vol = vol_ref[here]
        for c, field in enumerate((0, 7)):
            cells = with_sides(part_ref[field, here], lefts, rights, field)
            cells = with_ends(cells, step, steps, ids_ref[1], near_ref[field], far_ref[c])
            lines = exact_dot((cells * vol).reshape(rows * cols, depth), seg_ref[...])
            lines_ref[c, here] = jnp.sum(lines.reshape(rows, cols, -1) * spot_ref[...][None], axis=1)
        return carry

    lax.fori_loop(0, steps, add, 0)
    for c in range(2):
        sums = sum(dot(hit_ref[...], part) for part in parts_of(lines_ref[c], 3))
        out_ref[:, c * points : (c + 1) * points] = sums
    mine = lax.broadcasted_iota(jnp.int32, (tiles, points), 0) == ids_ref[2]
    out_ref[:, 2 * points :] = jnp.where(mine, rest_ref[8:9], 0.0)


def tile_sums(ids, part, vol, same, cross, near, far, rest, hits, seg, spot):
    _, rows, _, _ = part.shape
    points = seg.shape[1]
    tiles = hits.shape[0]
    return pl.pallas_call(
        tile_sum_kernel,
        in_specs=[SMEM] + [VMEM] * 10,
        out_specs=VMEM,
        out_shape=in_vmem(tiles, 3 * points),
        scratch_shapes=[pltpu.VMEM((2, rows, points), f32)],
        compiler_params=LARGE,
        cost_estimate=cost(1e3, 1e3),
        name="tile_sums",
    )(ids, *[pinned(x) for x in (part, vol, same, cross, near, far, rest)], hits, seg, spot)


def drifted(density, courant):
    for _ in range(DRIFT):
        density = density - courant * (density - pltpu.roll(density, 1, 1))
    return density


def columns_of(packed_ref, channels):
    turned = jnp.transpose(packed_ref[...])
    return [turned[:channels, i : i + 1] for i in range(4)]


def rest_kernel(density_ref, packed_ref, out_ref, spread_ref):
    _, channels, points = density_ref.shape
    courant, weight, first, second = columns_of(packed_ref, channels)
    rows = []
    for given in (first, second):
        for k, choices in enumerate((1.0, 3.0, 3.0, 1.0)):
            gain = (inner_step * choices) * weight * given
            for _ in range(k):
                gain = gain * courant
            for _ in range(DRIFT - k):
                gain = gain * (1.0 - courant)
            rows.append(jnp.broadcast_to(jnp.sum(gain, axis=0, keepdims=True), (1, points)))
    rest = jnp.sum(weight * drifted(density_ref[0], courant), axis=0, keepdims=True)
    out_ref[...] = jnp.concatenate(rows + [rest] * 8, axis=0)
    for i, column in enumerate((courant, first, second)):
        spread_ref[i] = jnp.broadcast_to(column, (channels, points))


def rest_of(density, packed):
    _, channels, points = density.shape
    return pl.pallas_call(
        rest_kernel,
        out_shape=[in_vmem(16, points), in_vmem(3, channels, points)],
        compiler_params=SMALL,
        cost_estimate=cost(1e3, 1e3),
        name="rest_pressure",
    )(density, packed)


def pressures_of(sums, rest_ref):
    points = sums.shape[1] // 3
    pressure = sums[:, 2 * points :]
    for c in range(2):
        source = sums[:, c * points : (c + 1) * points]
        for k in range(DRIFT + 1):
            shifted = pltpu.roll(source, k, 1) if k else source
            pressure = pressure + rest_ref[(DRIFT + 1) * c + k : (DRIFT + 1) * c + k + 1] * shifted
    return pressure


def finish_field(field, refs, part_ref, done, step_of=None):
    ids_ref, near_ref, far_a, far_b, same_ref, *cross_refs = refs
    rows = CHUNK
    steps = done.shape[1] // rows
    last_field = near_ref.shape[0] - 1

    def step(i, carry):
        here = pl.ds(pl.multiple_of(i * rows, rows), rows)
        lefts, rights = {}, {}
        first = REACH * PACKED.index(field)
        for t in range(first // 8, (first + REACH - 1) // 8 + 1):
            cross = cross_refs[0][here] if t == 0 else cross_refs[1][here, 8 * t - 8 : 8 * t]
            one = by_side(ids_ref[0], same_ref[here, 8 * t : 8 * t + 8], [cross])
            lefts[t], rights[t] = one[0][0], one[1][0]
        far = far_a[field // last_field] if field in (0, last_field) else far_b[field - 1]
        cells = with_sides(part_ref[field, here], lefts, rights, field)
        cells = with_ends(cells, i, steps, ids_ref[1], near_ref[field], far)
        done[min(field, done.shape[0] - 1), here] = cells if step_of is None else step_of(here, cells)
        return carry

    lax.fori_loop(0, steps, step, 0)


def most_kernel(ids_ref, part_ref, *refs):
    *sides, out_hbm, done, sem = refs
    copies = []
    for field in range(done.shape[0]):
        finish_field(field, (ids_ref, *sides), part_ref, done)
        copies.append(pltpu.make_async_copy(done.at[field], out_hbm.at[field], sem.at[field]))
        copies[-1].start()
    for copy in copies:
        copy.wait()


def last_kernel(ids_ref, part_ref, *refs):
    *sides, _, hit_ref, sums_ref, rest_ref, spot_ref, seg_ref, density_ref, spread_ref = refs[:-6]
    out_hbm, drifted_hbm, done, back_ref, moved, sem = refs[-6:]
    points = spot_ref.shape[1]
    _, _, cols, depth = done.shape
    last = part_ref.shape[0] - 1

    source = sums_ref[pl.ds(ids_ref[2], 1), :]
    density = density_ref[0] + inner_step * (
        spread_ref[1] * source[:, :points] + spread_ref[2] * source[:, points : 2 * points]
    )
    moved[0] = drifted(density, spread_ref[0])
    copies = [pltpu.make_async_copy(moved, drifted_hbm, sem.at[0])]
    copies[0].start()
    back_ref[...] = sum(dot(hit_ref[...], p) for p in parts_of(pressures_of(sums_ref[...], rest_ref), 3))

    def nudged(here, cells):
        spread = (back_ref[here][:, None, :] * spot_ref[...][None]).reshape(-1, points)
        returned = exact_dot(spread, seg_ref[...]).reshape(-1, cols, depth)
        return cells + nudge_rate * (returned - cells)

    finish_field(last, (ids_ref, *sides), part_ref, done, nudged)
    copies.append(pltpu.make_async_copy(done.at[0], out_hbm.at[last], sem.at[1]))
    copies[1].start()
    for copy in copies:
        copy.wait()


def pressures_of(sums, rest_ref):
    points = sums.shape[1] // 3
    pressure = sums[:, 2 * points :]
    for c in range(2):
        source = sums[:, c * points : (c + 1) * points]
        for k in range(DRIFT + 1):
            shifted = pltpu.roll(source, k, 1) if k else source
            pressure = pressure + rest_ref[(DRIFT + 1) * c + k : (DRIFT + 1) * c + k + 1] * shifted
    return pressure


def finish_most(ids, part, rad, same, crosses):
    fields, rows, cols, depth = part.shape
    pins = [pinned(x) for x in (part, *rad, same, *crosses)]
    return pl.pallas_call(
        most_kernel,
        in_specs=[SMEM] + [VMEM] * len(pins),
        out_specs=HBM,
        out_shape=jax.ShapeDtypeStruct(part.shape, f32),
        scratch_shapes=[pltpu.VMEM((fields - 1, rows, cols, depth), f32), pltpu.SemaphoreType.DMA((fields - 1,))],
        compiler_params=LARGE,
        cost_estimate=cost(1e8, 1.6e7),
        name="finish_most",
    )(ids, *pins)


def finish_last(ids, part, rad, same, crosses, most, hits, sums, rest, spot, seg, density, spread):
    fields, rows, cols, depth = part.shape
    pins = [pinned(x) for x in (part, *rad, same, *crosses)]
    return pl.pallas_call(
        last_kernel,
        in_specs=[SMEM] + [VMEM] * len(pins) + [HBM] + [VMEM] * 7,
        out_specs=[HBM, HBM],
        out_shape=[jax.ShapeDtypeStruct(part.shape, f32), jax.ShapeDtypeStruct(density.shape, f32)],
        input_output_aliases={1 + len(pins): 0},
        scratch_shapes=[
            pltpu.VMEM((1, rows, cols, depth), f32),
            pltpu.VMEM((rows, spot.shape[1]), f32),
            pltpu.VMEM(density.shape, f32),
            pltpu.SemaphoreType.DMA((2,)),
        ],
        compiler_params=LARGE,
        cost_estimate=cost(1e3, 1e3),
        name="finish_last",
    )(ids, *pins, most, hits, pinned(sums), pinned(rest), spot, seg, density, pinned(spread))


def swap(x, axis, bit):
    return lax.ppermute(x, axis, [(i, i ^ bit) for i in range(lax.axis_size(axis))])


def per_device(
    state,
    flux_matrices,
    wave_speed,
    flux_volume,
    block_tile,
    tile_of_device,
    phase_density,
    injection,
    drift_courant,
    energy_weight,
):
    fields, rows, cols, depth = state.shape
    n_rad, n_lon = lax.axis_size("rad"), lax.axis_size("lon")
    points = cols * ZSEG
    lon, rad, place = [lax.axis_index(axes).astype(jnp.int32).reshape(1) for axes in ("lon", "rad", ("rad", "lon"))]

    across = [(i, (i + 1 if i % 2 else i - 1) % n_lon) for i in range(n_lon)]
    beyond = [(i, j) for i in range(n_rad) for j in [i + 1 if i % 2 else i - 1] if 0 <= j < n_rad]
    rim, ids, same, *crosses = lon_edges(state, flux_matrices, wave_speed, lon, rad, place)
    cross_0 = lax.ppermute(crosses[0], "lon", across)
    same = swap(same, "lon", 1)
    cross_1 = lax.ppermute(crosses[1], "lon", across)

    near, far_a, far_b = rad_edges(ids, rim, flux_matrices, wave_speed)
    far_a = lax.ppermute(far_a, "rad", beyond)
    near = swap(near, "rad", 1)

    packed = jnp.concatenate([drift_courant[None], energy_weight[None], injection], axis=0)
    packed = jnp.pad(packed, ((0, 4), (0, -packed.shape[1] % 128)))
    rest, spread = rest_of(phase_density, packed)

    part = local_update(state, flux_matrices, wave_speed)

    targets = block_tile[0, :, 0]
    hits = (tile_of_device[:, None] == targets[None, :]).astype(bf16)
    hits_back = (targets[:, None] == tile_of_device[None, :]).astype(bf16)
    seg_cells = depth // ZSEG
    seg = np.array([[float(p % ZSEG == z // seg_cells) for p in range(points)] for z in range(depth)], np.float32)
    spot = np.array([[float(p // ZSEG == l) for p in range(points)] for l in range(cols)], np.float32)
    sums = tile_sums(
        ids, part, flux_volume, same, cross_0, near, far_a, rest, hits, jnp.asarray(seg, bf16), jnp.asarray(spot)
    )
    def summed(sums, axis, steps):
        return sum([swap(sums, axis, step) for step in steps], sums)

    far_b, sums = lax.optimization_barrier((far_b, sums))
    far_b = lax.ppermute(far_b, "rad", beyond)
    sums = summed(sums, "rad", range(1, n_rad))
    sums = summed(sums, "lon", [1])
    others = [swap(sums, "lon", step) for step in range(2, n_lon, 2)]
    rad_sums = (near, far_a, far_b)
    most = finish_most(ids, part, rad_sums, same, (cross_0, cross_1))
    sums, most = lax.optimization_barrier((sums, most))
    sums = sum(others, sums)
    done, density = finish_last(
        ids, part, rad_sums, same, (cross_0, cross_1), most, hits_back, sums, rest, jnp.asarray(spot),
        jnp.asarray(seg.T, bf16), phase_density, spread,
    )
    return done, density


def solution(mesh):
    in_specs = (
        P(None, "rad", "lon", None),
        P(),
        P(),
        P("rad", "lon", None),
        P("lon", "rad", None),
        P(),
        P(("rad", "lon"), None, None),
        P(),
        P(),
        P(),
    )
    out_specs = (P(None, "rad", "lon", None), P(("rad", "lon"), None, None))
    return jax.shard_map(per_device, mesh=mesh, in_specs=in_specs, out_specs=out_specs, check_vma=False)
```

```python
import functools

import jax
import jax.numpy as jnp
import numpy as np
from jax import lax
from jax.experimental import pallas as pl
from jax.experimental.pallas import tpu as pltpu
from jax.sharding import PartitionSpec as P

ZSEG = 8
DRIFT = 3
REACH = 3

courant_step = 0.4
nudge_rate = 0.5
inner_step = 0.5

SUM_TAPS = {k: v / 60.0 for k, v in zip(range(-3, 4), (-2.0, 18.0, -90.0, 0.0, 90.0, -18.0, 2.0))}
GAP_TAPS = {k: v / 60.0 for k, v in zip(range(-3, 4), (2.0, -12.0, 30.0, -40.0, 30.0, -12.0, 2.0))}

PACKED = (0, 7, 1, 2, 3, 4, 5, 6)

f32 = jnp.float32
bf16 = jnp.bfloat16


def cost(flops, bytes_accessed):
    return pl.CostEstimate(flops=int(flops), bytes_accessed=int(bytes_accessed), transcendentals=0)


def parts_of(x, count):
    parts = []
    for _ in range(count):
        part = x.astype(bf16)
        parts.append(part)
        x = x - part.astype(f32)
    return parts


def dot(a, b):
    return jnp.dot(a, b, preferred_element_type=f32)


def exact_dot(x, ones):
    return sum(dot(part, ones) for part in parts_of(x, 3))


def lon_tables(rows, cols):
    fields = 1 + max(f for f, _ in cols)
    pick_row = np.array([[float(f == a) for a in range(fields)] for f, _ in rows], np.float32)
    pick_col = np.array([[float(f == b) for f, _ in cols] for b in range(fields)], np.float32)
    summed = np.array([[0.0 if s is None else SUM_TAPS.get(s - t, 0.0) for _, s in cols] for _, t in rows], np.float32)
    gapped = np.array(
        [[0.0 if s is None or f != g else GAP_TAPS.get(s - t, 0.0) for g, s in cols] for f, t in rows], np.float32
    )
    return pick_row, pick_col, summed, gapped


def lon_weights(matrix, wave_rate, pick_row, pick_col, summed, gapped):
    half = 0.5 * courant_step
    spread = f32_dot(f32_dot(pick_row, matrix), pick_col)
    return (half * wave_rate) * gapped - half * spread * summed


def f32_dot(a, b):
    return jnp.dot(a, b, precision=lax.Precision.HIGHEST, preferred_element_type=f32)


def whole(array):
    zeros = (0,) * array.ndim
    return pl.BlockSpec(array.shape, lambda *_: zeros)


SMEM = pl.BlockSpec(memory_space=pltpu.SMEM)
VMEM = pl.BlockSpec(memory_space=pltpu.VMEM)
HBM = pl.BlockSpec(memory_space=pltpu.HBM)
LARGE = pltpu.CompilerParams(vmem_limit_bytes=12 * 2**20)
SMALL = pltpu.CompilerParams(vmem_limit_bytes=5 * 2**20)
CHUNK = 8
AHEAD = 3


def in_vmem(*shape):
    return pltpu.VMEM(shape, f32)


def pinned(x):
    return pltpu.with_memory_space_constraint(x, pltpu.VMEM)


def lon_edge_kernel(lon_ref, rad_ref, place_ref, state_hbm, speed_hbm, matrix_hbm, table_hbm, rim, ids_ref, same, *refs):
    *crosses, speed_ref, matrix_ref, table_ref, edges, weights, sem, few_sem = refs
    fields, rows, cols, depth = state_hbm.shape
    chunks = rows // CHUNK
    size = same.shape[1]
    keep = edges.shape[2] // 2

    def loads(c):
        here = pl.ds(c * CHUNK, CHUNK)
        return [
            pltpu.make_async_copy(
                state_hbm.at[:, here, pl.ds(first, keep)], edges.at[:, here, pl.ds(slot, keep)], sem.at[2 * c + i]
            )
            for i, (first, slot) in enumerate(((0, 0), (cols - keep, keep)))
        ]

    few = [(speed_hbm, speed_ref), (matrix_hbm, matrix_ref), (table_hbm, table_ref)]
    few += [(state_hbm.at[:, pl.ds(0, REACH)], rim.at[:, pl.ds(0, REACH)])]
    few += [(state_hbm.at[:, pl.ds(rows - REACH, REACH)], rim.at[:, pl.ds(REACH, REACH)])]
    few = [pltpu.make_async_copy(source, target, few_sem.at[i]) for i, (source, target) in enumerate(few)]
    for copy in few[:3]:
        copy.start()
    for c in range(chunks):
        for copy in loads(c):
            copy.start()
    for copy in few[3:]:
        copy.start()
    ids_ref[0] = lon_ref[0]
    ids_ref[1] = rad_ref[0]
    ids_ref[2] = place_ref[0]
    for copy in few[:3]:
        copy.wait()
    wide = 8 * fields
    w = lon_weights(
        matrix_ref[1], speed_ref[1], table_ref[0, :, :fields], table_ref[1, :fields, :wide], table_ref[2, :, :wide],
        table_ref[3, :, :wide],
    )
    swap = lon_ref[0] % 2 == 1
    w = jnp.concatenate([jnp.where(swap, w[size:], w[:size]), jnp.where(swap, w[:size], w[size:])], axis=0)
    high, low = parts_of(w, 2)
    weights[...] = jnp.concatenate([high, high, low], axis=1)

    def step(c, carry):
        for copy in loads(c):
            copy.wait()
        for j in range(CHUNK):
            r = c * CHUNK + j
            high, low = parts_of(edges[:, r].reshape(-1, depth), 2)
            sums = dot(weights[...], jnp.concatenate([high, low, high], axis=0))
            same[r] = sums[:size]
            first, rest = crosses
            first[r] = sums[size : size + 8]
            rest[r] = sums[size + 8 :]
        return carry

    lax.fori_loop(0, chunks, step, 0)
    for copy in few[3:]:
        copy.wait()


def lon_edges(state, matrices, speed, lon, rad, place):
    fields, rows, cols, depth = state.shape
    keep = 4
    sources = [(f, l if l < keep else cols - 2 * keep + l) for f in range(fields) for l in range(2 * keep)]
    sources = [(f, l if l < REACH or l >= cols - REACH else None) for f, l in sources]
    to_right = [(f, cols + t) for f in PACKED for t in range(REACH)]
    to_left = [(f, t - REACH) for f in PACKED for t in range(REACH)]
    size = fields * REACH
    tables = np.zeros((4, 2 * size, 128), np.float32)
    for i, table in enumerate(lon_tables(to_right + to_left, sources)):
        tables[i, : table.shape[0], : table.shape[1]] = table
    return pl.pallas_call(
        lon_edge_kernel,
        in_specs=[SMEM] * 3 + [HBM] * 4,
        out_specs=[VMEM, SMEM] + [VMEM] * 3,
        out_shape=[
            in_vmem(fields, 2 * REACH, cols, depth),
            jax.ShapeDtypeStruct((3,), jnp.int32),
            in_vmem(rows, size, depth),
            in_vmem(rows, 8, depth),
            in_vmem(rows, size - 8, depth),
        ],
        scratch_shapes=[
            pltpu.SMEM(speed.shape, f32),
            pltpu.VMEM(matrices.shape, f32),
            pltpu.VMEM(tables.shape, f32),
            pltpu.VMEM((fields, rows, 2 * keep, depth), f32),
            pltpu.VMEM((2 * size, 3 * len(sources)), bf16),
            pltpu.SemaphoreType.DMA((2 * rows // CHUNK,)),
            pltpu.SemaphoreType.DMA((5,)),
        ],
        compiler_params=LARGE,
        cost_estimate=cost(1e3, 1e3),
        name="lon_edges",
    )(lon, rad, place, *[pltpu.with_memory_space_constraint(x, pltpu.HBM) for x in (state, speed, matrices, jnp.asarray(tables))])


def turn_weights(matrix, pick, same):
    return (-0.5 * courant_step) * same * f32_dot(f32_dot(pick, matrix), pick.T)


def turn_tables(fields, cols):
    every = [(f, l) for f in range(fields) for l in range(cols)]
    pick = np.array([[float(f == a) for a in range(fields)] for f, _ in every], np.float32)
    same = np.array([[float(l == m) for _, m in every] for _, l in every], np.float32)
    return pick, same


def rad_edge_kernel(ids_ref, speed_ref, rim_ref, matrix_ref, pick_ref, same_ref, near_a, near_b, far_ref):
    fields, _, cols, depth = rim_ref.shape
    rate = (0.5 * courant_step) * speed_ref[0]
    even = ids_ref[1] % 2 == 0
    high, low = parts_of(turn_weights(matrix_ref[0], pick_ref[...], same_ref[...]), 2)
    w = jnp.concatenate([high, high, low], axis=1)

    def turned(cells):
        high, low = parts_of(cells.reshape(-1, depth), 2)
        return dot(w, jnp.concatenate([high, low, high], axis=0)).reshape(fields, cols, depth)

    first = [rim_ref[:, j] for j in range(REACH)]
    last = [rim_ref[:, REACH + j] for j in range(REACH)]
    first_turned = [turned(cells) for cells in first]
    last_turned = [turned(cells) for cells in last]
    for t in range(REACH):
        up = sum(
            SUM_TAPS[j - REACH - t] * last_turned[j] + (rate * GAP_TAPS[j - REACH - t]) * last[j]
            for j in range(t, REACH)
        )
        down = sum(
            SUM_TAPS[j + REACH - t] * first_turned[j] + (rate * GAP_TAPS[j + REACH - t]) * first[j]
            for j in range(t + 1)
        )
        near = jnp.where(even, up, down)
        near_a[0, t] = near[0]
        near_a[1, t] = near[fields - 1]
        near_b[:, t] = near[1 : fields - 1]
        far_ref[:, t] = jnp.where(even, down, up)


def rad_edges(ids, rim, matrices, speed):
    fields, _, cols, depth = rim.shape
    tables = turn_tables(fields, cols)
    return pl.pallas_call(
        rad_edge_kernel,
        in_specs=[SMEM] * 2 + [VMEM] * (2 + len(tables)),
        out_specs=[VMEM] * 3,
        out_shape=[in_vmem(n, REACH, cols, depth) for n in (2, fields - 2, fields)],
        compiler_params=LARGE,
        cost_estimate=cost(1e3, 1e3),
        name="rad_edges",
    )(ids, speed, pinned(rim), matrices, *tables)


def add_radial(speed_ref, cells, turned, total, fields, first):
    cols, depth = total.shape[2:]
    rate = (0.5 * courant_step) * speed_ref[0]
    for f in fields:
        for half in range(cols // 8):
            for lane in range(depth // 128):
                lanes = pl.ds(128 * lane, 128)
                u = [cells[f, first + j, pl.ds(8 * half, 8), lanes] for j in range(CHUNK + 2 * REACH)]
                v = [turned[first + j, pl.ds(f * cols + 8 * half, 8), lanes] for j in range(CHUNK + 2 * REACH)]
                for j in range(CHUNK):
                    at = j + REACH
                    value = total[f, first + j, pl.ds(8 * half, 8), lanes] + (rate * GAP_TAPS[0]) * u[at]
                    for k in range(1, REACH + 1):
                        value = value + SUM_TAPS[k] * (v[at + k] - v[at - k])
                        value = value + (rate * GAP_TAPS[k]) * (u[at + k] + u[at - k])
                    total[f, first + j, pl.ds(8 * half, 8), lanes] = value


def add_radial(speed_ref, cells, turned, total, fields, first):
    cols, depth = total.shape[2:]
    rate = (0.5 * courant_step) * speed_ref[0]
    for f in fields:
        for half in range(cols // 8):
            for lane in range(depth // 128):
                lanes, subs = pl.ds(128 * lane, 128), pl.ds(8 * half, 8)
                u = [cells[f, first + j, subs, lanes] for j in range(CHUNK + 2 * REACH)]
                v = [turned[first + j, pl.ds(f * cols + 8 * half, 8), lanes] for j in range(CHUNK + 2 * REACH)]
                for j in range(CHUNK):
                    at = j + REACH
                    value = total[f, first + j, subs, lanes] + (rate * GAP_TAPS[0]) * u[at]
                    for k in range(1, REACH + 1):
                        value = value + (SUM_TAPS[k] / SUM_TAPS[1]) * (v[at + k] - v[at - k])
                        value = value + (rate * GAP_TAPS[k]) * (u[at + k] + u[at - k])
                    total[f, first + j, subs, lanes] = value


def local_kernel(
    speed_ref, state_hbm, matrix_ref, pick_ref, same_ref, sum_ref, gap_ref, total, turned, cells, w_ref, sem
):
    fields, rows, cols, depth = total.shape
    chunks = rows // CHUNK
    size = fields * cols

    def load(c):
        return pltpu.make_async_copy(
            state_hbm.at[:, pl.ds(c * CHUNK, CHUNK)], cells.at[:, pl.ds(REACH + c * CHUNK, CHUNK)], sem.at[c]
        )

    for c in range(AHEAD):
        load(c).start()
    pick = pick_ref[...]
    own = lon_weights(matrix_ref[1], speed_ref[1], pick, pick.T, sum_ref[...], gap_ref[...])
    turn = SUM_TAPS[1] * turn_weights(matrix_ref[0], pick, same_ref[...])
    high, low = parts_of(jnp.concatenate([own, turn], axis=0), 2)
    w_ref[...] = jnp.concatenate([high, high, low], axis=1)
    for edge in (0, REACH + rows):
        cells[:, edge : edge + REACH] = jnp.zeros((fields, REACH, cols, depth), f32)
        turned[edge : edge + REACH] = jnp.zeros((REACH, size, depth), f32)

    def rows_of(c, carry):
        load(c).wait()

        @pl.when(c + AHEAD < chunks)
        def _():
            load(c + AHEAD).start()

        for j in range(CHUNK):
            r = c * CHUNK + j
            here = cells[:, REACH + r].reshape(size, depth)
            high, low = parts_of(here, 2)
            both = dot(w_ref[...], jnp.concatenate([high, low, high], axis=0))
            total[:, r] = (here + both[:size]).reshape(fields, cols, depth)
            turned[REACH + r] = both[size:]
        return carry

    def radial(c, carry):
        add_radial(speed_ref, cells, turned, total, (0, fields - 1), c * CHUNK)
        return carry

    lax.fori_loop(0, chunks, rows_of, 0)
    lax.fori_loop(0, chunks, radial, 0)


def local_update(state, matrices, speed):
    fields, rows, cols, depth = state.shape
    size = fields * cols
    every = [(f, l) for f in range(fields) for l in range(cols)]
    _, _, summed, gapped = lon_tables(every, every)
    padded = rows + 2 * REACH
    return pl.pallas_call(
        local_kernel,
        in_specs=[SMEM, HBM] + [VMEM] * 5,
        out_specs=[VMEM] * 3,
        out_shape=[in_vmem(*state.shape), in_vmem(padded, size, depth), in_vmem(fields, padded, cols, depth)],
        scratch_shapes=[pltpu.VMEM((2 * size, 3 * size), bf16), pltpu.SemaphoreType.DMA((rows // CHUNK,))],
        compiler_params=SMALL,
        cost_estimate=cost(1e3, 1e3),
        name="local_update",
    )(
        speed, pltpu.with_memory_space_constraint(state, pltpu.HBM), matrices, *turn_tables(fields, cols), summed, gapped
    )


def radial_kernel(fields, speed_ref, cells, turned, _, total):
    def radial(c, carry):
        add_radial(speed_ref, cells, turned, total, fields, c * CHUNK)
        return carry

    lax.fori_loop(0, total.shape[1] // CHUNK, radial, 0)


def radial_update(fields, cells, turned, part, speed):
    return pl.pallas_call(
        functools.partial(radial_kernel, fields),
        in_specs=[SMEM] + [VMEM] * 3,
        out_specs=VMEM,
        out_shape=in_vmem(*part.shape),
        input_output_aliases={3: 0},
        compiler_params=SMALL,
        cost_estimate=cost(1e8, 6e6),
        name="radial_update",
    )(speed, pinned(cells), pinned(turned), pinned(part))


def placed(tiles, field, from_left):
    start = REACH * PACKED.index(field)
    tile, offset = start // 8, start % 8
    cells = tiles[tile]
    sub = lax.broadcasted_iota(jnp.int32, cells.shape, 1)
    if offset + REACH > 8:
        cells = jnp.where(sub >= offset, cells, tiles[tile + 1])
    goal = 0 if from_left else 8 - REACH
    shift = (goal - offset) % 8
    if shift:
        cells = pltpu.roll(cells, shift, 1)
    keep = sub < REACH if from_left else sub >= 8 - REACH
    return jnp.where(keep, cells, 0.0)


def by_side(lon, same, crosses):
    even = lon % 2 == 0
    lefts, rights = {}, {}
    for t, cross in enumerate(crosses):
        near = same[:, 8 * t : 8 * t + 8]
        lefts[t] = jnp.where(even, cross, near)
        rights[t] = jnp.where(even, near, cross)
    return lefts, rights


def with_sides(cells, lefts, rights, field):
    cols = cells.shape[1]
    return jnp.concatenate(
        [cells[:, :8] + placed(lefts, field, True), cells[:, cols - 8 :] + placed(rights, field, False)], axis=1
    )


def with_ends(cells, step, steps, rad, near, far):
    rows = cells.shape[0]
    even = rad % 2 == 0
    below, above = jnp.where(even, far, near), jnp.where(even, near, far)
    at_low = (step == 0).astype(f32)
    at_top = (step == steps - 1).astype(f32)
    return jnp.concatenate(
        [cells[:REACH] + at_low * below, cells[REACH : rows - REACH], cells[rows - REACH :] + at_top * above], axis=0
    )


def tile_sum_kernel(
    ids_ref, part_ref, vol_ref, same_ref, cross_ref, near_ref, far_ref, rest_ref, hit_ref, seg_ref, spot_ref,
    out_ref, lines_ref,
):
    all_rows, cols, depth = vol_ref.shape
    tiles, points = out_ref.shape[0], out_ref.shape[1] // 3
    rows = 16
    steps = all_rows // rows

    def add(step, carry):
        here = pl.ds(pl.multiple_of(step * rows, rows), rows)
        lefts, rights = by_side(ids_ref[0], same_ref[here, :8], [cross_ref[here]])
        vol = vol_ref[here]
        for c, field in enumerate((0, 7)):
            cells = with_sides(part_ref[field, here], lefts, rights, field)
            cells = with_ends(cells, step, steps, ids_ref[1], near_ref[c], far_ref[field])
            lines = exact_dot((cells * vol).reshape(rows * cols, depth), seg_ref[...])
            lines_ref[c, here] = jnp.sum(lines.reshape(rows, cols, -1) * spot_ref[...][None], axis=1)
        return carry

    lax.fori_loop(0, steps, add, 0)
    for c in range(2):
        sums = sum(dot(hit_ref[...], part) for part in parts_of(lines_ref[c], 3))
        out_ref[:, c * points : (c + 1) * points] = sums
    mine = lax.broadcasted_iota(jnp.int32, (tiles, points), 0) == ids_ref[2]
    out_ref[:, 2 * points :] = jnp.where(mine, rest_ref[8:9], 0.0)


def tile_sums(ids, part, vol, same, cross, near, far, rest, hits, seg, spot):
    _, rows, _, _ = part.shape
    points = seg.shape[1]
    tiles = hits.shape[0]
    return pl.pallas_call(
        tile_sum_kernel,
        in_specs=[SMEM] + [VMEM] * 10,
        out_specs=VMEM,
        out_shape=in_vmem(tiles, 3 * points),
        scratch_shapes=[pltpu.VMEM((2, rows, points), f32)],
        compiler_params=LARGE,
        cost_estimate=cost(1e3, 1e3),
        name="tile_sums",
    )(ids, *[pinned(x) for x in (part, vol, same, cross, near, far, rest)], hits, seg, spot)


def drifted(density, courant):
    for _ in range(DRIFT):
        density = density - courant * (density - pltpu.roll(density, 1, 1))
    return density


def columns_of(packed_ref, channels):
    turned = jnp.transpose(packed_ref[...])
    return [turned[:channels, i : i + 1] for i in range(4)]


def rest_kernel(density_ref, packed_ref, out_ref, spread_ref):
    _, channels, points = density_ref.shape
    courant, weight, first, second = columns_of(packed_ref, channels)
    rows = []
    for given in (first, second):
        for k, choices in enumerate((1.0, 3.0, 3.0, 1.0)):
            gain = (inner_step * choices) * weight * given
            for _ in range(k):
                gain = gain * courant
            for _ in range(DRIFT - k):
                gain = gain * (1.0 - courant)
            rows.append(jnp.broadcast_to(jnp.sum(gain, axis=0, keepdims=True), (1, points)))
    rest = jnp.sum(weight * drifted(density_ref[0], courant), axis=0, keepdims=True)
    out_ref[...] = jnp.concatenate(rows + [rest] * 8, axis=0)
    for i, column in enumerate((courant, first, second)):
        spread_ref[i] = jnp.broadcast_to(column, (channels, points))


def rest_of(density, packed):
    _, channels, points = density.shape
    return pl.pallas_call(
        rest_kernel,
        out_shape=[in_vmem(16, points), in_vmem(3, channels, points)],
        compiler_params=SMALL,
        cost_estimate=cost(1e3, 1e3),
        name="rest_pressure",
    )(density, packed)


def pressures_of(sums, rest_ref):
    points = sums.shape[1] // 3
    pressure = sums[:, 2 * points :]
    for c in range(2):
        source = sums[:, c * points : (c + 1) * points]
        for k in range(DRIFT + 1):
            shifted = pltpu.roll(source, k, 1) if k else source
            pressure = pressure + rest_ref[(DRIFT + 1) * c + k : (DRIFT + 1) * c + k + 1] * shifted
    return pressure


def finish_field(field, refs, part_ref, out):
    ids_ref, near_a, near_b, far_ref, same_ref, *cross_refs = refs
    rows = 2 * CHUNK
    steps = out.shape[0] // rows
    last_field = far_ref.shape[0] - 1

    def step(i, carry):
        here = pl.ds(pl.multiple_of(i * rows, rows), rows)
        lefts, rights = {}, {}
        first = REACH * PACKED.index(field)
        for t in range(first // 8, (first + REACH - 1) // 8 + 1):
            cross = cross_refs[0][here] if t == 0 else cross_refs[1][here, 8 * t - 8 : 8 * t]
            one = by_side(ids_ref[0], same_ref[here, 8 * t : 8 * t + 8], [cross])
            lefts[t], rights[t] = one[0][0], one[1][0]
        near = near_a[field // last_field] if field in (0, last_field) else near_b[field - 1]
        cells = with_sides(part_ref[field, here], lefts, rights, field)
        out[here] = with_ends(cells, i, steps, ids_ref[1], near, far_ref[field])
        return carry

    lax.fori_loop(0, steps, step, 0)


def most_kernel(ids_ref, part_ref, *refs):
    *sides, out_hbm, last_ref, done, sem = refs
    copies = []
    for field in range(done.shape[0]):
        finish_field(field, (ids_ref, *sides), part_ref, done.at[field])
        copies.append(pltpu.make_async_copy(done.at[field], out_hbm.at[field], sem.at[field]))
        copies[-1].start()
    finish_field(done.shape[0], (ids_ref, *sides), part_ref, last_ref)
    for copy in copies:
        copy.wait()


def last_kernel(
    ids_ref, cells_ref, _, hit_ref, sums_ref, rest_ref, spot_ref, seg_ref, density_ref, spread_ref,
    out_hbm, drifted_hbm, done, back_ref, moved, sem,
):
    points = spot_ref.shape[1]
    rows, cols, depth = done.shape
    last = out_hbm.shape[0] - 1
    back_ref[...] = sum(dot(hit_ref[...], p) for p in parts_of(pressures_of(sums_ref[...], rest_ref), 3))
    copies = []
    size = 2 * CHUNK
    for first in range(0, rows, size):
        here = pl.ds(first, size)
        spread = (back_ref[here][:, None, :] * spot_ref[...][None]).reshape(-1, points)
        returned = exact_dot(spread, seg_ref[...]).reshape(-1, cols, depth)
        cells = cells_ref[here]
        done[here] = cells + nudge_rate * (returned - cells)
        copies.append(pltpu.make_async_copy(done.at[here], out_hbm.at[last, here], sem.at[len(copies)]))
        copies[-1].start()
    source = sums_ref[pl.ds(ids_ref[2], 1), :]
    density = density_ref[0] + inner_step * (
        spread_ref[1] * source[:, :points] + spread_ref[2] * source[:, points : 2 * points]
    )
    moved[0] = drifted(density, spread_ref[0])
    copies.append(pltpu.make_async_copy(moved, drifted_hbm, sem.at[len(copies)]))
    copies[-1].start()
    for copy in copies:
        copy.wait()


def pressures_of(sums, rest_ref):
    points = sums.shape[1] // 3
    pressure = sums[:, 2 * points :]
    for c in range(2):
        source = sums[:, c * points : (c + 1) * points]
        for k in range(DRIFT + 1):
            shifted = pltpu.roll(source, k, 1) if k else source
            pressure = pressure + rest_ref[(DRIFT + 1) * c + k : (DRIFT + 1) * c + k + 1] * shifted
    return pressure


def finish_most(ids, part, rad, same, crosses):
    fields, rows, cols, depth = part.shape
    pins = [pinned(x) for x in (part, *rad, same, *crosses)]
    return pl.pallas_call(
        most_kernel,
        in_specs=[SMEM] + [VMEM] * len(pins),
        out_specs=[HBM, VMEM],
        out_shape=[jax.ShapeDtypeStruct(part.shape, f32), in_vmem(rows, cols, depth)],
        scratch_shapes=[pltpu.VMEM((fields - 1, rows, cols, depth), f32), pltpu.SemaphoreType.DMA((fields - 1,))],
        compiler_params=LARGE,
        cost_estimate=cost(1e8, 1.6e7),
        name="finish_most",
    )(ids, *pins)


def finish_last(ids, cells, most, hits, sums, rest, spot, seg, density, spread):
    rows, cols, depth = cells.shape
    return pl.pallas_call(
        last_kernel,
        in_specs=[SMEM, VMEM, HBM] + [VMEM] * 7,
        out_specs=[HBM, HBM],
        out_shape=[jax.ShapeDtypeStruct(most.shape, f32), jax.ShapeDtypeStruct(density.shape, f32)],
        input_output_aliases={2: 0},
        scratch_shapes=[
            pltpu.VMEM(cells.shape, f32),
            pltpu.VMEM((rows, spot.shape[1]), f32),
            pltpu.VMEM(density.shape, f32),
            pltpu.SemaphoreType.DMA((rows // (2 * CHUNK) + 1,)),
        ],
        compiler_params=SMALL,
        cost_estimate=cost(1e3, 1e3),
        name="finish_last",
    )(ids, pinned(cells), most, hits, pinned(sums), pinned(rest), spot, seg, density, pinned(spread))


def swap(x, axis, bit):
    return lax.ppermute(x, axis, [(i, i ^ bit) for i in range(lax.axis_size(axis))])


def per_device(
    state,
    flux_matrices,
    wave_speed,
    flux_volume,
    block_tile,
    tile_of_device,
    phase_density,
    injection,
    drift_courant,
    energy_weight,
):
    fields, rows, cols, depth = state.shape
    n_rad, n_lon = lax.axis_size("rad"), lax.axis_size("lon")
    points = cols * ZSEG
    lon, rad, place = [lax.axis_index(axes).astype(jnp.int32).reshape(1) for axes in ("lon", "rad", ("rad", "lon"))]

    across = [(i, (i + 1 if i % 2 else i - 1) % n_lon) for i in range(n_lon)]
    beyond = [(i, j) for i in range(n_rad) for j in [i + 1 if i % 2 else i - 1] if 0 <= j < n_rad]
    rim, ids, same, *crosses = lon_edges(state, flux_matrices, wave_speed, lon, rad, place)
    cross_0 = lax.ppermute(crosses[0], "lon", across)
    same = swap(same, "lon", 1)
    cross_1 = lax.ppermute(crosses[1], "lon", across)

    near_a, near_b, far = rad_edges(ids, rim, flux_matrices, wave_speed)
    near_a = swap(near_a, "rad", 1)
    far = lax.ppermute(far, "rad", beyond)

    packed = jnp.concatenate([drift_courant[None], energy_weight[None], injection], axis=0)
    packed = jnp.pad(packed, ((0, 4), (0, -packed.shape[1] % 128)))
    rest, spread = rest_of(phase_density, packed)

    part, turned, cells = local_update(state, flux_matrices, wave_speed)

    targets = block_tile[0, :, 0]
    hits = (tile_of_device[:, None] == targets[None, :]).astype(bf16)
    hits_back = (targets[:, None] == tile_of_device[None, :]).astype(bf16)
    seg_cells = depth // ZSEG
    seg = np.array([[float(p % ZSEG == z // seg_cells) for p in range(points)] for z in range(depth)], np.float32)
    spot = np.array([[float(p // ZSEG == l) for p in range(points)] for l in range(cols)], np.float32)
    sums = tile_sums(
        ids, part, flux_volume, same, cross_0, near_a, far, rest, hits, jnp.asarray(seg, bf16), jnp.asarray(spot)
    )
    near_b, sums = lax.optimization_barrier((near_b, sums))
    near_b = swap(near_b, "rad", 1)
    part, sums = lax.optimization_barrier((part, sums))
    others = [swap(sums, "rad", step) for step in range(1, n_rad)]
    part = radial_update(tuple(range(1, fields - 1)), cells, turned, part, wave_speed)
    part, sums = lax.optimization_barrier((part, sums))
    sums = sum(others, sums)
    sums = sums + swap(sums, "lon", 1)
    others = [swap(sums, "lon", step) for step in range(2, n_lon, 2)]
    most, last = finish_most(ids, part, (near_a, near_b, far), same, (cross_0, cross_1))
    sums, most = lax.optimization_barrier((sums, most))
    sums = sum(others, sums)
    done, density = finish_last(
        ids, last, most, hits_back, sums, rest, jnp.asarray(spot), jnp.asarray(seg.T, bf16), phase_density, spread
    )
    return done, density


def solution(mesh):
    in_specs = (
        P(None, "rad", "lon", None),
        P(),
        P(),
        P("rad", "lon", None),
        P("lon", "rad", None),
        P(),
        P(("rad", "lon"), None, None),
        P(),
        P(),
        P(),
    )
    out_specs = (P(None, "rad", "lon", None), P(("rad", "lon"), None, None))
    return jax.shard_map(per_device, mesh=mesh, in_specs=in_specs, out_specs=out_specs, check_vma=False)
```

```python
import functools

import jax
import jax.numpy as jnp
import numpy as np
from jax import lax
from jax.experimental import pallas as pl
from jax.experimental.pallas import tpu as pltpu
from jax.sharding import PartitionSpec as P

ZSEG = 8
DRIFT = 3
REACH = 3

courant_step = 0.4
nudge_rate = 0.5
inner_step = 0.5

SUM_TAPS = {k: v / 60.0 for k, v in zip(range(-3, 4), (-2.0, 18.0, -90.0, 0.0, 90.0, -18.0, 2.0))}
GAP_TAPS = {k: v / 60.0 for k, v in zip(range(-3, 4), (2.0, -12.0, 30.0, -40.0, 30.0, -12.0, 2.0))}

PACKED = (0, 7, 1, 2, 3, 4, 5, 6)

f32 = jnp.float32
bf16 = jnp.bfloat16


def cost(flops, bytes_accessed):
    return pl.CostEstimate(flops=int(flops), bytes_accessed=int(bytes_accessed), transcendentals=0)


def parts_of(x, count):
    parts = []
    for _ in range(count):
        part = x.astype(bf16)
        parts.append(part)
        x = x - part.astype(f32)
    return parts


def dot(a, b):
    return jnp.dot(a, b, preferred_element_type=f32)


def exact_dot(x, ones):
    return sum(dot(part, ones) for part in parts_of(x, 3))


def lon_tables(rows, cols):
    fields = 1 + max(f for f, _ in cols)
    pick_row = np.array([[float(f == a) for a in range(fields)] for f, _ in rows], np.float32)
    pick_col = np.array([[float(f == b) for f, _ in cols] for b in range(fields)], np.float32)
    summed = np.array([[0.0 if s is None else SUM_TAPS.get(s - t, 0.0) for _, s in cols] for _, t in rows], np.float32)
    gapped = np.array(
        [[0.0 if s is None or f != g else GAP_TAPS.get(s - t, 0.0) for g, s in cols] for f, t in rows], np.float32
    )
    return pick_row, pick_col, summed, gapped


def lon_weights(matrix, wave_rate, pick_row, pick_col, summed, gapped):
    half = 0.5 * courant_step
    spread = f32_dot(f32_dot(pick_row, matrix), pick_col)
    return (half * wave_rate) * gapped - half * spread * summed


def f32_dot(a, b):
    return jnp.dot(a, b, precision=lax.Precision.HIGHEST, preferred_element_type=f32)


def whole(array):
    zeros = (0,) * array.ndim
    return pl.BlockSpec(array.shape, lambda *_: zeros)


SMEM = pl.BlockSpec(memory_space=pltpu.SMEM)
VMEM = pl.BlockSpec(memory_space=pltpu.VMEM)
HBM = pl.BlockSpec(memory_space=pltpu.HBM)
LARGE = pltpu.CompilerParams(vmem_limit_bytes=12 * 2**20)
SMALL = pltpu.CompilerParams(vmem_limit_bytes=5 * 2**20)
CHUNK = 8
BLOCK = 16
AHEAD = 3


def in_vmem(*shape):
    return pltpu.VMEM(shape, f32)


def pinned(x):
    return pltpu.with_memory_space_constraint(x, pltpu.VMEM)


def lon_edge_kernel(lon_ref, rad_ref, place_ref, state_hbm, speed_hbm, matrix_hbm, table_hbm, rim, ids_ref, same, *refs):
    *crosses, speed_ref, matrix_ref, table_ref, edges, weights, sem, few_sem = refs
    fields, rows, cols, depth = state_hbm.shape
    chunks = rows // BLOCK
    size = same.shape[1]
    keep = edges.shape[2] // 2

    def loads(c):
        here = pl.ds(c * BLOCK, BLOCK)
        return [
            pltpu.make_async_copy(
                state_hbm.at[:, here, pl.ds(first, keep)], edges.at[:, here, pl.ds(slot, keep)], sem.at[2 * c + i]
            )
            for i, (first, slot) in enumerate(((0, 0), (cols - keep, keep)))
        ]

    few = [(speed_hbm, speed_ref), (matrix_hbm, matrix_ref), (table_hbm, table_ref)]
    few += [(state_hbm.at[:, pl.ds(0, REACH)], rim.at[:, pl.ds(0, REACH)])]
    few += [(state_hbm.at[:, pl.ds(rows - REACH, REACH)], rim.at[:, pl.ds(REACH, REACH)])]
    few = [pltpu.make_async_copy(source, target, few_sem.at[i]) for i, (source, target) in enumerate(few)]
    for copy in few[:3]:
        copy.start()
    for c in range(chunks):
        for copy in loads(c):
            copy.start()
    for copy in few[3:]:
        copy.start()
    ids_ref[0] = lon_ref[0]
    ids_ref[1] = rad_ref[0]
    ids_ref[2] = place_ref[0]
    for copy in few[:3]:
        copy.wait()
    wide = 8 * fields
    w = lon_weights(
        matrix_ref[1], speed_ref[1], table_ref[0, :, :fields], table_ref[1, :fields, :wide], table_ref[2, :, :wide],
        table_ref[3, :, :wide],
    )
    swap = lon_ref[0] % 2 == 1
    w = jnp.concatenate([jnp.where(swap, w[size:], w[:size]), jnp.where(swap, w[:size], w[size:])], axis=0)
    high, low = parts_of(w, 2)
    weights[...] = jnp.concatenate([high, high, low], axis=1)

    def step(c, carry):
        for copy in loads(c):
            copy.wait()
        for j in range(BLOCK):
            r = c * BLOCK + j
            high, low = parts_of(edges[:, r].reshape(-1, depth), 2)
            sums = dot(weights[...], jnp.concatenate([high, low, high], axis=0))
            same[r] = sums[:size]
            first, rest = crosses
            first[r] = sums[size : size + 8]
            rest[r] = sums[size + 8 :]
        return carry

    lax.fori_loop(0, chunks, step, 0)
    for copy in few[3:]:
        copy.wait()


def lon_edges(state, matrices, speed, lon, rad, place):
    fields, rows, cols, depth = state.shape
    keep = 4
    sources = [(f, l if l < keep else cols - 2 * keep + l) for f in range(fields) for l in range(2 * keep)]
    sources = [(f, l if l < REACH or l >= cols - REACH else None) for f, l in sources]
    to_right = [(f, cols + t) for f in PACKED for t in range(REACH)]
    to_left = [(f, t - REACH) for f in PACKED for t in range(REACH)]
    size = fields * REACH
    tables = np.zeros((4, 2 * size, 128), np.float32)
    for i, table in enumerate(lon_tables(to_right + to_left, sources)):
        tables[i, : table.shape[0], : table.shape[1]] = table
    return pl.pallas_call(
        lon_edge_kernel,
        in_specs=[SMEM] * 3 + [HBM] * 4,
        out_specs=[VMEM, SMEM] + [VMEM] * 3,
        out_shape=[
            in_vmem(fields, 2 * REACH, cols, depth),
            jax.ShapeDtypeStruct((3,), jnp.int32),
            in_vmem(rows, size, depth),
            in_vmem(rows, 8, depth),
            in_vmem(rows, size - 8, depth),
        ],
        scratch_shapes=[
            pltpu.SMEM(speed.shape, f32),
            pltpu.VMEM(matrices.shape, f32),
            pltpu.VMEM(tables.shape, f32),
            pltpu.VMEM((fields, rows, 2 * keep, depth), f32),
            pltpu.VMEM((2 * size, 3 * len(sources)), bf16),
            pltpu.SemaphoreType.DMA((2 * rows // BLOCK,)),
            pltpu.SemaphoreType.DMA((5,)),
        ],
        compiler_params=LARGE,
        cost_estimate=cost(1e3, 1e3),
        name="lon_edges",
    )(lon, rad, place, *[pltpu.with_memory_space_constraint(x, pltpu.HBM) for x in (state, speed, matrices, jnp.asarray(tables))])


def turn_weights(matrix, pick, same):
    return (-0.5 * courant_step) * same * f32_dot(f32_dot(pick, matrix), pick.T)


def turn_tables(fields, cols):
    every = [(f, l) for f in range(fields) for l in range(cols)]
    pick = np.array([[float(f == a) for a in range(fields)] for f, _ in every], np.float32)
    same = np.array([[float(l == m) for _, m in every] for _, l in every], np.float32)
    return pick, same


def rad_edge_kernel(ids_ref, speed_ref, rim_ref, matrix_ref, pick_ref, same_ref, near_a, near_b, far_ref):
    fields, _, cols, depth = rim_ref.shape
    rate = (0.5 * courant_step) * speed_ref[0]
    even = ids_ref[1] % 2 == 0
    high, low = parts_of(turn_weights(matrix_ref[0], pick_ref[...], same_ref[...]), 2)
    w = jnp.concatenate([high, high, low], axis=1)

    def turned(cells):
        high, low = parts_of(cells.reshape(-1, depth), 2)
        return dot(w, jnp.concatenate([high, low, high], axis=0)).reshape(fields, cols, depth)

    first = [rim_ref[:, j] for j in range(REACH)]
    last = [rim_ref[:, REACH + j] for j in range(REACH)]
    first_turned = [turned(cells) for cells in first]
    last_turned = [turned(cells) for cells in last]
    for t in range(REACH):
        up = sum(
            SUM_TAPS[j - REACH - t] * last_turned[j] + (rate * GAP_TAPS[j - REACH - t]) * last[j]
            for j in range(t, REACH)
        )
        down = sum(
            SUM_TAPS[j + REACH - t] * first_turned[j] + (rate * GAP_TAPS[j + REACH - t]) * first[j]
            for j in range(t + 1)
        )
        near = jnp.where(even, up, down)
        near_a[0, t] = near[0]
        near_a[1, t] = near[fields - 1]
        near_b[:, t] = near[1 : fields - 1]
        far_ref[:, t] = jnp.where(even, down, up)


def rad_edges(ids, rim, matrices, speed):
    fields, _, cols, depth = rim.shape
    tables = turn_tables(fields, cols)
    return pl.pallas_call(
        rad_edge_kernel,
        in_specs=[SMEM] * 2 + [VMEM] * (2 + len(tables)),
        out_specs=[VMEM] * 3,
        out_shape=[in_vmem(n, REACH, cols, depth) for n in (2, fields - 2, fields)],
        compiler_params=LARGE,
        cost_estimate=cost(1e3, 1e3),
        name="rad_edges",
    )(ids, speed, pinned(rim), matrices, *tables)


def add_radial(speed_ref, cells, turned, total, fields, first):
    cols, depth = total.shape[2:]
    rate = (0.5 * courant_step) * speed_ref[0]
    for f in fields:
        for half in range(cols // 8):
            for lane in range(depth // 128):
                lanes = pl.ds(128 * lane, 128)
                u = [cells[f, first + j, pl.ds(8 * half, 8), lanes] for j in range(CHUNK + 2 * REACH)]
                v = [turned[first + j, pl.ds(f * cols + 8 * half, 8), lanes] for j in range(CHUNK + 2 * REACH)]
                for j in range(CHUNK):
                    at = j + REACH
                    value = total[f, first + j, pl.ds(8 * half, 8), lanes] + (rate * GAP_TAPS[0]) * u[at]
                    for k in range(1, REACH + 1):
                        value = value + SUM_TAPS[k] * (v[at + k] - v[at - k])
                        value = value + (rate * GAP_TAPS[k]) * (u[at + k] + u[at - k])
                    total[f, first + j, pl.ds(8 * half, 8), lanes] = value


def add_radial(speed_ref, cells, turned, total, fields, first):
    cols, depth = total.shape[2:]
    rate = (0.5 * courant_step) * speed_ref[0]
    for f in fields:
        for half in range(cols // 8):
            for lane in range(depth // 128):
                lanes, subs = pl.ds(128 * lane, 128), pl.ds(8 * half, 8)
                u = [cells[f, first + j, subs, lanes] for j in range(CHUNK + 2 * REACH)]
                v = [turned[first + j, pl.ds(f * cols + 8 * half, 8), lanes] for j in range(CHUNK + 2 * REACH)]
                for j in range(CHUNK):
                    at = j + REACH
                    value = total[f, first + j, subs, lanes] + (rate * GAP_TAPS[0]) * u[at]
                    for k in range(1, REACH + 1):
                        value = value + (SUM_TAPS[k] / SUM_TAPS[1]) * (v[at + k] - v[at - k])
                        value = value + (rate * GAP_TAPS[k]) * (u[at + k] + u[at - k])
                    total[f, first + j, subs, lanes] = value


def local_kernel(
    speed_ref, state_hbm, matrix_ref, pick_ref, same_ref, sum_ref, gap_ref, density_ref, packed_ref,
    total, turned, cells, rest_ref, spread_ref, w_ref, sem,
):
    fields, rows, cols, depth = total.shape
    chunks = rows // CHUNK
    size = fields * cols

    def load(c):
        return pltpu.make_async_copy(
            state_hbm.at[:, pl.ds(c * CHUNK, CHUNK)], cells.at[:, pl.ds(REACH + c * CHUNK, CHUNK)], sem.at[c]
        )

    for c in range(AHEAD):
        load(c).start()
    pick = pick_ref[...]
    own = lon_weights(matrix_ref[1], speed_ref[1], pick, pick.T, sum_ref[...], gap_ref[...])
    turn = SUM_TAPS[1] * turn_weights(matrix_ref[0], pick, same_ref[...])
    high, low = parts_of(jnp.concatenate([own, turn], axis=0), 2)
    w_ref[...] = jnp.concatenate([high, high, low], axis=1)
    for edge in (0, REACH + rows):
        cells[:, edge : edge + REACH] = jnp.zeros((fields, REACH, cols, depth), f32)
        turned[edge : edge + REACH] = jnp.zeros((REACH, size, depth), f32)

    keep_rest(density_ref, packed_ref, rest_ref, spread_ref)

    def rows_of(c, carry):
        load(c).wait()

        @pl.when(c + AHEAD < chunks)
        def _():
            load(c + AHEAD).start()

        for j in range(CHUNK):
            r = c * CHUNK + j
            here = cells[:, REACH + r].reshape(size, depth)
            high, low = parts_of(here, 2)
            both = dot(w_ref[...], jnp.concatenate([high, low, high], axis=0))
            total[:, r] = (here + both[:size]).reshape(fields, cols, depth)
            turned[REACH + r] = both[size:]
        return carry

    def radial(c, carry):
        add_radial(speed_ref, cells, turned, total, (0, fields - 1), c * CHUNK)
        return carry

    lax.fori_loop(0, chunks, rows_of, 0)
    lax.fori_loop(0, chunks, radial, 0)


def local_update(state, matrices, speed, density, packed):
    fields, rows, cols, depth = state.shape
    size = fields * cols
    every = [(f, l) for f in range(fields) for l in range(cols)]
    _, _, summed, gapped = lon_tables(every, every)
    padded = rows + 2 * REACH
    return pl.pallas_call(
        local_kernel,
        in_specs=[SMEM, HBM] + [VMEM] * 7,
        out_specs=[VMEM] * 5,
        out_shape=[
            in_vmem(*state.shape),
            in_vmem(padded, size, depth),
            in_vmem(fields, padded, cols, depth),
            in_vmem(16, density.shape[2]),
            in_vmem(3, *density.shape[1:]),
        ],
        scratch_shapes=[pltpu.VMEM((2 * size, 3 * size), bf16), pltpu.SemaphoreType.DMA((rows // CHUNK,))],
        compiler_params=SMALL,
        cost_estimate=cost(1e3, 1e3),
        name="local_update",
    )(
        speed, pltpu.with_memory_space_constraint(state, pltpu.HBM), matrices, *turn_tables(fields, cols), summed, gapped,
        density, packed,
    )


def radial_kernel(fields, speed_ref, cells, turned, _, total):
    def radial(c, carry):
        add_radial(speed_ref, cells, turned, total, fields, c * CHUNK)
        return carry

    lax.fori_loop(0, total.shape[1] // CHUNK, radial, 0)


def radial_update(fields, cells, turned, part, speed):
    return pl.pallas_call(
        functools.partial(radial_kernel, fields),
        in_specs=[SMEM] + [VMEM] * 3,
        out_specs=VMEM,
        out_shape=in_vmem(*part.shape),
        input_output_aliases={3: 0},
        compiler_params=SMALL,
        cost_estimate=cost(1e8, 6e6),
        name="radial_update",
    )(speed, pinned(cells), pinned(turned), pinned(part))


def placed(tiles, field, from_left):
    start = REACH * PACKED.index(field)
    tile, offset = start // 8, start % 8
    cells = tiles[tile]
    sub = lax.broadcasted_iota(jnp.int32, cells.shape, 1)
    if offset + REACH > 8:
        cells = jnp.where(sub >= offset, cells, tiles[tile + 1])
    goal = 0 if from_left else 8 - REACH
    shift = (goal - offset) % 8
    if shift:
        cells = pltpu.roll(cells, shift, 1)
    keep = sub < REACH if from_left else sub >= 8 - REACH
    return jnp.where(keep, cells, 0.0)


def by_side(lon, same, crosses):
    even = lon % 2 == 0
    lefts, rights = {}, {}
    for t, cross in enumerate(crosses):
        near = same[:, 8 * t : 8 * t + 8]
        lefts[t] = jnp.where(even, cross, near)
        rights[t] = jnp.where(even, near, cross)
    return lefts, rights


def with_sides(cells, lefts, rights, field):
    cols = cells.shape[1]
    return jnp.concatenate(
        [cells[:, :8] + placed(lefts, field, True), cells[:, cols - 8 :] + placed(rights, field, False)], axis=1
    )


def with_ends(cells, step, steps, rad, near, far):
    rows = cells.shape[0]
    even = rad % 2 == 0
    below, above = jnp.where(even, far, near), jnp.where(even, near, far)
    at_low = (step == 0).astype(f32)
    at_top = (step == steps - 1).astype(f32)
    return jnp.concatenate(
        [cells[:REACH] + at_low * below, cells[REACH : rows - REACH], cells[rows - REACH :] + at_top * above], axis=0
    )


def tile_sum_kernel(
    ids_ref, part_ref, vol_ref, same_ref, cross_ref, near_ref, far_ref, rest_ref, hit_ref, seg_ref, spot_ref,
    out_ref, lines_ref,
):
    all_rows, cols, depth = vol_ref.shape
    tiles, points = out_ref.shape[0], out_ref.shape[1] // 3
    rows = 16
    steps = all_rows // rows

    def add(step, carry):
        here = pl.ds(pl.multiple_of(step * rows, rows), rows)
        lefts, rights = by_side(ids_ref[0], same_ref[here, :8], [cross_ref[here]])
        vol = vol_ref[here]
        for c, field in enumerate((0, 7)):
            cells = with_sides(part_ref[field, here], lefts, rights, field)
            cells = with_ends(cells, step, steps, ids_ref[1], near_ref[c], far_ref[field])
            lines = exact_dot((cells * vol).reshape(rows * cols, depth), seg_ref[...])
            lines_ref[c, here] = jnp.sum(lines.reshape(rows, cols, -1) * spot_ref[...][None], axis=1)
        return carry

    lax.fori_loop(0, steps, add, 0)
    for c in range(2):
        sums = sum(dot(hit_ref[...], part) for part in parts_of(lines_ref[c], 3))
        out_ref[:, c * points : (c + 1) * points] = sums
    mine = lax.broadcasted_iota(jnp.int32, (tiles, points), 0) == ids_ref[2]
    out_ref[:, 2 * points :] = jnp.where(mine, rest_ref[8:9], 0.0)


def tile_sums(ids, part, vol, same, cross, near, far, rest, hits, seg, spot):
    _, rows, _, _ = part.shape
    points = seg.shape[1]
    tiles = hits.shape[0]
    return pl.pallas_call(
        tile_sum_kernel,
        in_specs=[SMEM] + [VMEM] * 10,
        out_specs=VMEM,
        out_shape=in_vmem(tiles, 3 * points),
        scratch_shapes=[pltpu.VMEM((2, rows, points), f32)],
        compiler_params=LARGE,
        cost_estimate=cost(1e3, 1e3),
        name="tile_sums",
    )(ids, *[pinned(x) for x in (part, vol, same, cross, near, far, rest)], hits, seg, spot)


def drifted(density, courant):
    for _ in range(DRIFT):
        density = density - courant * (density - pltpu.roll(density, 1, 1))
    return density


def columns_of(packed_ref, channels):
    turned = jnp.transpose(packed_ref[...])
    return [turned[:channels, i : i + 1] for i in range(4)]


def keep_rest(density_ref, packed_ref, out_ref, spread_ref):
    _, channels, points = density_ref.shape
    courant, weight, first, second = columns_of(packed_ref, channels)
    rows = []
    for given in (first, second):
        for k, choices in enumerate((1.0, 3.0, 3.0, 1.0)):
            gain = (inner_step * choices) * weight * given
            for _ in range(k):
                gain = gain * courant
            for _ in range(DRIFT - k):
                gain = gain * (1.0 - courant)
            rows.append(jnp.broadcast_to(jnp.sum(gain, axis=0, keepdims=True), (1, points)))
    rest = jnp.sum(weight * drifted(density_ref[0], courant), axis=0, keepdims=True)
    out_ref[...] = jnp.concatenate(rows + [rest] * 8, axis=0)
    for i, column in enumerate((courant, first, second)):
        spread_ref[i] = jnp.broadcast_to(column, (channels, points))


def pressures_of(sums, rest_ref):
    points = sums.shape[1] // 3
    pressure = sums[:, 2 * points :]
    for c in range(2):
        source = sums[:, c * points : (c + 1) * points]
        for k in range(DRIFT + 1):
            shifted = pltpu.roll(source, k, 1) if k else source
            pressure = pressure + rest_ref[(DRIFT + 1) * c + k : (DRIFT + 1) * c + k + 1] * shifted
    return pressure


def finish_field(field, refs, part_ref, out):
    ids_ref, near_a, near_b, far_ref, same_ref, *cross_refs = refs
    rows = 2 * CHUNK
    steps = out.shape[0] // rows
    last_field = far_ref.shape[0] - 1

    def step(i, carry):
        here = pl.ds(pl.multiple_of(i * rows, rows), rows)
        lefts, rights = {}, {}
        first = REACH * PACKED.index(field)
        for t in range(first // 8, (first + REACH - 1) // 8 + 1):
            cross = cross_refs[0][here] if t == 0 else cross_refs[1][here, 8 * t - 8 : 8 * t]
            one = by_side(ids_ref[0], same_ref[here, 8 * t : 8 * t + 8], [cross])
            lefts[t], rights[t] = one[0][0], one[1][0]
        near = near_a[field // last_field] if field in (0, last_field) else near_b[field - 1]
        cells = with_sides(part_ref[field, here], lefts, rights, field)
        out[here] = with_ends(cells, i, steps, ids_ref[1], near, far_ref[field])
        return carry

    lax.fori_loop(0, steps, step, 0)


def most_kernel(ids_ref, part_ref, *refs):
    *sides, out_hbm, last_ref, done, sem = refs
    copies = []
    for field in range(done.shape[0]):
        finish_field(field, (ids_ref, *sides), part_ref, done.at[field])
        copies.append(pltpu.make_async_copy(done.at[field], out_hbm.at[field], sem.at[field]))
        copies[-1].start()
    finish_field(done.shape[0], (ids_ref, *sides), part_ref, last_ref)
    for copy in copies:
        copy.wait()


def last_kernel(
    ids_ref, cells_ref, _, hit_ref, sums_ref, rest_ref, spot_ref, seg_ref, density_ref, spread_ref,
    out_hbm, drifted_hbm, done, back_ref, moved, sem,
):
    points = spot_ref.shape[1]
    rows, cols, depth = done.shape
    last = out_hbm.shape[0] - 1
    back_ref[...] = sum(dot(hit_ref[...], p) for p in parts_of(pressures_of(sums_ref[...], rest_ref), 3))
    copies = []
    size = 2 * CHUNK
    for first in range(0, rows, size):
        here = pl.ds(first, size)
        spread = (back_ref[here][:, None, :] * spot_ref[...][None]).reshape(-1, points)
        returned = exact_dot(spread, seg_ref[...]).reshape(-1, cols, depth)
        cells = cells_ref[here]
        done[here] = cells + nudge_rate * (returned - cells)
        copies.append(pltpu.make_async_copy(done.at[here], out_hbm.at[last, here], sem.at[len(copies)]))
        copies[-1].start()
    source = sums_ref[pl.ds(ids_ref[2], 1), :]
    density = density_ref[0] + inner_step * (
        spread_ref[1] * source[:, :points] + spread_ref[2] * source[:, points : 2 * points]
    )
    moved[0] = drifted(density, spread_ref[0])
    copies.append(pltpu.make_async_copy(moved, drifted_hbm, sem.at[len(copies)]))
    copies[-1].start()
    for copy in copies:
        copy.wait()


def pressures_of(sums, rest_ref):
    points = sums.shape[1] // 3
    pressure = sums[:, 2 * points :]
    for c in range(2):
        source = sums[:, c * points : (c + 1) * points]
        for k in range(DRIFT + 1):
            shifted = pltpu.roll(source, k, 1) if k else source
            pressure = pressure + rest_ref[(DRIFT + 1) * c + k : (DRIFT + 1) * c + k + 1] * shifted
    return pressure


def finish_most(ids, part, rad, same, crosses):
    fields, rows, cols, depth = part.shape
    pins = [pinned(x) for x in (part, *rad, same, *crosses)]
    return pl.pallas_call(
        most_kernel,
        in_specs=[SMEM] + [VMEM] * len(pins),
        out_specs=[HBM, VMEM],
        out_shape=[jax.ShapeDtypeStruct(part.shape, f32), in_vmem(rows, cols, depth)],
        scratch_shapes=[pltpu.VMEM((fields - 1, rows, cols, depth), f32), pltpu.SemaphoreType.DMA((fields - 1,))],
        compiler_params=LARGE,
        cost_estimate=cost(1e8, 1.6e7),
        name="finish_most",
    )(ids, *pins)


def finish_last(ids, cells, most, hits, sums, rest, spot, seg, density, spread):
    rows, cols, depth = cells.shape
    return pl.pallas_call(
        last_kernel,
        in_specs=[SMEM, VMEM, HBM] + [VMEM] * 7,
        out_specs=[HBM, HBM],
        out_shape=[jax.ShapeDtypeStruct(most.shape, f32), jax.ShapeDtypeStruct(density.shape, f32)],
        input_output_aliases={2: 0},
        scratch_shapes=[
            pltpu.VMEM(cells.shape, f32),
            pltpu.VMEM((rows, spot.shape[1]), f32),
            pltpu.VMEM(density.shape, f32),
            pltpu.SemaphoreType.DMA((rows // (2 * CHUNK) + 1,)),
        ],
        compiler_params=SMALL,
        cost_estimate=cost(1e3, 1e3),
        name="finish_last",
    )(ids, pinned(cells), most, hits, pinned(sums), pinned(rest), spot, seg, density, pinned(spread))


def swap(x, axis, bit):
    return lax.ppermute(x, axis, [(i, i ^ bit) for i in range(lax.axis_size(axis))])


def per_device(
    state,
    flux_matrices,
    wave_speed,
    flux_volume,
    block_tile,
    tile_of_device,
    phase_density,
    injection,
    drift_courant,
    energy_weight,
):
    fields, rows, cols, depth = state.shape
    n_rad, n_lon = lax.axis_size("rad"), lax.axis_size("lon")
    points = cols * ZSEG
    lon, rad, place = [lax.axis_index(axes).astype(jnp.int32).reshape(1) for axes in ("lon", "rad", ("rad", "lon"))]

    across = [(i, (i + 1 if i % 2 else i - 1) % n_lon) for i in range(n_lon)]
    beyond = [(i, j) for i in range(n_rad) for j in [i + 1 if i % 2 else i - 1] if 0 <= j < n_rad]
    rim, ids, same, *crosses = lon_edges(state, flux_matrices, wave_speed, lon, rad, place)
    cross_0 = lax.ppermute(crosses[0], "lon", across)
    same = swap(same, "lon", 1)
    cross_1 = lax.ppermute(crosses[1], "lon", across)

    near_a, near_b, far = rad_edges(ids, rim, flux_matrices, wave_speed)
    near_a = swap(near_a, "rad", 1)
    far = lax.ppermute(far, "rad", beyond)

    packed = jnp.concatenate([drift_courant[None], energy_weight[None], injection], axis=0)
    packed = jnp.pad(packed, ((0, 4), (0, -packed.shape[1] % 128)))

    part, turned, cells, rest, spread = local_update(state, flux_matrices, wave_speed, phase_density, packed)

    targets = block_tile[0, :, 0]
    hits = (tile_of_device[:, None] == targets[None, :]).astype(bf16)
    hits_back = (targets[:, None] == tile_of_device[None, :]).astype(bf16)
    seg_cells = depth // ZSEG
    seg = np.array([[float(p % ZSEG == z // seg_cells) for p in range(points)] for z in range(depth)], np.float32)
    spot = np.array([[float(p // ZSEG == l) for p in range(points)] for l in range(cols)], np.float32)
    sums = tile_sums(
        ids, part, flux_volume, same, cross_0, near_a, far, rest, hits, jnp.asarray(seg, bf16), jnp.asarray(spot)
    )
    near_b, sums = lax.optimization_barrier((near_b, sums))
    near_b = swap(near_b, "rad", 1)
    part, sums = lax.optimization_barrier((part, sums))
    others = [swap(sums, "rad", step) for step in range(1, n_rad)]
    part = radial_update(tuple(range(1, fields - 1)), cells, turned, part, wave_speed)
    part, sums = lax.optimization_barrier((part, sums))
    sums = sum(others, sums)
    sums = sums + swap(sums, "lon", 1)
    others = [swap(sums, "lon", step) for step in range(2, n_lon, 2)]
    most, last = finish_most(ids, part, (near_a, near_b, far), same, (cross_0, cross_1))
    sums, most = lax.optimization_barrier((sums, most))
    sums = sum(others, sums)
    done, density = finish_last(
        ids, last, most, hits_back, sums, rest, jnp.asarray(spot), jnp.asarray(seg.T, bf16), phase_density, spread
    )
    return done, density


def solution(mesh):
    in_specs = (
        P(None, "rad", "lon", None),
        P(),
        P(),
        P("rad", "lon", None),
        P("lon", "rad", None),
        P(),
        P(("rad", "lon"), None, None),
        P(),
        P(),
        P(),
    )
    out_specs = (P(None, "rad", "lon", None), P(("rad", "lon"), None, None))
    return jax.shard_map(per_device, mesh=mesh, in_specs=in_specs, out_specs=out_specs, check_vma=False)
```

```python
import functools

import jax
import jax.numpy as jnp
import numpy as np
from jax import lax
from jax.experimental import pallas as pl
from jax.experimental.pallas import tpu as pltpu
from jax.sharding import PartitionSpec as P

ZSEG = 8
DRIFT = 3
REACH = 3

courant_step = 0.4
nudge_rate = 0.5
inner_step = 0.5

SUM_TAPS = {k: v / 60.0 for k, v in zip(range(-3, 4), (-2.0, 18.0, -90.0, 0.0, 90.0, -18.0, 2.0))}
GAP_TAPS = {k: v / 60.0 for k, v in zip(range(-3, 4), (2.0, -12.0, 30.0, -40.0, 30.0, -12.0, 2.0))}

PACKED = (0, 7, 1, 2, 3, 4, 5, 6)

f32 = jnp.float32
bf16 = jnp.bfloat16


def cost(flops, bytes_accessed):
    return pl.CostEstimate(flops=int(flops), bytes_accessed=int(bytes_accessed), transcendentals=0)


def parts_of(x, count):
    parts = []
    for _ in range(count):
        part = x.astype(bf16)
        parts.append(part)
        x = x - part.astype(f32)
    return parts


def dot(a, b):
    return jnp.dot(a, b, preferred_element_type=f32)


def exact_dot(x, ones):
    return sum(dot(part, ones) for part in parts_of(x, 3))


def lon_tables(rows, cols):
    fields = 1 + max(f for f, _ in cols)
    pick_row = np.array([[float(f == a) for a in range(fields)] for f, _ in rows], np.float32)
    pick_col = np.array([[float(f == b) for f, _ in cols] for b in range(fields)], np.float32)
    summed = np.array([[0.0 if s is None else SUM_TAPS.get(s - t, 0.0) for _, s in cols] for _, t in rows], np.float32)
    gapped = np.array(
        [[0.0 if s is None or f != g else GAP_TAPS.get(s - t, 0.0) for g, s in cols] for f, t in rows], np.float32
    )
    return pick_row, pick_col, summed, gapped


def lon_weights(matrix, wave_rate, pick_row, pick_col, summed, gapped):
    half = 0.5 * courant_step
    spread = f32_dot(f32_dot(pick_row, matrix), pick_col)
    return (half * wave_rate) * gapped - half * spread * summed


def f32_dot(a, b):
    return jnp.dot(a, b, precision=lax.Precision.HIGHEST, preferred_element_type=f32)


def whole(array):
    zeros = (0,) * array.ndim
    return pl.BlockSpec(array.shape, lambda *_: zeros)


SMEM = pl.BlockSpec(memory_space=pltpu.SMEM)
VMEM = pl.BlockSpec(memory_space=pltpu.VMEM)
HBM = pl.BlockSpec(memory_space=pltpu.HBM)
LARGE = pltpu.CompilerParams(vmem_limit_bytes=12 * 2**20)
SMALL = pltpu.CompilerParams(vmem_limit_bytes=5 * 2**20)
CHUNK = 8
BLOCK = 16
AHEAD = 3


def in_vmem(*shape):
    return pltpu.VMEM(shape, f32)


def pinned(x):
    return pltpu.with_memory_space_constraint(x, pltpu.VMEM)


def lon_edge_kernel(lon_ref, rad_ref, place_ref, state_hbm, speed_hbm, matrix_hbm, table_hbm, rim, ids_ref, same, *refs):
    *crosses, speed_ref, matrix_ref, table_ref, edges, weights, sem, few_sem = refs
    fields, rows, cols, depth = state_hbm.shape
    chunks = rows // BLOCK
    size = same.shape[1]
    keep = edges.shape[2] // 2

    def loads(c):
        here = pl.ds(c * BLOCK, BLOCK)
        return [
            pltpu.make_async_copy(
                state_hbm.at[:, here, pl.ds(first, keep)], edges.at[:, here, pl.ds(slot, keep)], sem.at[2 * c + i]
            )
            for i, (first, slot) in enumerate(((0, 0), (cols - keep, keep)))
        ]

    few = [(speed_hbm, speed_ref), (matrix_hbm, matrix_ref), (table_hbm, table_ref)]
    few += [(state_hbm.at[:, pl.ds(0, REACH)], rim.at[:, pl.ds(0, REACH)])]
    few += [(state_hbm.at[:, pl.ds(rows - REACH, REACH)], rim.at[:, pl.ds(REACH, REACH)])]
    few = [pltpu.make_async_copy(source, target, few_sem.at[i]) for i, (source, target) in enumerate(few)]
    for copy in few[:3]:
        copy.start()
    for c in range(chunks):
        for copy in loads(c):
            copy.start()
    for copy in few[3:]:
        copy.start()
    ids_ref[0] = lon_ref[0]
    ids_ref[1] = rad_ref[0]
    ids_ref[2] = place_ref[0]
    for copy in few[:3]:
        copy.wait()
    wide = 8 * fields
    w = lon_weights(
        matrix_ref[1], speed_ref[1], table_ref[0, :, :fields], table_ref[1, :fields, :wide], table_ref[2, :, :wide],
        table_ref[3, :, :wide],
    )
    swap = lon_ref[0] % 2 == 1
    w = jnp.concatenate([jnp.where(swap, w[size:], w[:size]), jnp.where(swap, w[:size], w[size:])], axis=0)
    high, low = parts_of(w, 2)
    weights[...] = jnp.concatenate([high, high, low], axis=1)

    def step(c, carry):
        for copy in loads(c):
            copy.wait()
        for j in range(BLOCK):
            r = c * BLOCK + j
            high, low = parts_of(edges[:, r].reshape(-1, depth), 2)
            sums = dot(weights[...], jnp.concatenate([high, low, high], axis=0))
            same[r] = sums[:size]
            first, rest = crosses
            first[r] = sums[size : size + 8]
            rest[r] = sums[size + 8 :]
        return carry

    lax.fori_loop(0, chunks, step, 0)
    for copy in few[3:]:
        copy.wait()


def lon_edges(state, matrices, speed, lon, rad, place):
    fields, rows, cols, depth = state.shape
    keep = 4
    sources = [(f, l if l < keep else cols - 2 * keep + l) for f in range(fields) for l in range(2 * keep)]
    sources = [(f, l if l < REACH or l >= cols - REACH else None) for f, l in sources]
    to_right = [(f, cols + t) for f in PACKED for t in range(REACH)]
    to_left = [(f, t - REACH) for f in PACKED for t in range(REACH)]
    size = fields * REACH
    tables = np.zeros((4, 2 * size, 128), np.float32)
    for i, table in enumerate(lon_tables(to_right + to_left, sources)):
        tables[i, : table.shape[0], : table.shape[1]] = table
    return pl.pallas_call(
        lon_edge_kernel,
        in_specs=[SMEM] * 3 + [HBM] * 4,
        out_specs=[VMEM, SMEM] + [VMEM] * 3,
        out_shape=[
            in_vmem(fields, 2 * REACH, cols, depth),
            jax.ShapeDtypeStruct((3,), jnp.int32),
            in_vmem(rows, size, depth),
            in_vmem(rows, 8, depth),
            in_vmem(rows, size - 8, depth),
        ],
        scratch_shapes=[
            pltpu.SMEM(speed.shape, f32),
            pltpu.VMEM(matrices.shape, f32),
            pltpu.VMEM(tables.shape, f32),
            pltpu.VMEM((fields, rows, 2 * keep, depth), f32),
            pltpu.VMEM((2 * size, 3 * len(sources)), bf16),
            pltpu.SemaphoreType.DMA((2 * rows // BLOCK,)),
            pltpu.SemaphoreType.DMA((5,)),
        ],
        compiler_params=LARGE,
        cost_estimate=cost(1e3, 1e3),
        name="lon_edges",
    )(lon, rad, place, *[pltpu.with_memory_space_constraint(x, pltpu.HBM) for x in (state, speed, matrices, jnp.asarray(tables))])


def turn_weights(matrix, pick, same):
    return (-0.5 * courant_step) * same * f32_dot(f32_dot(pick, matrix), pick.T)


def turn_tables(fields, cols):
    every = [(f, l) for f in range(fields) for l in range(cols)]
    pick = np.array([[float(f == a) for a in range(fields)] for f, _ in every], np.float32)
    same = np.array([[float(l == m) for _, m in every] for _, l in every], np.float32)
    return pick, same


def rad_edge_kernel(ids_ref, speed_ref, rim_ref, matrix_ref, pick_ref, same_ref, near_a, near_b, far_ref):
    fields, _, cols, depth = rim_ref.shape
    rate = (0.5 * courant_step) * speed_ref[0]
    even = ids_ref[1] % 2 == 0
    high, low = parts_of(turn_weights(matrix_ref[0], pick_ref[...], same_ref[...]), 2)
    w = jnp.concatenate([high, high, low], axis=1)

    def turned(cells):
        high, low = parts_of(cells.reshape(-1, depth), 2)
        return dot(w, jnp.concatenate([high, low, high], axis=0)).reshape(fields, cols, depth)

    first = [rim_ref[:, j] for j in range(REACH)]
    last = [rim_ref[:, REACH + j] for j in range(REACH)]
    first_turned = [turned(cells) for cells in first]
    last_turned = [turned(cells) for cells in last]
    for t in range(REACH):
        up = sum(
            SUM_TAPS[j - REACH - t] * last_turned[j] + (rate * GAP_TAPS[j - REACH - t]) * last[j]
            for j in range(t, REACH)
        )
        down = sum(
            SUM_TAPS[j + REACH - t] * first_turned[j] + (rate * GAP_TAPS[j + REACH - t]) * first[j]
            for j in range(t + 1)
        )
        near = jnp.where(even, up, down)
        near_a[0, t] = near[0]
        near_a[1, t] = near[fields - 1]
        near_b[:, t] = near[1 : fields - 1]
        far_ref[:, t] = jnp.where(even, down, up)


def rad_edges(ids, rim, matrices, speed):
    fields, _, cols, depth = rim.shape
    tables = turn_tables(fields, cols)
    return pl.pallas_call(
        rad_edge_kernel,
        in_specs=[SMEM] * 2 + [VMEM] * (2 + len(tables)),
        out_specs=[VMEM] * 3,
        out_shape=[in_vmem(n, REACH, cols, depth) for n in (2, fields - 2, fields)],
        compiler_params=LARGE,
        cost_estimate=cost(1e3, 1e3),
        name="rad_edges",
    )(ids, speed, pinned(rim), matrices, *tables)


def add_radial(speed_ref, cells, turned, total, fields, first):
    cols, depth = total.shape[2:]
    rate = (0.5 * courant_step) * speed_ref[0]
    for f in fields:
        for half in range(cols // 8):
            for lane in range(depth // 128):
                lanes = pl.ds(128 * lane, 128)
                u = [cells[f, first + j, pl.ds(8 * half, 8), lanes] for j in range(CHUNK + 2 * REACH)]
                v = [turned[first + j, pl.ds(f * cols + 8 * half, 8), lanes] for j in range(CHUNK + 2 * REACH)]
                for j in range(CHUNK):
                    at = j + REACH
                    value = total[f, first + j, pl.ds(8 * half, 8), lanes] + (rate * GAP_TAPS[0]) * u[at]
                    for k in range(1, REACH + 1):
                        value = value + SUM_TAPS[k] * (v[at + k] - v[at - k])
                        value = value + (rate * GAP_TAPS[k]) * (u[at + k] + u[at - k])
                    total[f, first + j, pl.ds(8 * half, 8), lanes] = value


def add_radial(speed_ref, cells, turned, total, fields, first):
    cols, depth = total.shape[2:]
    rate = (0.5 * courant_step) * speed_ref[0]
    for f in fields:
        for half in range(cols // 8):
            for lane in range(depth // 128):
                lanes, subs = pl.ds(128 * lane, 128), pl.ds(8 * half, 8)
                u = [cells[f, first + j, subs, lanes] for j in range(CHUNK + 2 * REACH)]
                v = [turned[first + j, pl.ds(f * cols + 8 * half, 8), lanes] for j in range(CHUNK + 2 * REACH)]
                for j in range(CHUNK):
                    at = j + REACH
                    value = total[f, first + j, subs, lanes] + (rate * GAP_TAPS[0]) * u[at]
                    for k in range(1, REACH + 1):
                        value = value + (SUM_TAPS[k] / SUM_TAPS[1]) * (v[at + k] - v[at - k])
                        value = value + (rate * GAP_TAPS[k]) * (u[at + k] + u[at - k])
                    total[f, first + j, subs, lanes] = value


def local_kernel(
    speed_ref, state_hbm, matrix_ref, pick_ref, same_ref, sum_ref, gap_ref, density_ref, packed_ref,
    total, turned, cells, rest_ref, spread_ref, w_ref, sem,
):
    fields, rows, cols, depth = total.shape
    chunks = rows // CHUNK
    size = fields * cols

    def load(c):
        return pltpu.make_async_copy(
            state_hbm.at[:, pl.ds(c * CHUNK, CHUNK)], cells.at[:, pl.ds(REACH + c * CHUNK, CHUNK)], sem.at[c]
        )

    for c in range(AHEAD):
        load(c).start()
    pick = pick_ref[...]
    own = lon_weights(matrix_ref[1], speed_ref[1], pick, pick.T, sum_ref[...], gap_ref[...])
    turn = SUM_TAPS[1] * turn_weights(matrix_ref[0], pick, same_ref[...])
    high, low = parts_of(jnp.concatenate([own, turn], axis=0), 2)
    w_ref[...] = jnp.concatenate([high, high, low], axis=1)
    for edge in (0, REACH + rows):
        cells[:, edge : edge + REACH] = jnp.zeros((fields, REACH, cols, depth), f32)
        turned[edge : edge + REACH] = jnp.zeros((REACH, size, depth), f32)

    keep_rest(density_ref, packed_ref, rest_ref, spread_ref)

    def rows_of(c, carry):
        load(c).wait()

        @pl.when(c + AHEAD < chunks)
        def _():
            load(c + AHEAD).start()

        for j in range(CHUNK):
            r = c * CHUNK + j
            here = cells[:, REACH + r].reshape(size, depth)
            high, low = parts_of(here, 2)
            both = dot(w_ref[...], jnp.concatenate([high, low, high], axis=0))
            total[:, r] = (here + both[:size]).reshape(fields, cols, depth)
            turned[REACH + r] = both[size:]
        return carry

    def radial(c, carry):
        add_radial(speed_ref, cells, turned, total, (0, fields - 1), c * CHUNK)
        return carry

    lax.fori_loop(0, chunks, rows_of, 0)
    lax.fori_loop(0, chunks, radial, 0)


def local_update(state, matrices, speed, density, packed):
    fields, rows, cols, depth = state.shape
    size = fields * cols
    every = [(f, l) for f in range(fields) for l in range(cols)]
    _, _, summed, gapped = lon_tables(every, every)
    padded = rows + 2 * REACH
    return pl.pallas_call(
        local_kernel,
        in_specs=[SMEM, HBM] + [VMEM] * 7,
        out_specs=[VMEM] * 5,
        out_shape=[
            in_vmem(*state.shape),
            in_vmem(padded, size, depth),
            in_vmem(fields, padded, cols, depth),
            in_vmem(16, density.shape[2]),
            in_vmem(3, *density.shape[1:]),
        ],
        scratch_shapes=[pltpu.VMEM((2 * size, 3 * size), bf16), pltpu.SemaphoreType.DMA((rows // CHUNK,))],
        compiler_params=SMALL,
        cost_estimate=cost(1e3, 1e3),
        name="local_update",
    )(
        speed, pltpu.with_memory_space_constraint(state, pltpu.HBM), matrices, *turn_tables(fields, cols), summed, gapped,
        density, packed,
    )


def radial_kernel(fields, speed_ref, cells, turned, _, total):
    def radial(c, carry):
        add_radial(speed_ref, cells, turned, total, fields, c * CHUNK)
        return carry

    lax.fori_loop(0, total.shape[1] // CHUNK, radial, 0)


def radial_update(fields, cells, turned, part, speed):
    return pl.pallas_call(
        functools.partial(radial_kernel, fields),
        in_specs=[SMEM] + [VMEM] * 3,
        out_specs=VMEM,
        out_shape=in_vmem(*part.shape),
        input_output_aliases={3: 0},
        compiler_params=SMALL,
        cost_estimate=cost(1e8, 6e6),
        name="radial_update",
    )(speed, pinned(cells), pinned(turned), pinned(part))


def placed(tiles, field, from_left):
    start = REACH * PACKED.index(field)
    tile, offset = start // 8, start % 8
    cells = tiles[tile]
    sub = lax.broadcasted_iota(jnp.int32, cells.shape, 1)
    if offset + REACH > 8:
        cells = jnp.where(sub >= offset, cells, tiles[tile + 1])
    goal = 0 if from_left else 8 - REACH
    shift = (goal - offset) % 8
    if shift:
        cells = pltpu.roll(cells, shift, 1)
    keep = sub < REACH if from_left else sub >= 8 - REACH
    return jnp.where(keep, cells, 0.0)


def by_side(lon, same, crosses):
    even = lon % 2 == 0
    lefts, rights = {}, {}
    for t, cross in enumerate(crosses):
        near = same[:, 8 * t : 8 * t + 8]
        lefts[t] = jnp.where(even, cross, near)
        rights[t] = jnp.where(even, near, cross)
    return lefts, rights


def with_sides(cells, lefts, rights, field):
    cols = cells.shape[1]
    return jnp.concatenate(
        [cells[:, :8] + placed(lefts, field, True), cells[:, cols - 8 :] + placed(rights, field, False)], axis=1
    )


def with_ends(cells, step, steps, rad, near, far):
    rows = cells.shape[0]
    even = rad % 2 == 0
    below, above = jnp.where(even, far, near), jnp.where(even, near, far)
    at_low = (step == 0).astype(f32)
    at_top = (step == steps - 1).astype(f32)
    return jnp.concatenate(
        [cells[:REACH] + at_low * below, cells[REACH : rows - REACH], cells[rows - REACH :] + at_top * above], axis=0
    )


def tile_sum_kernel(
    ids_ref, part_ref, vol_ref, same_ref, cross_ref, near_ref, far_ref, rest_ref, hit_ref, seg_ref, spot_ref,
    out_ref, lines_ref,
):
    all_rows, cols, depth = vol_ref.shape
    tiles, points = out_ref.shape[0], out_ref.shape[1] // 3
    rows = 16
    steps = all_rows // rows

    def add(step, carry):
        here = pl.ds(pl.multiple_of(step * rows, rows), rows)
        lefts, rights = by_side(ids_ref[0], same_ref[here, :8], [cross_ref[here]])
        vol = vol_ref[here]
        for c, field in enumerate((0, 7)):
            cells = with_sides(part_ref[field, here], lefts, rights, field)
            cells = with_ends(cells, step, steps, ids_ref[1], near_ref[c], far_ref[field])
            lines = exact_dot((cells * vol).reshape(rows * cols, depth), seg_ref[...])
            lines_ref[c, here] = jnp.sum(lines.reshape(rows, cols, -1) * spot_ref[...][None], axis=1)
        return carry

    lax.fori_loop(0, steps, add, 0)
    for c in range(2):
        sums = sum(dot(hit_ref[...], part) for part in parts_of(lines_ref[c], 3))
        out_ref[:, c * points : (c + 1) * points] = sums
    mine = lax.broadcasted_iota(jnp.int32, (tiles, points), 0) == ids_ref[2]
    out_ref[:, 2 * points :] = jnp.where(mine, rest_ref[8:9], 0.0)


def tile_sums(ids, part, vol, same, cross, near, far, rest, hits, seg, spot):
    _, rows, _, _ = part.shape
    points = seg.shape[1]
    tiles = hits.shape[0]
    return pl.pallas_call(
        tile_sum_kernel,
        in_specs=[SMEM] + [VMEM] * 10,
        out_specs=VMEM,
        out_shape=in_vmem(tiles, 3 * points),
        scratch_shapes=[pltpu.VMEM((2, rows, points), f32)],
        compiler_params=LARGE,
        cost_estimate=cost(1e3, 1e3),
        name="tile_sums",
    )(ids, *[pinned(x) for x in (part, vol, same, cross, near, far, rest)], hits, seg, spot)


def drifted(density, courant):
    for _ in range(DRIFT):
        density = density - courant * (density - pltpu.roll(density, 1, 1))
    return density


def columns_of(packed_ref, channels):
    turned = jnp.transpose(packed_ref[...])
    return [turned[:channels, i : i + 1] for i in range(4)]


def keep_rest(density_ref, packed_ref, out_ref, spread_ref):
    _, channels, points = density_ref.shape
    courant, weight, first, second = columns_of(packed_ref, channels)
    rows = []
    for given in (first, second):
        for k, choices in enumerate((1.0, 3.0, 3.0, 1.0)):
            gain = (inner_step * choices) * weight * given
            for _ in range(k):
                gain = gain * courant
            for _ in range(DRIFT - k):
                gain = gain * (1.0 - courant)
            rows.append(jnp.broadcast_to(jnp.sum(gain, axis=0, keepdims=True), (1, points)))
    rest = jnp.sum(weight * drifted(density_ref[0], courant), axis=0, keepdims=True)
    out_ref[...] = jnp.concatenate(rows + [rest] * 8, axis=0)
    for i, column in enumerate((courant, first, second)):
        spread_ref[i] = jnp.broadcast_to(column, (channels, points))


def message_kernel(ids_ref, sums_ref, other_ref, rest_ref, *outs):
    *outs, total_ref = outs
    total_ref[...] = sums_ref[...] + other_ref[...]
    tiles, size = total_ref.shape
    points = size // 3
    pressure = pressures_of(total_ref[...], rest_ref)
    for i, out in enumerate(outs):
        owner = ids_ref[2] - ids_ref[0] + (ids_ref[0] ^ (2 * i))
        source = total_ref[pl.ds(owner, 1), :]
        out[:tiles] = pressure
        out[tiles:] = jnp.concatenate(
            [source[:, :points], source[:, points : 2 * points], jnp.zeros((6, points), f32)], axis=0
        )


def messages(ids, sums, other, rest, count):
    tiles, size = sums.shape
    return pl.pallas_call(
        message_kernel,
        in_specs=[SMEM] + [VMEM] * 3,
        out_specs=[VMEM] * count,
        out_shape=[in_vmem(tiles + 8, size // 3)] * count,
        scratch_shapes=[pltpu.VMEM(sums.shape, f32)],
        compiler_params=SMALL,
        cost_estimate=cost(1e3, 1e3),
        name="messages",
    )(ids, pinned(sums), pinned(other), pinned(rest))


def pressures_of(sums, rest_ref):
    points = sums.shape[1] // 3
    pressure = sums[:, 2 * points :]
    for c in range(2):
        source = sums[:, c * points : (c + 1) * points]
        for k in range(DRIFT + 1):
            shifted = pltpu.roll(source, k, 1) if k else source
            pressure = pressure + rest_ref[(DRIFT + 1) * c + k : (DRIFT + 1) * c + k + 1] * shifted
    return pressure


def finish_field(field, refs, part_ref, out):
    ids_ref, near_a, near_b, far_ref, same_ref, *cross_refs = refs
    rows = 2 * CHUNK
    steps = out.shape[0] // rows
    last_field = far_ref.shape[0] - 1

    def step(i, carry):
        here = pl.ds(pl.multiple_of(i * rows, rows), rows)
        lefts, rights = {}, {}
        first = REACH * PACKED.index(field)
        for t in range(first // 8, (first + REACH - 1) // 8 + 1):
            cross = cross_refs[0][here] if t == 0 else cross_refs[1][here, 8 * t - 8 : 8 * t]
            one = by_side(ids_ref[0], same_ref[here, 8 * t : 8 * t + 8], [cross])
            lefts[t], rights[t] = one[0][0], one[1][0]
        near = near_a[field // last_field] if field in (0, last_field) else near_b[field - 1]
        cells = with_sides(part_ref[field, here], lefts, rights, field)
        out[here] = with_ends(cells, i, steps, ids_ref[1], near, far_ref[field])
        return carry

    lax.fori_loop(0, steps, step, 0)


def most_kernel(ids_ref, part_ref, *refs):
    *sides, out_hbm, last_ref, done, sem = refs
    copies = []
    for field in range(done.shape[0]):
        finish_field(field, (ids_ref, *sides), part_ref, done.at[field])
        copies.append(pltpu.make_async_copy(done.at[field], out_hbm.at[field], sem.at[field]))
        copies[-1].start()
    finish_field(done.shape[0], (ids_ref, *sides), part_ref, last_ref)
    for copy in copies:
        copy.wait()


def last_kernel(
    cells_ref, _, hit_ref, sums_ref, spot_ref, seg_ref, density_ref, spread_ref,
    out_hbm, drifted_hbm, done, back_ref, moved, sem,
):
    points = spot_ref.shape[1]
    rows, cols, depth = done.shape
    tiles = hit_ref.shape[1]
    last = out_hbm.shape[0] - 1
    back_ref[...] = sum(dot(hit_ref[...], p) for p in parts_of(sums_ref[:tiles], 3))
    copies = []
    size = 2 * CHUNK
    for first in range(0, rows, size):
        here = pl.ds(first, size)
        spread = (back_ref[here][:, None, :] * spot_ref[...][None]).reshape(-1, points)
        returned = exact_dot(spread, seg_ref[...]).reshape(-1, cols, depth)
        cells = cells_ref[here]
        done[here] = cells + nudge_rate * (returned - cells)
        copies.append(pltpu.make_async_copy(done.at[here], out_hbm.at[last, here], sem.at[len(copies)]))
        copies[-1].start()
    density = density_ref[0] + inner_step * (
        spread_ref[1] * sums_ref[tiles : tiles + 1] + spread_ref[2] * sums_ref[tiles + 1 : tiles + 2]
    )
    moved[0] = drifted(density, spread_ref[0])
    copies.append(pltpu.make_async_copy(moved, drifted_hbm, sem.at[len(copies)]))
    copies[-1].start()
    for copy in copies:
        copy.wait()


def message_kernel(ids_ref, sums_ref, other_ref, rest_ref, *outs):
    *outs, total_ref = outs
    total_ref[...] = sums_ref[...] + other_ref[...]
    tiles, size = total_ref.shape
    points = size // 3
    pressure = pressures_of(total_ref[...], rest_ref)
    for i, out in enumerate(outs):
        owner = ids_ref[2] - ids_ref[0] + (ids_ref[0] ^ (2 * i))
        source = total_ref[pl.ds(owner, 1), :]
        out[:tiles] = pressure
        out[tiles:] = jnp.concatenate(
            [source[:, :points], source[:, points : 2 * points], jnp.zeros((6, points), f32)], axis=0
        )


def messages(ids, sums, other, rest, count):
    tiles, size = sums.shape
    return pl.pallas_call(
        message_kernel,
        in_specs=[SMEM] + [VMEM] * 3,
        out_specs=[VMEM] * count,
        out_shape=[in_vmem(tiles + 8, size // 3)] * count,
        scratch_shapes=[pltpu.VMEM(sums.shape, f32)],
        compiler_params=SMALL,
        cost_estimate=cost(1e3, 1e3),
        name="messages",
    )(ids, pinned(sums), pinned(other), pinned(rest))


def pressures_of(sums, rest_ref):
    points = sums.shape[1] // 3
    pressure = sums[:, 2 * points :]
    for c in range(2):
        source = sums[:, c * points : (c + 1) * points]
        for k in range(DRIFT + 1):
            shifted = pltpu.roll(source, k, 1) if k else source
            pressure = pressure + rest_ref[(DRIFT + 1) * c + k : (DRIFT + 1) * c + k + 1] * shifted
    return pressure


def finish_most(ids, part, rad, same, crosses):
    fields, rows, cols, depth = part.shape
    pins = [pinned(x) for x in (part, *rad, same, *crosses)]
    return pl.pallas_call(
        most_kernel,
        in_specs=[SMEM] + [VMEM] * len(pins),
        out_specs=[HBM, VMEM],
        out_shape=[jax.ShapeDtypeStruct(part.shape, f32), in_vmem(rows, cols, depth)],
        scratch_shapes=[pltpu.VMEM((fields - 1, rows, cols, depth), f32), pltpu.SemaphoreType.DMA((fields - 1,))],
        compiler_params=LARGE,
        cost_estimate=cost(1e8, 1.6e7),
        name="finish_most",
    )(ids, *pins)


def finish_last(cells, most, hits, sums, spot, seg, density, spread):
    rows, cols, depth = cells.shape
    return pl.pallas_call(
        last_kernel,
        in_specs=[VMEM, HBM] + [VMEM] * 6,
        out_specs=[HBM, HBM],
        out_shape=[jax.ShapeDtypeStruct(most.shape, f32), jax.ShapeDtypeStruct(density.shape, f32)],
        input_output_aliases={1: 0},
        scratch_shapes=[
            pltpu.VMEM(cells.shape, f32),
            pltpu.VMEM((rows, spot.shape[1]), f32),
            pltpu.VMEM(density.shape, f32),
            pltpu.SemaphoreType.DMA((rows // (2 * CHUNK) + 1,)),
        ],
        compiler_params=SMALL,
        cost_estimate=cost(1e3, 1e3),
        name="finish_last",
    )(pinned(cells), most, hits, pinned(sums), spot, seg, density, pinned(spread))


def swap(x, axis, bit):
    return lax.ppermute(x, axis, [(i, i ^ bit) for i in range(lax.axis_size(axis))])


def per_device(
    state,
    flux_matrices,
    wave_speed,
    flux_volume,
    block_tile,
    tile_of_device,
    phase_density,
    injection,
    drift_courant,
    energy_weight,
):
    fields, rows, cols, depth = state.shape
    n_rad, n_lon = lax.axis_size("rad"), lax.axis_size("lon")
    points = cols * ZSEG
    lon, rad, place = [lax.axis_index(axes).astype(jnp.int32).reshape(1) for axes in ("lon", "rad", ("rad", "lon"))]

    across = [(i, (i + 1 if i % 2 else i - 1) % n_lon) for i in range(n_lon)]
    beyond = [(i, j) for i in range(n_rad) for j in [i + 1 if i % 2 else i - 1] if 0 <= j < n_rad]
    rim, ids, same, *crosses = lon_edges(state, flux_matrices, wave_speed, lon, rad, place)
    cross_0 = lax.ppermute(crosses[0], "lon", across)
    same = swap(same, "lon", 1)
    cross_1 = lax.ppermute(crosses[1], "lon", across)

    near_a, near_b, far = rad_edges(ids, rim, flux_matrices, wave_speed)
    near_a = swap(near_a, "rad", 1)
    far = lax.ppermute(far, "rad", beyond)

    packed = jnp.concatenate([drift_courant[None], energy_weight[None], injection], axis=0)
    packed = jnp.pad(packed, ((0, 4), (0, -packed.shape[1] % 128)))

    part, turned, cells, rest, spread = local_update(state, flux_matrices, wave_speed, phase_density, packed)

    targets = block_tile[0, :, 0]
    hits = (tile_of_device[:, None] == targets[None, :]).astype(bf16)
    hits_back = (targets[:, None] == tile_of_device[None, :]).astype(bf16)
    seg_cells = depth // ZSEG
    seg = np.array([[float(p % ZSEG == z // seg_cells) for p in range(points)] for z in range(depth)], np.float32)
    spot = np.array([[float(p // ZSEG == l) for p in range(points)] for l in range(cols)], np.float32)
    sums = tile_sums(
        ids, part, flux_volume, same, cross_0, near_a, far, rest, hits, jnp.asarray(seg, bf16), jnp.asarray(spot)
    )
    near_b, sums = lax.optimization_barrier((near_b, sums))
    near_b = swap(near_b, "rad", 1)
    part, sums = lax.optimization_barrier((part, sums))
    others = [swap(sums, "rad", step) for step in range(1, n_rad)]
    part = radial_update(tuple(range(1, fields - 1)), cells, turned, part, wave_speed)
    part, sums = lax.optimization_barrier((part, sums))
    sums = sum(others, sums)
    sums, *shares = messages(ids, sums, swap(sums, "lon", 1), rest, n_lon // 2)
    others = [swap(share, "lon", 2 * i + 2) for i, share in enumerate(shares)]
    most, last = finish_most(ids, part, (near_a, near_b, far), same, (cross_0, cross_1))
    sums, most = lax.optimization_barrier((sums, most))
    sums = sum(others, sums)
    done, density = finish_last(
        last, most, hits_back, sums, jnp.asarray(spot), jnp.asarray(seg.T, bf16), phase_density, spread
    )
    return done, density


def solution(mesh):
    in_specs = (
        P(None, "rad", "lon", None),
        P(),
        P(),
        P("rad", "lon", None),
        P("lon", "rad", None),
        P(),
        P(("rad", "lon"), None, None),
        P(),
        P(),
        P(),
    )
    out_specs = (P(None, "rad", "lon", None), P(("rad", "lon"), None, None))
    return jax.shard_map(per_device, mesh=mesh, in_specs=in_specs, out_specs=out_specs, check_vma=False)
```

```python
import functools

import jax
import jax.numpy as jnp
import numpy as np
from jax import lax
from jax.experimental import pallas as pl
from jax.experimental.pallas import tpu as pltpu
from jax.sharding import PartitionSpec as P

ZSEG = 8
DRIFT = 3
REACH = 3

courant_step = 0.4
nudge_rate = 0.5
inner_step = 0.5

SUM_TAPS = {k: v / 60.0 for k, v in zip(range(-3, 4), (-2.0, 18.0, -90.0, 0.0, 90.0, -18.0, 2.0))}
GAP_TAPS = {k: v / 60.0 for k, v in zip(range(-3, 4), (2.0, -12.0, 30.0, -40.0, 30.0, -12.0, 2.0))}

PACKED = (0, 7, 1, 2, 3, 4, 5, 6)

f32 = jnp.float32
bf16 = jnp.bfloat16


def cost(flops, bytes_accessed):
    return pl.CostEstimate(flops=int(flops), bytes_accessed=int(bytes_accessed), transcendentals=0)


def parts_of(x, count):
    parts = []
    for _ in range(count):
        part = x.astype(bf16)
        parts.append(part)
        x = x - part.astype(f32)
    return parts


def dot(a, b):
    return jnp.dot(a, b, preferred_element_type=f32)


def exact_dot(x, ones):
    return sum(dot(part, ones) for part in parts_of(x, 3))


def lon_tables(rows, cols):
    fields = 1 + max(f for f, _ in cols)
    pick_row = np.array([[float(f == a) for a in range(fields)] for f, _ in rows], np.float32)
    pick_col = np.array([[float(f == b) for f, _ in cols] for b in range(fields)], np.float32)
    summed = np.array([[0.0 if s is None else SUM_TAPS.get(s - t, 0.0) for _, s in cols] for _, t in rows], np.float32)
    gapped = np.array(
        [[0.0 if s is None or f != g else GAP_TAPS.get(s - t, 0.0) for g, s in cols] for f, t in rows], np.float32
    )
    return pick_row, pick_col, summed, gapped


def lon_weights(matrix, wave_rate, pick_row, pick_col, summed, gapped):
    half = 0.5 * courant_step
    spread = f32_dot(f32_dot(pick_row, matrix), pick_col)
    return (half * wave_rate) * gapped - half * spread * summed


def f32_dot(a, b):
    return jnp.dot(a, b, precision=lax.Precision.HIGHEST, preferred_element_type=f32)


def whole(array):
    zeros = (0,) * array.ndim
    return pl.BlockSpec(array.shape, lambda *_: zeros)


SMEM = pl.BlockSpec(memory_space=pltpu.SMEM)
VMEM = pl.BlockSpec(memory_space=pltpu.VMEM)
HBM = pl.BlockSpec(memory_space=pltpu.HBM)
LARGE = pltpu.CompilerParams(vmem_limit_bytes=12 * 2**20)
SMALL = pltpu.CompilerParams(vmem_limit_bytes=5 * 2**20)
CHUNK = 8
BLOCK = 16
AHEAD = 3


def in_vmem(*shape):
    return pltpu.VMEM(shape, f32)


def pinned(x):
    return pltpu.with_memory_space_constraint(x, pltpu.VMEM)


def lon_edge_kernel(lon_ref, rad_ref, place_ref, state_hbm, speed_hbm, matrix_hbm, table_hbm, rim, ids_ref, same, *refs):
    *crosses, speed_ref, matrix_ref, table_ref, edges, weights, sem, few_sem = refs
    fields, rows, cols, depth = state_hbm.shape
    chunks = rows // BLOCK
    size = same.shape[1]
    keep = edges.shape[2] // 2

    def loads(c):
        here = pl.ds(c * BLOCK, BLOCK)
        return [
            pltpu.make_async_copy(
                state_hbm.at[:, here, pl.ds(first, keep)], edges.at[:, here, pl.ds(slot, keep)], sem.at[2 * c + i]
            )
            for i, (first, slot) in enumerate(((0, 0), (cols - keep, keep)))
        ]

    few = [(speed_hbm, speed_ref), (matrix_hbm, matrix_ref), (table_hbm, table_ref)]
    few += [(state_hbm.at[:, pl.ds(0, REACH)], rim.at[:, pl.ds(0, REACH)])]
    few += [(state_hbm.at[:, pl.ds(rows - REACH, REACH)], rim.at[:, pl.ds(REACH, REACH)])]
    few = [pltpu.make_async_copy(source, target, few_sem.at[i]) for i, (source, target) in enumerate(few)]
    for copy in few[:3]:
        copy.start()
    for c in range(chunks):
        for copy in loads(c):
            copy.start()
    for copy in few[3:]:
        copy.start()
    ids_ref[0] = lon_ref[0]
    ids_ref[1] = rad_ref[0]
    ids_ref[2] = place_ref[0]
    for copy in few[:3]:
        copy.wait()
    wide = 8 * fields
    w = lon_weights(
        matrix_ref[1], speed_ref[1], table_ref[0, :, :fields], table_ref[1, :fields, :wide], table_ref[2, :, :wide],
        table_ref[3, :, :wide],
    )
    swap = lon_ref[0] % 2 == 1
    w = jnp.concatenate([jnp.where(swap, w[size:], w[:size]), jnp.where(swap, w[:size], w[size:])], axis=0)
    high, low = parts_of(w, 2)
    weights[...] = jnp.concatenate([high, high, low], axis=1)

    def step(c, carry):
        for copy in loads(c):
            copy.wait()
        for j in range(BLOCK):
            r = c * BLOCK + j
            high, low = parts_of(edges[:, r].reshape(-1, depth), 2)
            sums = dot(weights[...], jnp.concatenate([high, low, high], axis=0))
            same[r] = sums[:size]
            first, rest = crosses
            first[r] = sums[size : size + 8]
            rest[r] = sums[size + 8 :]
        return carry

    lax.fori_loop(0, chunks, step, 0)
    for copy in few[3:]:
        copy.wait()


def lon_edges(state, matrices, speed, lon, rad, place):
    fields, rows, cols, depth = state.shape
    keep = 4
    sources = [(f, l if l < keep else cols - 2 * keep + l) for f in range(fields) for l in range(2 * keep)]
    sources = [(f, l if l < REACH or l >= cols - REACH else None) for f, l in sources]
    to_right = [(f, cols + t) for f in PACKED for t in range(REACH)]
    to_left = [(f, t - REACH) for f in PACKED for t in range(REACH)]
    size = fields * REACH
    tables = np.zeros((4, 2 * size, 128), np.float32)
    for i, table in enumerate(lon_tables(to_right + to_left, sources)):
        tables[i, : table.shape[0], : table.shape[1]] = table
    return pl.pallas_call(
        lon_edge_kernel,
        in_specs=[SMEM] * 3 + [HBM] * 4,
        out_specs=[VMEM, SMEM] + [VMEM] * 3,
        out_shape=[
            in_vmem(fields, 2 * REACH, cols, depth),
            jax.ShapeDtypeStruct((3,), jnp.int32),
            in_vmem(rows, size, depth),
            in_vmem(rows, 8, depth),
            in_vmem(rows, size - 8, depth),
        ],
        scratch_shapes=[
            pltpu.SMEM(speed.shape, f32),
            pltpu.VMEM(matrices.shape, f32),
            pltpu.VMEM(tables.shape, f32),
            pltpu.VMEM((fields, rows, 2 * keep, depth), f32),
            pltpu.VMEM((2 * size, 3 * len(sources)), bf16),
            pltpu.SemaphoreType.DMA((2 * rows // BLOCK,)),
            pltpu.SemaphoreType.DMA((5,)),
        ],
        compiler_params=LARGE,
        cost_estimate=cost(1e3, 1e3),
        name="lon_edges",
    )(lon, rad, place, *[pltpu.with_memory_space_constraint(x, pltpu.HBM) for x in (state, speed, matrices, jnp.asarray(tables))])


def turn_weights(matrix, pick, same):
    return (-0.5 * courant_step) * same * f32_dot(f32_dot(pick, matrix), pick.T)


def turn_tables(fields, cols):
    every = [(f, l) for f in range(fields) for l in range(cols)]
    pick = np.array([[float(f == a) for a in range(fields)] for f, _ in every], np.float32)
    same = np.array([[float(l == m) for _, m in every] for _, l in every], np.float32)
    return pick, same


def rad_edge_kernel(ids_ref, speed_ref, rim_ref, matrix_ref, pick_ref, same_ref, near_a, near_b, far_ref):
    fields, _, cols, depth = rim_ref.shape
    rate = (0.5 * courant_step) * speed_ref[0]
    even = ids_ref[1] % 2 == 0
    high, low = parts_of(turn_weights(matrix_ref[0], pick_ref[...], same_ref[...]), 2)
    w = jnp.concatenate([high, high, low], axis=1)

    def turned(cells):
        high, low = parts_of(cells.reshape(-1, depth), 2)
        return dot(w, jnp.concatenate([high, low, high], axis=0)).reshape(fields, cols, depth)

    first = [rim_ref[:, j] for j in range(REACH)]
    last = [rim_ref[:, REACH + j] for j in range(REACH)]
    first_turned = [turned(cells) for cells in first]
    last_turned = [turned(cells) for cells in last]
    for t in range(REACH):
        up = sum(
            SUM_TAPS[j - REACH - t] * last_turned[j] + (rate * GAP_TAPS[j - REACH - t]) * last[j]
            for j in range(t, REACH)
        )
        down = sum(
            SUM_TAPS[j + REACH - t] * first_turned[j] + (rate * GAP_TAPS[j + REACH - t]) * first[j]
            for j in range(t + 1)
        )
        near = jnp.where(even, up, down)
        near_a[0, t] = near[0]
        near_a[1, t] = near[fields - 1]
        near_b[:, t] = near[1 : fields - 1]
        far_ref[:, t] = jnp.where(even, down, up)


def rad_edges(ids, rim, matrices, speed):
    fields, _, cols, depth = rim.shape
    tables = turn_tables(fields, cols)
    return pl.pallas_call(
        rad_edge_kernel,
        in_specs=[SMEM] * 2 + [VMEM] * (2 + len(tables)),
        out_specs=[VMEM] * 3,
        out_shape=[in_vmem(n, REACH, cols, depth) for n in (2, fields - 2, fields)],
        compiler_params=LARGE,
        cost_estimate=cost(1e3, 1e3),
        name="rad_edges",
    )(ids, speed, pinned(rim), matrices, *tables)


def add_radial(speed_ref, cells, turned, total, fields, first):
    cols, depth = total.shape[2:]
    rate = (0.5 * courant_step) * speed_ref[0]
    for f in fields:
        for half in range(cols // 8):
            for lane in range(depth // 128):
                lanes = pl.ds(128 * lane, 128)
                u = [cells[f, first + j, pl.ds(8 * half, 8), lanes] for j in range(CHUNK + 2 * REACH)]
                v = [turned[first + j, pl.ds(f * cols + 8 * half, 8), lanes] for j in range(CHUNK + 2 * REACH)]
                for j in range(CHUNK):
                    at = j + REACH
                    value = total[f, first + j, pl.ds(8 * half, 8), lanes] + (rate * GAP_TAPS[0]) * u[at]
                    for k in range(1, REACH + 1):
                        value = value + SUM_TAPS[k] * (v[at + k] - v[at - k])
                        value = value + (rate * GAP_TAPS[k]) * (u[at + k] + u[at - k])
                    total[f, first + j, pl.ds(8 * half, 8), lanes] = value


def add_radial(speed_ref, cells, turned, total, fields, first):
    cols, depth = total.shape[2:]
    rate = (0.5 * courant_step) * speed_ref[0]
    for f in fields:
        for half in range(cols // 8):
            for lane in range(depth // 128):
                lanes, subs = pl.ds(128 * lane, 128), pl.ds(8 * half, 8)
                u = [cells[f, first + j, subs, lanes] for j in range(CHUNK + 2 * REACH)]
                v = [turned[first + j, pl.ds(f * cols + 8 * half, 8), lanes] for j in range(CHUNK + 2 * REACH)]
                for j in range(CHUNK):
                    at = j + REACH
                    value = total[f, first + j, subs, lanes] + (rate * GAP_TAPS[0]) * u[at]
                    for k in range(1, REACH + 1):
                        value = value + (SUM_TAPS[k] / SUM_TAPS[1]) * (v[at + k] - v[at - k])
                        value = value + (rate * GAP_TAPS[k]) * (u[at + k] + u[at - k])
                    total[f, first + j, subs, lanes] = value


def local_kernel(
    speed_ref, state_hbm, matrix_ref, pick_ref, same_ref, sum_ref, gap_ref, density_ref, packed_ref,
    total, turned, cells, rest_ref, spread_ref, w_ref, sem,
):
    fields, rows, cols, depth = total.shape
    chunks = rows // CHUNK
    size = fields * cols

    def load(c):
        return pltpu.make_async_copy(
            state_hbm.at[:, pl.ds(c * CHUNK, CHUNK)], cells.at[:, pl.ds(REACH + c * CHUNK, CHUNK)], sem.at[c]
        )

    for c in range(AHEAD):
        load(c).start()
    pick = pick_ref[...]
    own = lon_weights(matrix_ref[1], speed_ref[1], pick, pick.T, sum_ref[...], gap_ref[...])
    turn = SUM_TAPS[1] * turn_weights(matrix_ref[0], pick, same_ref[...])
    high, low = parts_of(jnp.concatenate([own, turn], axis=0), 2)
    w_ref[...] = jnp.concatenate([high, high, low], axis=1)
    for edge in (0, REACH + rows):
        cells[:, edge : edge + REACH] = jnp.zeros((fields, REACH, cols, depth), f32)
        turned[edge : edge + REACH] = jnp.zeros((REACH, size, depth), f32)

    keep_rest(density_ref, packed_ref, rest_ref, spread_ref)

    def rows_of(c, carry):
        load(c).wait()

        @pl.when(c + AHEAD < chunks)
        def _():
            load(c + AHEAD).start()

        for j in range(CHUNK):
            r = c * CHUNK + j
            here = cells[:, REACH + r].reshape(size, depth)
            high, low = parts_of(here, 2)
            both = dot(w_ref[...], jnp.concatenate([high, low, high], axis=0))
            total[:, r] = (here + both[:size]).reshape(fields, cols, depth)
            turned[REACH + r] = both[size:]
        return carry

    def radial(c, carry):
        add_radial(speed_ref, cells, turned, total, (0, fields - 1), c * CHUNK)
        return carry

    lax.fori_loop(0, chunks, rows_of, 0)
    lax.fori_loop(0, chunks, radial, 0)


def local_update(state, matrices, speed, density, packed):
    fields, rows, cols, depth = state.shape
    size = fields * cols
    every = [(f, l) for f in range(fields) for l in range(cols)]
    _, _, summed, gapped = lon_tables(every, every)
    padded = rows + 2 * REACH
    return pl.pallas_call(
        local_kernel,
        in_specs=[SMEM, HBM] + [VMEM] * 7,
        out_specs=[VMEM] * 5,
        out_shape=[
            in_vmem(*state.shape),
            in_vmem(padded, size, depth),
            in_vmem(fields, padded, cols, depth),
            in_vmem(16, density.shape[2]),
            in_vmem(3, *density.shape[1:]),
        ],
        scratch_shapes=[pltpu.VMEM((2 * size, 3 * size), bf16), pltpu.SemaphoreType.DMA((rows // CHUNK,))],
        compiler_params=SMALL,
        cost_estimate=cost(1e3, 1e3),
        name="local_update",
    )(
        speed, pltpu.with_memory_space_constraint(state, pltpu.HBM), matrices, *turn_tables(fields, cols), summed, gapped,
        density, packed,
    )


def radial_kernel(fields, speed_ref, ids_ref, cells, turned, near_a, far_ref, same_ref, cross_ref, _, total, out_hbm, done, sem):
    finish_field(0, (ids_ref, near_a, None, far_ref, same_ref, cross_ref), total, done)
    store = pltpu.make_async_copy(done, out_hbm.at[0], sem)
    store.start()

    def radial(c, carry):
        add_radial(speed_ref, cells, turned, total, fields, c * CHUNK)
        return carry

    lax.fori_loop(0, total.shape[1] // CHUNK, radial, 0)
    store.wait()


def radial_update(fields, ids, cells, turned, part, speed, near_a, far, same, cross_0):
    pins = [pinned(x) for x in (cells, turned, near_a, far, same, cross_0, part)]
    return pl.pallas_call(
        functools.partial(radial_kernel, fields),
        in_specs=[SMEM] * 2 + [VMEM] * len(pins),
        out_specs=[VMEM, HBM],
        out_shape=[in_vmem(*part.shape), jax.ShapeDtypeStruct(part.shape, f32)],
        input_output_aliases={1 + len(pins): 0},
        scratch_shapes=[pltpu.VMEM(part.shape[1:], f32), pltpu.SemaphoreType.DMA],
        compiler_params=SMALL,
        cost_estimate=cost(1e8, 6e6),
        name="radial_update",
    )(speed, ids, *pins)


def placed(tiles, field, from_left):
    start = REACH * PACKED.index(field)
    tile, offset = start // 8, start % 8
    cells = tiles[tile]
    sub = lax.broadcasted_iota(jnp.int32, cells.shape, 1)
    if offset + REACH > 8:
        cells = jnp.where(sub >= offset, cells, tiles[tile + 1])
    goal = 0 if from_left else 8 - REACH
    shift = (goal - offset) % 8
    if shift:
        cells = pltpu.roll(cells, shift, 1)
    keep = sub < REACH if from_left else sub >= 8 - REACH
    return jnp.where(keep, cells, 0.0)


def by_side(lon, same, crosses):
    even = lon % 2 == 0
    lefts, rights = {}, {}
    for t, cross in enumerate(crosses):
        near = same[:, 8 * t : 8 * t + 8]
        lefts[t] = jnp.where(even, cross, near)
        rights[t] = jnp.where(even, near, cross)
    return lefts, rights


def with_sides(cells, lefts, rights, field):
    cols = cells.shape[1]
    return jnp.concatenate(
        [cells[:, :8] + placed(lefts, field, True), cells[:, cols - 8 :] + placed(rights, field, False)], axis=1
    )


def with_ends(cells, step, steps, rad, near, far):
    rows = cells.shape[0]
    even = rad % 2 == 0
    below, above = jnp.where(even, far, near), jnp.where(even, near, far)
    at_low = (step == 0).astype(f32)
    at_top = (step == steps - 1).astype(f32)
    return jnp.concatenate(
        [cells[:REACH] + at_low * below, cells[REACH : rows - REACH], cells[rows - REACH :] + at_top * above], axis=0
    )


def tile_sum_kernel(
    ids_ref, part_ref, vol_ref, same_ref, cross_ref, near_ref, far_ref, rest_ref, hit_ref, seg_ref, spot_ref,
    out_ref, lines_ref,
):
    all_rows, cols, depth = vol_ref.shape
    tiles, points = out_ref.shape[0], out_ref.shape[1] // 3
    rows = 16
    steps = all_rows // rows

    def add(step, carry):
        here = pl.ds(pl.multiple_of(step * rows, rows), rows)
        lefts, rights = by_side(ids_ref[0], same_ref[here, :8], [cross_ref[here]])
        vol = vol_ref[here]
        for c, field in enumerate((0, 7)):
            cells = with_sides(part_ref[field, here], lefts, rights, field)
            cells = with_ends(cells, step, steps, ids_ref[1], near_ref[c], far_ref[field])
            lines = exact_dot((cells * vol).reshape(rows * cols, depth), seg_ref[...])
            lines_ref[c, here] = jnp.sum(lines.reshape(rows, cols, -1) * spot_ref[...][None], axis=1)
        return carry

    lax.fori_loop(0, steps, add, 0)
    for c in range(2):
        sums = sum(dot(hit_ref[...], part) for part in parts_of(lines_ref[c], 3))
        out_ref[:, c * points : (c + 1) * points] = sums
    mine = lax.broadcasted_iota(jnp.int32, (tiles, points), 0) == ids_ref[2]
    out_ref[:, 2 * points :] = jnp.where(mine, rest_ref[8:9], 0.0)


def tile_sums(ids, part, vol, same, cross, near, far, rest, hits, seg, spot):
    _, rows, _, _ = part.shape
    points = seg.shape[1]
    tiles = hits.shape[0]
    return pl.pallas_call(
        tile_sum_kernel,
        in_specs=[SMEM] + [VMEM] * 10,
        out_specs=VMEM,
        out_shape=in_vmem(tiles, 3 * points),
        scratch_shapes=[pltpu.VMEM((2, rows, points), f32)],
        compiler_params=LARGE,
        cost_estimate=cost(1e3, 1e3),
        name="tile_sums",
    )(ids, *[pinned(x) for x in (part, vol, same, cross, near, far, rest)], hits, seg, spot)


def drifted(density, courant):
    for _ in range(DRIFT):
        density = density - courant * (density - pltpu.roll(density, 1, 1))
    return density


def columns_of(packed_ref, channels):
    turned = jnp.transpose(packed_ref[...])
    return [turned[:channels, i : i + 1] for i in range(4)]


def keep_rest(density_ref, packed_ref, out_ref, spread_ref):
    _, channels, points = density_ref.shape
    courant, weight, first, second = columns_of(packed_ref, channels)
    rows = []
    for given in (first, second):
        for k, choices in enumerate((1.0, 3.0, 3.0, 1.0)):
            gain = (inner_step * choices) * weight * given
            for _ in range(k):
                gain = gain * courant
            for _ in range(DRIFT - k):
                gain = gain * (1.0 - courant)
            rows.append(jnp.broadcast_to(jnp.sum(gain, axis=0, keepdims=True), (1, points)))
    rest = jnp.sum(weight * drifted(density_ref[0], courant), axis=0, keepdims=True)
    out_ref[...] = jnp.concatenate(rows + [rest] * 8, axis=0)
    for i, column in enumerate((courant, first, second)):
        spread_ref[i] = jnp.broadcast_to(column, (channels, points))


def message_kernel(ids_ref, sums_ref, other_ref, rest_ref, *outs):
    *outs, total_ref = outs
    total_ref[...] = sums_ref[...] + other_ref[...]
    tiles, size = total_ref.shape
    points = size // 3
    pressure = pressures_of(total_ref[...], rest_ref)
    for i, out in enumerate(outs):
        owner = ids_ref[2] - ids_ref[0] + (ids_ref[0] ^ (2 * i))
        source = total_ref[pl.ds(owner, 1), :]
        out[:tiles] = pressure
        out[tiles:] = jnp.concatenate(
            [source[:, :points], source[:, points : 2 * points], jnp.zeros((6, points), f32)], axis=0
        )


def messages(ids, sums, other, rest, count):
    tiles, size = sums.shape
    return pl.pallas_call(
        message_kernel,
        in_specs=[SMEM] + [VMEM] * 3,
        out_specs=[VMEM] * count,
        out_shape=[in_vmem(tiles + 8, size // 3)] * count,
        scratch_shapes=[pltpu.VMEM(sums.shape, f32)],
        compiler_params=SMALL,
        cost_estimate=cost(1e3, 1e3),
        name="messages",
    )(ids, pinned(sums), pinned(other), pinned(rest))


def pressures_of(sums, rest_ref):
    points = sums.shape[1] // 3
    pressure = sums[:, 2 * points :]
    for c in range(2):
        source = sums[:, c * points : (c + 1) * points]
        for k in range(DRIFT + 1):
            shifted = pltpu.roll(source, k, 1) if k else source
            pressure = pressure + rest_ref[(DRIFT + 1) * c + k : (DRIFT + 1) * c + k + 1] * shifted
    return pressure


def finish_field(field, refs, part_ref, out, scale=None):
    ids_ref, near_a, near_b, far_ref, same_ref, *cross_refs = refs
    rows = 2 * CHUNK
    steps = out.shape[0] // rows
    last_field = far_ref.shape[0] - 1

    def step(i, carry):
        here = pl.ds(pl.multiple_of(i * rows, rows), rows)
        lefts, rights = {}, {}
        first = REACH * PACKED.index(field)
        for t in range(first // 8, (first + REACH - 1) // 8 + 1):
            cross = cross_refs[0][here] if t == 0 else cross_refs[1][here, 8 * t - 8 : 8 * t]
            one = by_side(ids_ref[0], same_ref[here, 8 * t : 8 * t + 8], [cross])
            lefts[t], rights[t] = one[0][0], one[1][0]
        near = near_a[field // last_field] if field in (0, last_field) else near_b[field - 1]
        cells = with_sides(part_ref[field, here], lefts, rights, field)
        cells = with_ends(cells, i, steps, ids_ref[1], near, far_ref[field])
        out[here] = cells if scale is None else scale * cells
        return carry

    lax.fori_loop(0, steps, step, 0)


def most_kernel(ids_ref, part_ref, *refs):
    *sides, _, out_hbm, last_ref, done, sem = refs
    copies = []
    for i in range(done.shape[0]):
        finish_field(i + 1, (ids_ref, *sides), part_ref, done.at[i])
        copies.append(pltpu.make_async_copy(done.at[i], out_hbm.at[i + 1], sem.at[i]))
        copies[-1].start()
    finish_field(done.shape[0] + 1, (ids_ref, *sides), part_ref, last_ref, 1.0 - nudge_rate)
    for copy in copies:
        copy.wait()


def last_kernel(
    cells_ref, _, hit_ref, sums_ref, spot_ref, seg_ref, density_ref, spread_ref,
    out_hbm, drifted_hbm, done, back_ref, moved, sem,
):
    points = spot_ref.shape[1]
    rows, cols, depth = done.shape
    tiles = hit_ref.shape[1]
    last = out_hbm.shape[0] - 1
    back = sum(dot(hit_ref[...], p) for p in parts_of(sums_ref[:tiles], 3))
    for i, part in enumerate(parts_of(nudge_rate * back, 3)):
        back_ref[i] = part.astype(f32)
    copies = []
    size = 2 * CHUNK
    for first in range(0, rows, size):
        here = pl.ds(first, size)
        spread = [(back_ref[i, here][:, None, :] * spot_ref[...][None]).reshape(-1, points) for i in range(3)]
        returned = dot(jnp.concatenate(spread, axis=1).astype(bf16), seg_ref[...])
        done[here] = cells_ref[here] + returned.reshape(-1, cols, depth)
        copies.append(pltpu.make_async_copy(done.at[here], out_hbm.at[last, here], sem.at[len(copies)]))
        copies[-1].start()
    density = density_ref[0] + inner_step * (
        spread_ref[1] * sums_ref[tiles : tiles + 1] + spread_ref[2] * sums_ref[tiles + 1 : tiles + 2]
    )
    moved[0] = drifted(density, spread_ref[0])
    copies.append(pltpu.make_async_copy(moved, drifted_hbm, sem.at[len(copies)]))
    copies[-1].start()
    for copy in copies:
        copy.wait()


def message_kernel(ids_ref, sums_ref, other_ref, rest_ref, *outs):
    *outs, total_ref = outs
    total_ref[...] = sums_ref[...] + other_ref[...]
    tiles, size = total_ref.shape
    points = size // 3
    pressure = pressures_of(total_ref[...], rest_ref)
    for i, out in enumerate(outs):
        owner = ids_ref[2] - ids_ref[0] + (ids_ref[0] ^ (2 * i))
        source = total_ref[pl.ds(owner, 1), :]
        out[:tiles] = pressure
        out[tiles:] = jnp.concatenate(
            [source[:, :points], source[:, points : 2 * points], jnp.zeros((6, points), f32)], axis=0
        )


def messages(ids, sums, other, rest, count):
    tiles, size = sums.shape
    return pl.pallas_call(
        message_kernel,
        in_specs=[SMEM] + [VMEM] * 3,
        out_specs=[VMEM] * count,
        out_shape=[in_vmem(tiles + 8, size // 3)] * count,
        scratch_shapes=[pltpu.VMEM(sums.shape, f32)],
        compiler_params=SMALL,
        cost_estimate=cost(1e3, 1e3),
        name="messages",
    )(ids, pinned(sums), pinned(other), pinned(rest))


def pressures_of(sums, rest_ref):
    points = sums.shape[1] // 3
    pressure = sums[:, 2 * points :]
    for c in range(2):
        source = sums[:, c * points : (c + 1) * points]
        for k in range(DRIFT + 1):
            shifted = pltpu.roll(source, k, 1) if k else source
            pressure = pressure + rest_ref[(DRIFT + 1) * c + k : (DRIFT + 1) * c + k + 1] * shifted
    return pressure


def finish_most(ids, part, rad, same, crosses, result):
    fields, rows, cols, depth = part.shape
    pins = [pinned(x) for x in (part, *rad, same, *crosses)]
    return pl.pallas_call(
        most_kernel,
        in_specs=[SMEM] + [VMEM] * len(pins) + [HBM],
        out_specs=[HBM, VMEM],
        out_shape=[jax.ShapeDtypeStruct(part.shape, f32), in_vmem(rows, cols, depth)],
        input_output_aliases={1 + len(pins): 0},
        scratch_shapes=[pltpu.VMEM((fields - 2, rows, cols, depth), f32), pltpu.SemaphoreType.DMA((fields - 2,))],
        compiler_params=LARGE,
        cost_estimate=cost(1e8, 1.6e7),
        name="finish_most",
    )(ids, *pins, result)


def finish_last(cells, most, hits, sums, spot, seg, density, spread):
    rows, cols, depth = cells.shape
    return pl.pallas_call(
        last_kernel,
        in_specs=[VMEM, HBM] + [VMEM] * 6,
        out_specs=[HBM, HBM],
        out_shape=[jax.ShapeDtypeStruct(most.shape, f32), jax.ShapeDtypeStruct(density.shape, f32)],
        input_output_aliases={1: 0},
        scratch_shapes=[
            pltpu.VMEM(cells.shape, f32),
            pltpu.VMEM((3, rows, spot.shape[1]), f32),
            pltpu.VMEM(density.shape, f32),
            pltpu.SemaphoreType.DMA((rows // (2 * CHUNK) + 1,)),
        ],
        compiler_params=SMALL,
        cost_estimate=cost(1e3, 1e3),
        name="finish_last",
    )(pinned(cells), most, hits, pinned(sums), spot, seg, density, pinned(spread))


def swap(x, axis, bit):
    return lax.ppermute(x, axis, [(i, i ^ bit) for i in range(lax.axis_size(axis))])


def per_device(
    state,
    flux_matrices,
    wave_speed,
    flux_volume,
    block_tile,
    tile_of_device,
    phase_density,
    injection,
    drift_courant,
    energy_weight,
):
    fields, rows, cols, depth = state.shape
    n_rad, n_lon = lax.axis_size("rad"), lax.axis_size("lon")
    points = cols * ZSEG
    lon, rad, place = [lax.axis_index(axes).astype(jnp.int32).reshape(1) for axes in ("lon", "rad", ("rad", "lon"))]

    across = [(i, (i + 1 if i % 2 else i - 1) % n_lon) for i in range(n_lon)]
    beyond = [(i, j) for i in range(n_rad) for j in [i + 1 if i % 2 else i - 1] if 0 <= j < n_rad]
    rim, ids, same, *crosses = lon_edges(state, flux_matrices, wave_speed, lon, rad, place)
    cross_0 = lax.ppermute(crosses[0], "lon", across)
    same = swap(same, "lon", 1)
    cross_1 = lax.ppermute(crosses[1], "lon", across)

    near_a, near_b, far = rad_edges(ids, rim, flux_matrices, wave_speed)
    near_a = swap(near_a, "rad", 1)
    far = lax.ppermute(far, "rad", beyond)

    packed = jnp.concatenate([drift_courant[None], energy_weight[None], injection], axis=0)
    packed = jnp.pad(packed, ((0, 4), (0, -packed.shape[1] % 128)))

    part, turned, cells, rest, spread = local_update(state, flux_matrices, wave_speed, phase_density, packed)

    targets = block_tile[0, :, 0]
    hits = (tile_of_device[:, None] == targets[None, :]).astype(bf16)
    hits_back = (targets[:, None] == tile_of_device[None, :]).astype(bf16)
    seg_cells = depth // ZSEG
    seg = np.array([[float(p % ZSEG == z // seg_cells) for p in range(points)] for z in range(depth)], np.float32)
    spot = np.array([[float(p // ZSEG == l) for p in range(points)] for l in range(cols)], np.float32)
    sums = tile_sums(
        ids, part, flux_volume, same, cross_0, near_a, far, rest, hits, jnp.asarray(seg, bf16), jnp.asarray(spot)
    )
    near_b, sums = lax.optimization_barrier((near_b, sums))
    near_b = swap(near_b, "rad", 1)
    part, sums = lax.optimization_barrier((part, sums))
    others = [swap(sums, "rad", step) for step in range(1, n_rad)]
    part, result = radial_update(
        tuple(range(1, fields - 1)), ids, cells, turned, part, wave_speed, near_a, far, same, cross_0
    )
    part, sums = lax.optimization_barrier((part, sums))
    sums = sum(others, sums)
    sums, *shares = messages(ids, sums, swap(sums, "lon", 1), rest, n_lon // 2)
    others = [swap(share, "lon", 2 * i + 2) for i, share in enumerate(shares)]
    most, last = finish_most(ids, part, (near_a, near_b, far), same, (cross_0, cross_1), result)
    sums, most = lax.optimization_barrier((sums, most))
    sums = sum(others, sums)
    done, density = finish_last(
        last, most, hits_back, sums, jnp.asarray(spot), jnp.asarray(np.tile(seg.T, (3, 1)), bf16), phase_density, spread
    )
    return done, density


def solution(mesh):
    in_specs = (
        P(None, "rad", "lon", None),
        P(),
        P(),
        P("rad", "lon", None),
        P("lon", "rad", None),
        P(),
        P(("rad", "lon"), None, None),
        P(),
        P(),
        P(),
    )
    out_specs = (P(None, "rad", "lon", None), P(("rad", "lon"), None, None))
    return jax.shard_map(per_device, mesh=mesh, in_specs=in_specs, out_specs=out_specs, check_vma=False)
```

```python
import functools

import jax
import jax.numpy as jnp
import numpy as np
from jax import lax
from jax.experimental import pallas as pl
from jax.experimental.pallas import tpu as pltpu
from jax.sharding import PartitionSpec as P

ZSEG = 8
DRIFT = 3
REACH = 3

courant_step = 0.4
nudge_rate = 0.5
inner_step = 0.5

SUM_TAPS = {k: v / 60.0 for k, v in zip(range(-3, 4), (-2.0, 18.0, -90.0, 0.0, 90.0, -18.0, 2.0))}
GAP_TAPS = {k: v / 60.0 for k, v in zip(range(-3, 4), (2.0, -12.0, 30.0, -40.0, 30.0, -12.0, 2.0))}

PACKED = (0, 7, 1, 2, 3, 4, 5, 6)

f32 = jnp.float32
bf16 = jnp.bfloat16


def cost(flops, bytes_accessed):
    return pl.CostEstimate(flops=int(flops), bytes_accessed=int(bytes_accessed), transcendentals=0)


def parts_of(x, count):
    parts = []
    for _ in range(count):
        part = x.astype(bf16)
        parts.append(part)
        x = x - part.astype(f32)
    return parts


def dot(a, b):
    return jnp.dot(a, b, preferred_element_type=f32)


def exact_dot(x, ones):
    return sum(dot(part, ones) for part in parts_of(x, 3))


def lon_tables(rows, cols):
    fields = 1 + max(f for f, _ in cols)
    pick_row = np.array([[float(f == a) for a in range(fields)] for f, _ in rows], np.float32)
    pick_col = np.array([[float(f == b) for f, _ in cols] for b in range(fields)], np.float32)
    summed = np.array([[0.0 if s is None else SUM_TAPS.get(s - t, 0.0) for _, s in cols] for _, t in rows], np.float32)
    gapped = np.array(
        [[0.0 if s is None or f != g else GAP_TAPS.get(s - t, 0.0) for g, s in cols] for f, t in rows], np.float32
    )
    return pick_row, pick_col, summed, gapped


def lon_weights(matrix, wave_rate, pick_row, pick_col, summed, gapped):
    half = 0.5 * courant_step
    spread = f32_dot(f32_dot(pick_row, matrix), pick_col)
    return (half * wave_rate) * gapped - half * spread * summed


def f32_dot(a, b):
    return jnp.dot(a, b, precision=lax.Precision.HIGHEST, preferred_element_type=f32)


def whole(array):
    zeros = (0,) * array.ndim
    return pl.BlockSpec(array.shape, lambda *_: zeros)


SMEM = pl.BlockSpec(memory_space=pltpu.SMEM)
VMEM = pl.BlockSpec(memory_space=pltpu.VMEM)
HBM = pl.BlockSpec(memory_space=pltpu.HBM)
LARGE = pltpu.CompilerParams(vmem_limit_bytes=12 * 2**20)
SMALL = pltpu.CompilerParams(vmem_limit_bytes=5 * 2**20)
CHUNK = 8
BLOCK = 16
AHEAD = 3


def in_vmem(*shape):
    return pltpu.VMEM(shape, f32)


def pinned(x):
    return pltpu.with_memory_space_constraint(x, pltpu.VMEM)


def lon_edge_kernel(lon_ref, rad_ref, place_ref, state_hbm, speed_hbm, matrix_hbm, table_hbm, rim, ids_ref, same, *refs):
    *crosses, speed_ref, matrix_ref, table_ref, edges, weights, sem, few_sem = refs
    fields, rows, cols, depth = state_hbm.shape
    chunks = rows // BLOCK
    size = same.shape[1]
    keep = edges.shape[2] // 2

    def loads(c):
        here = pl.ds(c * BLOCK, BLOCK)
        return [
            pltpu.make_async_copy(
                state_hbm.at[:, here, pl.ds(first, keep)], edges.at[:, here, pl.ds(slot, keep)], sem.at[2 * c + i]
            )
            for i, (first, slot) in enumerate(((0, 0), (cols - keep, keep)))
        ]

    few = [(speed_hbm, speed_ref), (matrix_hbm, matrix_ref), (table_hbm, table_ref)]
    few += [(state_hbm.at[:, pl.ds(0, REACH)], rim.at[:, pl.ds(0, REACH)])]
    few += [(state_hbm.at[:, pl.ds(rows - REACH, REACH)], rim.at[:, pl.ds(REACH, REACH)])]
    few = [pltpu.make_async_copy(source, target, few_sem.at[i]) for i, (source, target) in enumerate(few)]
    for copy in few[:3]:
        copy.start()
    for c in range(chunks):
        for copy in loads(c):
            copy.start()
    for copy in few[3:]:
        copy.start()
    ids_ref[0] = lon_ref[0]
    ids_ref[1] = rad_ref[0]
    ids_ref[2] = place_ref[0]
    for copy in few[:3]:
        copy.wait()
    wide = 8 * fields
    w = lon_weights(
        matrix_ref[1], speed_ref[1], table_ref[0, :, :fields], table_ref[1, :fields, :wide], table_ref[2, :, :wide],
        table_ref[3, :, :wide],
    )
    swap = lon_ref[0] % 2 == 1
    w = jnp.concatenate([jnp.where(swap, w[size:], w[:size]), jnp.where(swap, w[:size], w[size:])], axis=0)
    high, low = parts_of(w, 2)
    weights[...] = jnp.concatenate([high, high, low], axis=1)

    def step(c, carry):
        for copy in loads(c):
            copy.wait()
        for j in range(BLOCK):
            r = c * BLOCK + j
            high, low = parts_of(edges[:, r].reshape(-1, depth), 2)
            sums = dot(weights[...], jnp.concatenate([high, low, high], axis=0))
            same[r] = sums[:size]
            first, rest = crosses
            first[r] = sums[size : size + 8]
            rest[r] = sums[size + 8 :]
        return carry

    lax.fori_loop(0, chunks, step, 0)
    for copy in few[3:]:
        copy.wait()


def lon_edges(state, matrices, speed, lon, rad, place):
    fields, rows, cols, depth = state.shape
    keep = 4
    sources = [(f, l if l < keep else cols - 2 * keep + l) for f in range(fields) for l in range(2 * keep)]
    sources = [(f, l if l < REACH or l >= cols - REACH else None) for f, l in sources]
    to_right = [(f, cols + t) for f in PACKED for t in range(REACH)]
    to_left = [(f, t - REACH) for f in PACKED for t in range(REACH)]
    size = fields * REACH
    tables = np.zeros((4, 2 * size, 128), np.float32)
    for i, table in enumerate(lon_tables(to_right + to_left, sources)):
        tables[i, : table.shape[0], : table.shape[1]] = table
    return pl.pallas_call(
        lon_edge_kernel,
        in_specs=[SMEM] * 3 + [HBM] * 4,
        out_specs=[VMEM, SMEM] + [VMEM] * 3,
        out_shape=[
            in_vmem(fields, 2 * REACH, cols, depth),
            jax.ShapeDtypeStruct((3,), jnp.int32),
            in_vmem(rows, size, depth),
            in_vmem(rows, 8, depth),
            in_vmem(rows, size - 8, depth),
        ],
        scratch_shapes=[
            pltpu.SMEM(speed.shape, f32),
            pltpu.VMEM(matrices.shape, f32),
            pltpu.VMEM(tables.shape, f32),
            pltpu.VMEM((fields, rows, 2 * keep, depth), f32),
            pltpu.VMEM((2 * size, 3 * len(sources)), bf16),
            pltpu.SemaphoreType.DMA((2 * rows // BLOCK,)),
            pltpu.SemaphoreType.DMA((5,)),
        ],
        compiler_params=LARGE,
        cost_estimate=cost(1e3, 1e3),
        name="lon_edges",
    )(lon, rad, place, *[pltpu.with_memory_space_constraint(x, pltpu.HBM) for x in (state, speed, matrices, jnp.asarray(tables))])


def turn_weights(matrix, pick, same):
    return (-0.5 * courant_step) * same * f32_dot(f32_dot(pick, matrix), pick.T)


def turn_tables(fields, cols):
    every = [(f, l) for f in range(fields) for l in range(cols)]
    pick = np.array([[float(f == a) for a in range(fields)] for f, _ in every], np.float32)
    same = np.array([[float(l == m) for _, m in every] for _, l in every], np.float32)
    return pick, same


def rad_edge_kernel(ids_ref, speed_ref, rim_ref, matrix_ref, pick_ref, same_ref, near_a, near_b, far_ref):
    fields, _, cols, depth = rim_ref.shape
    rate = (0.5 * courant_step) * speed_ref[0]
    even = ids_ref[1] % 2 == 0
    high, low = parts_of(turn_weights(matrix_ref[0], pick_ref[...], same_ref[...]), 2)
    w = jnp.concatenate([high, high, low], axis=1)

    def turned(cells):
        high, low = parts_of(cells.reshape(-1, depth), 2)
        return dot(w, jnp.concatenate([high, low, high], axis=0)).reshape(fields, cols, depth)

    first = [rim_ref[:, j] for j in range(REACH)]
    last = [rim_ref[:, REACH + j] for j in range(REACH)]
    first_turned = [turned(cells) for cells in first]
    last_turned = [turned(cells) for cells in last]
    for t in range(REACH):
        up = sum(
            SUM_TAPS[j - REACH - t] * last_turned[j] + (rate * GAP_TAPS[j - REACH - t]) * last[j]
            for j in range(t, REACH)
        )
        down = sum(
            SUM_TAPS[j + REACH - t] * first_turned[j] + (rate * GAP_TAPS[j + REACH - t]) * first[j]
            for j in range(t + 1)
        )
        near = jnp.where(even, up, down)
        near_a[0, t] = near[0]
        near_a[1, t] = near[fields - 1]
        near_b[:, t] = near[1 : fields - 1]
        far_ref[:, t] = jnp.where(even, down, up)


def rad_edges(ids, rim, matrices, speed):
    fields, _, cols, depth = rim.shape
    tables = turn_tables(fields, cols)
    return pl.pallas_call(
        rad_edge_kernel,
        in_specs=[SMEM] * 2 + [VMEM] * (2 + len(tables)),
        out_specs=[VMEM] * 3,
        out_shape=[in_vmem(n, REACH, cols, depth) for n in (2, fields - 2, fields)],
        compiler_params=LARGE,
        cost_estimate=cost(1e3, 1e3),
        name="rad_edges",
    )(ids, speed, pinned(rim), matrices, *tables)


def add_radial(speed_ref, cells, turned, total, fields, first):
    cols, depth = total.shape[2:]
    rate = (0.5 * courant_step) * speed_ref[0]
    for f in fields:
        for half in range(cols // 8):
            for lane in range(depth // 128):
                lanes = pl.ds(128 * lane, 128)
                u = [cells[f, first + j, pl.ds(8 * half, 8), lanes] for j in range(CHUNK + 2 * REACH)]
                v = [turned[first + j, pl.ds(f * cols + 8 * half, 8), lanes] for j in range(CHUNK + 2 * REACH)]
                for j in range(CHUNK):
                    at = j + REACH
                    value = total[f, first + j, pl.ds(8 * half, 8), lanes] + (rate * GAP_TAPS[0]) * u[at]
                    for k in range(1, REACH + 1):
                        value = value + SUM_TAPS[k] * (v[at + k] - v[at - k])
                        value = value + (rate * GAP_TAPS[k]) * (u[at + k] + u[at - k])
                    total[f, first + j, pl.ds(8 * half, 8), lanes] = value


def add_radial(speed_ref, cells, turned, total, fields, first):
    cols, depth = total.shape[2:]
    rate = (0.5 * courant_step) * speed_ref[0]
    for f in fields:
        for half in range(cols // 8):
            for lane in range(depth // 128):
                lanes, subs = pl.ds(128 * lane, 128), pl.ds(8 * half, 8)
                u = [cells[f, first + j, subs, lanes] for j in range(CHUNK + 2 * REACH)]
                v = [turned[first + j, pl.ds(f * cols + 8 * half, 8), lanes] for j in range(CHUNK + 2 * REACH)]
                for j in range(CHUNK):
                    at = j + REACH
                    value = total[f, first + j, subs, lanes] + (rate * GAP_TAPS[0]) * u[at]
                    for k in range(1, REACH + 1):
                        value = value + (SUM_TAPS[k] / SUM_TAPS[1]) * (v[at + k] - v[at - k])
                        value = value + (rate * GAP_TAPS[k]) * (u[at + k] + u[at - k])
                    total[f, first + j, subs, lanes] = value


def local_kernel(
    speed_ref, state_hbm, matrix_ref, pick_ref, same_ref, sum_ref, gap_ref, density_ref, packed_ref,
    total, turned, cells, rest_ref, spread_ref, w_ref, sem,
):
    fields, rows, cols, depth = total.shape
    chunks = rows // CHUNK
    size = fields * cols

    def load(c):
        return pltpu.make_async_copy(
            state_hbm.at[:, pl.ds(c * CHUNK, CHUNK)], cells.at[:, pl.ds(REACH + c * CHUNK, CHUNK)], sem.at[c]
        )

    for c in range(AHEAD):
        load(c).start()
    pick = pick_ref[...]
    own = lon_weights(matrix_ref[1], speed_ref[1], pick, pick.T, sum_ref[...], gap_ref[...])
    turn = SUM_TAPS[1] * turn_weights(matrix_ref[0], pick, same_ref[...])
    high, low = parts_of(jnp.concatenate([own, turn], axis=0), 2)
    w_ref[...] = jnp.concatenate([high, high, low], axis=1)
    for edge in (0, REACH + rows):
        cells[:, edge : edge + REACH] = jnp.zeros((fields, REACH, cols, depth), f32)
        turned[edge : edge + REACH] = jnp.zeros((REACH, size, depth), f32)

    keep_rest(density_ref, packed_ref, rest_ref, spread_ref)

    def rows_of(c, carry):
        load(c).wait()

        @pl.when(c + AHEAD < chunks)
        def _():
            load(c + AHEAD).start()

        for j in range(CHUNK):
            r = c * CHUNK + j
            here = cells[:, REACH + r].reshape(size, depth)
            high, low = parts_of(here, 2)
            both = dot(w_ref[...], jnp.concatenate([high, low, high], axis=0))
            total[:, r] = (here + both[:size]).reshape(fields, cols, depth)
            turned[REACH + r] = both[size:]
        return carry

    def radial(c, carry):
        add_radial(speed_ref, cells, turned, total, (0, fields - 1), c * CHUNK)
        return carry

    lax.fori_loop(0, chunks, rows_of, 0)
    lax.fori_loop(0, chunks, radial, 0)


def local_update(state, matrices, speed, density, packed):
    fields, rows, cols, depth = state.shape
    size = fields * cols
    every = [(f, l) for f in range(fields) for l in range(cols)]
    _, _, summed, gapped = lon_tables(every, every)
    padded = rows + 2 * REACH
    return pl.pallas_call(
        local_kernel,
        in_specs=[SMEM, HBM] + [VMEM] * 7,
        out_specs=[VMEM] * 5,
        out_shape=[
            in_vmem(*state.shape),
            in_vmem(padded, size, depth),
            in_vmem(fields, padded, cols, depth),
            in_vmem(16, density.shape[2]),
            in_vmem(3, *density.shape[1:]),
        ],
        scratch_shapes=[pltpu.VMEM((2 * size, 3 * size), bf16), pltpu.SemaphoreType.DMA((rows // CHUNK,))],
        compiler_params=SMALL,
        cost_estimate=cost(1e3, 1e3),
        name="local_update",
    )(
        speed, pltpu.with_memory_space_constraint(state, pltpu.HBM), matrices, *turn_tables(fields, cols), summed, gapped,
        density, packed,
    )


def radial_kernel(fields, speed_ref, ids_ref, cells, turned, near_a, far_ref, same_ref, cross_ref, _, total, out_hbm, done, sem):
    finish_field(0, (ids_ref, near_a, None, far_ref, same_ref, cross_ref), total, done)
    store = pltpu.make_async_copy(done, out_hbm.at[0], sem)
    store.start()

    def radial(c, carry):
        add_radial(speed_ref, cells, turned, total, fields, c * CHUNK)
        return carry

    lax.fori_loop(0, total.shape[1] // CHUNK, radial, 0)
    store.wait()


def radial_update(fields, ids, cells, turned, part, speed, near_a, far, same, cross_0):
    pins = [pinned(x) for x in (cells, turned, near_a, far, same, cross_0, part)]
    return pl.pallas_call(
        functools.partial(radial_kernel, fields),
        in_specs=[SMEM] * 2 + [VMEM] * len(pins),
        out_specs=[VMEM, HBM],
        out_shape=[in_vmem(*part.shape), jax.ShapeDtypeStruct(part.shape, f32)],
        input_output_aliases={1 + len(pins): 0},
        scratch_shapes=[pltpu.VMEM(part.shape[1:], f32), pltpu.SemaphoreType.DMA],
        compiler_params=SMALL,
        cost_estimate=cost(1e8, 6e6),
        name="radial_update",
    )(speed, ids, *pins)


def placed(tiles, field, from_left):
    start = REACH * PACKED.index(field)
    tile, offset = start // 8, start % 8
    cells = tiles[tile]
    sub = lax.broadcasted_iota(jnp.int32, cells.shape, 1)
    if offset + REACH > 8:
        cells = jnp.where(sub >= offset, cells, tiles[tile + 1])
    goal = 0 if from_left else 8 - REACH
    shift = (goal - offset) % 8
    if shift:
        cells = pltpu.roll(cells, shift, 1)
    keep = sub < REACH if from_left else sub >= 8 - REACH
    return jnp.where(keep, cells, 0.0)


def by_side(lon, same, crosses):
    even = lon % 2 == 0
    lefts, rights = {}, {}
    for t, cross in enumerate(crosses):
        near = same[:, 8 * t : 8 * t + 8]
        lefts[t] = jnp.where(even, cross, near)
        rights[t] = jnp.where(even, near, cross)
    return lefts, rights


def with_sides(cells, lefts, rights, field):
    cols = cells.shape[1]
    return jnp.concatenate(
        [cells[:, :8] + placed(lefts, field, True), cells[:, cols - 8 :] + placed(rights, field, False)], axis=1
    )


def with_ends(cells, step, steps, rad, near, far):
    rows = cells.shape[0]
    even = rad % 2 == 0
    below, above = jnp.where(even, far, near), jnp.where(even, near, far)
    at_low = (step == 0).astype(f32)
    at_top = (step == steps - 1).astype(f32)
    return jnp.concatenate(
        [cells[:REACH] + at_low * below, cells[REACH : rows - REACH], cells[rows - REACH :] + at_top * above], axis=0
    )


def tile_sum_kernel(
    ids_ref, part_ref, vol_ref, same_ref, cross_ref, near_ref, far_ref, rest_ref, hit_ref, seg_ref, spot_ref,
    out_ref, lines_ref,
):
    all_rows, cols, depth = vol_ref.shape
    tiles, points = out_ref.shape[0], out_ref.shape[1] // 3
    rows = 16
    steps = all_rows // rows

    def add(step, carry):
        here = pl.ds(pl.multiple_of(step * rows, rows), rows)
        lefts, rights = by_side(ids_ref[0], same_ref[here, :8], [cross_ref[here]])
        vol = vol_ref[here]
        for c, field in enumerate((0, 7)):
            cells = with_sides(part_ref[field, here], lefts, rights, field)
            cells = with_ends(cells, step, steps, ids_ref[1], near_ref[c], far_ref[field])
            lines = exact_dot((cells * vol).reshape(rows * cols, depth), seg_ref[...])
            lines_ref[c, here] = jnp.sum(lines.reshape(rows, cols, -1) * spot_ref[...][None], axis=1)
        return carry

    lax.fori_loop(0, steps, add, 0)
    for c in range(2):
        sums = sum(dot(hit_ref[...], part) for part in parts_of(lines_ref[c], 3))
        out_ref[:, c * points : (c + 1) * points] = sums
    mine = lax.broadcasted_iota(jnp.int32, (tiles, points), 0) == ids_ref[2]
    out_ref[:, 2 * points :] = jnp.where(mine, rest_ref[8:9], 0.0)


def tile_sums(ids, part, vol, same, cross, near, far, rest, hits, seg, spot):
    _, rows, _, _ = part.shape
    points = seg.shape[1]
    tiles = hits.shape[0]
    return pl.pallas_call(
        tile_sum_kernel,
        in_specs=[SMEM] + [VMEM] * 10,
        out_specs=VMEM,
        out_shape=in_vmem(tiles, 3 * points),
        scratch_shapes=[pltpu.VMEM((2, rows, points), f32)],
        compiler_params=LARGE,
        cost_estimate=cost(1e3, 1e3),
        name="tile_sums",
    )(ids, *[pinned(x) for x in (part, vol, same, cross, near, far, rest)], hits, seg, spot)


def drifted(density, courant):
    for _ in range(DRIFT):
        density = density - courant * (density - pltpu.roll(density, 1, 1))
    return density


def columns_of(packed_ref, channels):
    turned = jnp.transpose(packed_ref[...])
    return [turned[:channels, i : i + 1] for i in range(4)]


def keep_rest(density_ref, packed_ref, out_ref, spread_ref):
    _, channels, points = density_ref.shape
    courant, weight, first, second = columns_of(packed_ref, channels)
    rows = []
    for given in (first, second):
        for k, choices in enumerate((1.0, 3.0, 3.0, 1.0)):
            gain = (inner_step * choices) * weight * given
            for _ in range(k):
                gain = gain * courant
            for _ in range(DRIFT - k):
                gain = gain * (1.0 - courant)
            rows.append(jnp.broadcast_to(jnp.sum(gain, axis=0, keepdims=True), (1, points)))
    rest = jnp.sum(weight * drifted(density_ref[0], courant), axis=0, keepdims=True)
    out_ref[...] = jnp.concatenate(rows + [rest] * 8, axis=0)
    for i, column in enumerate((courant, first, second)):
        spread_ref[i] = jnp.broadcast_to(column, (channels, points))


def message_kernel(ids_ref, sums_ref, other_ref, rest_ref, *outs):
    *outs, total_ref = outs
    total_ref[...] = sums_ref[...] + other_ref[...]
    tiles, size = total_ref.shape
    points = size // 3
    pressure = pressures_of(total_ref[...], rest_ref)
    for i, out in enumerate(outs):
        owner = ids_ref[2] - ids_ref[0] + (ids_ref[0] ^ (2 * i))
        source = total_ref[pl.ds(owner, 1), :]
        out[:tiles] = pressure
        out[tiles:] = jnp.concatenate(
            [source[:, :points], source[:, points : 2 * points], jnp.zeros((6, points), f32)], axis=0
        )


def messages(ids, sums, other, rest, count):
    tiles, size = sums.shape
    return pl.pallas_call(
        message_kernel,
        in_specs=[SMEM] + [VMEM] * 3,
        out_specs=[VMEM] * count,
        out_shape=[in_vmem(tiles + 8, size // 3)] * count,
        scratch_shapes=[pltpu.VMEM(sums.shape, f32)],
        compiler_params=SMALL,
        cost_estimate=cost(1e3, 1e3),
        name="messages",
    )(ids, pinned(sums), pinned(other), pinned(rest))


def pressures_of(sums, rest_ref):
    points = sums.shape[1] // 3
    pressure = sums[:, 2 * points :]
    for c in range(2):
        source = sums[:, c * points : (c + 1) * points]
        for k in range(DRIFT + 1):
            shifted = pltpu.roll(source, k, 1) if k else source
            pressure = pressure + rest_ref[(DRIFT + 1) * c + k : (DRIFT + 1) * c + k + 1] * shifted
    return pressure


def finish_field(field, refs, part_ref, out, scale=None):
    ids_ref, near_a, near_b, far_ref, same_ref, *cross_refs = refs
    rows = 2 * CHUNK
    steps = out.shape[0] // rows
    last_field = far_ref.shape[0] - 1

    def step(i, carry):
        here = pl.ds(pl.multiple_of(i * rows, rows), rows)
        lefts, rights = {}, {}
        first = REACH * PACKED.index(field)
        for t in range(first // 8, (first + REACH - 1) // 8 + 1):
            cross = cross_refs[0][here] if t == 0 else cross_refs[1][here, 8 * t - 8 : 8 * t]
            one = by_side(ids_ref[0], same_ref[here, 8 * t : 8 * t + 8], [cross])
            lefts[t], rights[t] = one[0][0], one[1][0]
        near = near_a[field // last_field] if field in (0, last_field) else near_b[field - 1]
        cells = with_sides(part_ref[field, here], lefts, rights, field)
        cells = with_ends(cells, i, steps, ids_ref[1], near, far_ref[field])
        out[here] = cells if scale is None else scale * cells
        return carry

    lax.fori_loop(0, steps, step, 0)


def most_kernel(ids_ref, part_ref, *refs):
    *sides, _, out_hbm, last_ref, done, sem = refs
    copies = []
    for i in range(done.shape[0]):
        finish_field(i + 1, (ids_ref, *sides), part_ref, done.at[i])
        copies.append(pltpu.make_async_copy(done.at[i], out_hbm.at[i + 1], sem.at[i]))
        copies[-1].start()
    finish_field(done.shape[0] + 1, (ids_ref, *sides), part_ref, last_ref, 1.0 - nudge_rate)
    for copy in copies:
        copy.wait()


def last_kernel(
    cells_ref, _, hit_ref, sums_ref, spot_ref, seg_ref, density_ref, spread_ref,
    out_hbm, drifted_hbm, done, back_ref, moved, sem,
):
    points = spot_ref.shape[1]
    rows, cols, depth = done.shape
    tiles = hit_ref.shape[1]
    last = out_hbm.shape[0] - 1
    back = sum(dot(hit_ref[...], p) for p in parts_of(sums_ref[:tiles], 3))
    for i, part in enumerate(parts_of(nudge_rate * back, 3)):
        back_ref[i] = part.astype(f32)
    copies = []
    density = density_ref[0] + inner_step * (
        spread_ref[1] * sums_ref[tiles : tiles + 1] + spread_ref[2] * sums_ref[tiles + 1 : tiles + 2]
    )
    moved[0] = drifted(density, spread_ref[0])
    copies.append(pltpu.make_async_copy(moved, drifted_hbm, sem.at[len(copies)]))
    copies[-1].start()
    size = 2 * CHUNK
    for first in range(0, rows, size):
        here = pl.ds(first, size)
        spread = [(back_ref[i, here][:, None, :] * spot_ref[...][None]).reshape(-1, points) for i in range(3)]
        returned = dot(jnp.concatenate(spread, axis=1).astype(bf16), seg_ref[...])
        done[here] = cells_ref[here] + returned.reshape(-1, cols, depth)
        copies.append(pltpu.make_async_copy(done.at[here], out_hbm.at[last, here], sem.at[len(copies)]))
        copies[-1].start()
    for copy in copies:
        copy.wait()


def message_kernel(ids_ref, sums_ref, other_ref, rest_ref, *outs):
    *outs, total_ref = outs
    total_ref[...] = sums_ref[...] + other_ref[...]
    tiles, size = total_ref.shape
    points = size // 3
    pressure = pressures_of(total_ref[...], rest_ref)
    for i, out in enumerate(outs):
        owner = ids_ref[2] - ids_ref[0] + (ids_ref[0] ^ (2 * i))
        source = total_ref[pl.ds(owner, 1), :]
        out[:tiles] = pressure
        out[tiles:] = jnp.concatenate(
            [source[:, :points], source[:, points : 2 * points], jnp.zeros((6, points), f32)], axis=0
        )


def messages(ids, sums, other, rest, count):
    tiles, size = sums.shape
    return pl.pallas_call(
        message_kernel,
        in_specs=[SMEM] + [VMEM] * 3,
        out_specs=[VMEM] * count,
        out_shape=[in_vmem(tiles + 8, size // 3)] * count,
        scratch_shapes=[pltpu.VMEM(sums.shape, f32)],
        compiler_params=SMALL,
        cost_estimate=cost(1e3, 1e3),
        name="messages",
    )(ids, pinned(sums), pinned(other), pinned(rest))


def pressures_of(sums, rest_ref):
    points = sums.shape[1] // 3
    pressure = sums[:, 2 * points :]
    for c in range(2):
        source = sums[:, c * points : (c + 1) * points]
        for k in range(DRIFT + 1):
            shifted = pltpu.roll(source, k, 1) if k else source
            pressure = pressure + rest_ref[(DRIFT + 1) * c + k : (DRIFT + 1) * c + k + 1] * shifted
    return pressure


def finish_most(ids, part, rad, same, crosses, result):
    fields, rows, cols, depth = part.shape
    pins = [pinned(x) for x in (part, *rad, same, *crosses)]
    return pl.pallas_call(
        most_kernel,
        in_specs=[SMEM] + [VMEM] * len(pins) + [HBM],
        out_specs=[HBM, VMEM],
        out_shape=[jax.ShapeDtypeStruct(part.shape, f32), in_vmem(rows, cols, depth)],
        input_output_aliases={1 + len(pins): 0},
        scratch_shapes=[pltpu.VMEM((fields - 2, rows, cols, depth), f32), pltpu.SemaphoreType.DMA((fields - 2,))],
        compiler_params=LARGE,
        cost_estimate=cost(1e8, 1.6e7),
        name="finish_most",
    )(ids, *pins, result)


def finish_last(cells, most, hits, sums, spot, seg, density, spread):
    rows, cols, depth = cells.shape
    return pl.pallas_call(
        last_kernel,
        in_specs=[VMEM, HBM] + [VMEM] * 6,
        out_specs=[HBM, HBM],
        out_shape=[jax.ShapeDtypeStruct(most.shape, f32), jax.ShapeDtypeStruct(density.shape, f32)],
        input_output_aliases={1: 0},
        scratch_shapes=[
            pltpu.VMEM(cells.shape, f32),
            pltpu.VMEM((3, rows, spot.shape[1]), f32),
            pltpu.VMEM(density.shape, f32),
            pltpu.SemaphoreType.DMA((rows // (2 * CHUNK) + 1,)),
        ],
        compiler_params=SMALL,
        cost_estimate=cost(1e3, 1e3),
        name="finish_last",
    )(pinned(cells), most, hits, pinned(sums), spot, seg, density, pinned(spread))


def swap(x, axis, bit):
    return lax.ppermute(x, axis, [(i, i ^ bit) for i in range(lax.axis_size(axis))])


def per_device(
    state,
    flux_matrices,
    wave_speed,
    flux_volume,
    block_tile,
    tile_of_device,
    phase_density,
    injection,
    drift_courant,
    energy_weight,
):
    fields, rows, cols, depth = state.shape
    n_rad, n_lon = lax.axis_size("rad"), lax.axis_size("lon")
    points = cols * ZSEG
    lon, rad, place = [lax.axis_index(axes).astype(jnp.int32).reshape(1) for axes in ("lon", "rad", ("rad", "lon"))]

    across = [(i, (i + 1 if i % 2 else i - 1) % n_lon) for i in range(n_lon)]
    beyond = [(i, j) for i in range(n_rad) for j in [i + 1 if i % 2 else i - 1] if 0 <= j < n_rad]
    rim, ids, same, *crosses = lon_edges(state, flux_matrices, wave_speed, lon, rad, place)
    cross_0 = lax.ppermute(crosses[0], "lon", across)
    same = swap(same, "lon", 1)
    cross_1 = lax.ppermute(crosses[1], "lon", across)

    near_a, near_b, far = rad_edges(ids, rim, flux_matrices, wave_speed)
    near_a = swap(near_a, "rad", 1)
    far = lax.ppermute(far, "rad", beyond)

    packed = jnp.concatenate([drift_courant[None], energy_weight[None], injection], axis=0)
    packed = jnp.pad(packed, ((0, 4), (0, -packed.shape[1] % 128)))

    part, turned, cells, rest, spread = local_update(state, flux_matrices, wave_speed, phase_density, packed)

    targets = block_tile[0, :, 0]
    hits = (tile_of_device[:, None] == targets[None, :]).astype(bf16)
    hits_back = (targets[:, None] == tile_of_device[None, :]).astype(bf16)
    seg_cells = depth // ZSEG
    seg = np.array([[float(p % ZSEG == z // seg_cells) for p in range(points)] for z in range(depth)], np.float32)
    spot = np.array([[float(p // ZSEG == l) for p in range(points)] for l in range(cols)], np.float32)
    sums = tile_sums(
        ids, part, flux_volume, same, cross_0, near_a, far, rest, hits, jnp.asarray(seg, bf16), jnp.asarray(spot)
    )
    near_b, sums = lax.optimization_barrier((near_b, sums))
    near_b = swap(near_b, "rad", 1)
    part, sums = lax.optimization_barrier((part, sums))
    others = [swap(sums, "rad", step) for step in range(1, n_rad)]
    part, result = radial_update(
        tuple(range(1, fields - 1)), ids, cells, turned, part, wave_speed, near_a, far, same, cross_0
    )
    part, sums = lax.optimization_barrier((part, sums))
    sums = sum(others, sums)
    sums, *shares = messages(ids, sums, swap(sums, "lon", 1), rest, n_lon // 2)
    others = [swap(share, "lon", 2 * i + 2) for i, share in enumerate(shares)]
    most, last = finish_most(ids, part, (near_a, near_b, far), same, (cross_0, cross_1), result)
    sums, most = lax.optimization_barrier((sums, most))
    sums = sum(others, sums)
    done, density = finish_last(
        last, most, hits_back, sums, jnp.asarray(spot), jnp.asarray(np.tile(seg.T, (3, 1)), bf16), phase_density, spread
    )
    return done, density


def solution(mesh):
    in_specs = (
        P(None, "rad", "lon", None),
        P(),
        P(),
        P("rad", "lon", None),
        P("lon", "rad", None),
        P(),
        P(("rad", "lon"), None, None),
        P(),
        P(),
        P(),
    )
    out_specs = (P(None, "rad", "lon", None), P(("rad", "lon"), None, None))
    return jax.shard_map(per_device, mesh=mesh, in_specs=in_specs, out_specs=out_specs, check_vma=False)
```
